32 devices in a mesh: sx: 4 (over y, x), sy: 2 (over core), cells: 4 (over z).
Axes of the slice: x: 2, y: 2, z: 4, core: 2. Of those that a mesh axis runs over, the one named last changes fastest.
Arguments:
- logits: float32 [5632, 16, 512], P('cells', 'sx', 'sy'), may hold values from -8 to 8
- cells_expr: bfloat16 [5632, 2048], P('cells'), may hold values from -48 to 48
- spatial: float32 [16, 512, 2048], P('sx', 'sy'), may hold values from -6 to 6
- gene_mask: int32 [2, 2048], replicated, may hold values 0 or 1
- slide_id: int32 [16, 512], P('sx', 'sy'), may hold values from 0 to 1
- edge_weight: float32 [6, 16, 512], P(None, 'sx', 'sy'), may hold values from 0.1 to 0.4
- edge_mask: int32 [6, 16, 512], P(None, 'sx', 'sy'), may hold values 0 or 1
Outputs:
- losses: float32 [2], replicated
- g_pred: float32 [16, 512, 2048], P('sx', 'sy', 'cells')
- d_logits: float32 [5632, 16, 512], P('cells', 'sx', 'sy')
- d_cells: float32 [5632, 2048], P('cells', ('sx', 'sy'))
The draws below stay inside these ranges and needn't reach their ends.
All inputs are finite; a program needn't handle non-finite values. No bound on the sum of `edge_mask` on one device may be relied on, other than what follows from the above.
Results may differ from the reference program's by a relative error of at most 0.012.
Values may be sent and summed in bfloat16 or wider, within the bound.
A program may use at most 192 MiB of HBM per device.

```python
import jax
import jax.numpy as jnp
from jax import lax

GENES = 2048
NCELL = 5632
ROWS = 16
COLS = 512


def set_ends(values, key, least, top_value):
    dims = values.shape
    index_at = [jax.random.randint(jax.random.fold_in(key, axis), (), 0, dims[axis]) for axis in range(len(dims))]
    values = values.at[tuple(index_at)].set(least)
    longest = dims.index(max(dims))
    index_at[longest] = (index_at[longest] + 1) % dims[longest]
    return values.at[tuple(index_at)].set(top_value)


def levels(own_key, extent, shards, low, top_value):
    factor_of = 1.0
    for position, shards_of in shards:
        draws = jax.random.uniform(jax.random.fold_in(jax.random.fold_in(own_key, 6), position), (shards_of,), jnp.float32, low / len(shards), top_value / len(shards))
        factor_of = factor_of * jnp.repeat(jnp.exp(draws), extent[position] // shards_of).reshape((-1,) + (1,) * (len(extent) - 1 - position))
    return factor_of


def bell_draw(stream_key, extent, width, bound, shards=(), held_as=jnp.bfloat16):
    result = jax.random.normal(stream_key, extent, jnp.float32) * width
    if len(shards) > 0:
        result = levels(stream_key, extent, shards, -0.22, 0.18) * result
    return jnp.clip(result, min=-bound, max=bound).astype(held_as)


def setup_inputs(seed: int = 0) -> dict:
    arg_keys = jax.random.split(jax.random.key(seed), 8)
    logits = bell_draw(arg_keys[0], (NCELL, ROWS, COLS), 1.5, 8.0, ((0, 4), (1, 4), (2, 2)), jnp.float32)
    cells_expr = bell_draw(arg_keys[1], (NCELL, GENES), 8.0, 48.0, ((0, 4),))
    spatial = bell_draw(arg_keys[2], (ROWS, COLS, GENES), 1.0, 6.0, ((0, 4), (1, 2)), jnp.float32)
    gene_mask = set_ends((jax.random.randint(arg_keys[3], (2, GENES), 0, 4) < 3).astype(jnp.int32), jax.random.fold_in(arg_keys[3], 1), 0, 1)
    slide_id = set_ends(jax.random.randint(arg_keys[4], (ROWS, COLS), 0, 2), jax.random.fold_in(arg_keys[4], 1), 0, 1).astype(jnp.int32)
    edge_weight = jnp.clip(0.1 + 0.3 * jax.random.uniform(arg_keys[5], (6, ROWS, COLS), jnp.float32) ** levels(arg_keys[5], (6, ROWS, COLS), ((1, 4), (2, 2)), -0.2, 0.2), 0.1, 0.4)
    edge_mask = set_ends((jax.random.randint(arg_keys[6], (6, ROWS, COLS), 0, 4) < 3).astype(jnp.int32), jax.random.fold_in(arg_keys[6], 1), 0, 1)
    return dict(logits=logits, cells_expr=cells_expr, spatial=spatial, gene_mask=gene_mask, slide_id=slide_id, edge_weight=edge_weight, edge_mask=edge_mask)


@jax.custom_vjp
def low(v):
    return lax.optimization_barrier(v.astype(jnp.bfloat16)).astype(jnp.float32)

@jax.custom_vjp
def low_back(v):
    return v

def low_keep(v):
    return (low(v), None)

def low_pass(kept, grad):
    return (grad,)

def back_keep(v):
    return (v, None)

def back_low(kept, grad):
    return (low(grad),)
low.defvjp(low_keep, low_pass)
low_back.defvjp(back_keep, back_low)
eps = 1e-06
OFFSETS = ((0, 1), (0, -1), (1, 0), (-1, 0), (-1, 1), (1, -1))
HIGH = lax.Precision.HIGHEST

def neighbour(field, row_off, col_off):
    grid_rows, grid_cols = (field.shape[0], field.shape[1])
    padded = jnp.pad(field, ((1, 1), (1, 1), (0, 0)))
    return padded[1 + row_off:1 + row_off + grid_rows, 1 + col_off:1 + col_off + grid_cols]

def forward(logits, cells_expr, spatial, mask_f, slide_hot, coeff):
    col_top = lax.optimization_barrier(jnp.max(logits, axis=0))
    exps_all = jnp.exp(logits - col_top)
    mapping = exps_all / lax.optimization_barrier(jnp.sum(exps_all, axis=0))
    mapping_low = low(mapping)
    predicted = jnp.einsum('nrc,ng->rcg', mapping_low, cells_expr, precision=HIGH)
    predicted = low_back(predicted)
    smooth = predicted
    for slot in range(6):
        smooth = smooth + coeff[slot][:, :, None] * neighbour(predicted, OFFSETS[slot][0], OFFSETS[slot][1])
    product = smooth * spatial
    gene_a = jnp.einsum('src,rcg->sg', slide_hot, product, precision=HIGH)
    gene_b = jnp.einsum('src,rcg->sg', slide_hot, smooth * smooth, precision=HIGH)
    gene_c = jnp.einsum('src,rcg->sg', slide_hot, spatial * spatial, precision=HIGH)
    gene_cos = gene_a * lax.rsqrt(gene_b + eps) * lax.rsqrt(gene_c + eps)
    count = jnp.maximum(lax.optimization_barrier(jnp.sum(mask_f, axis=1)), 1.0)
    gene_loss = -jnp.sum(lax.optimization_barrier(jnp.sum(mask_f * gene_cos, axis=1)) / count) / 2.0
    spot_mask = jnp.einsum('src,sg->rcg', slide_hot, mask_f, precision=HIGH)
    spot_a = lax.optimization_barrier(jnp.sum(spot_mask * product, axis=-1))
    spot_b = lax.optimization_barrier(jnp.sum(spot_mask * smooth * smooth, axis=-1))
    spot_c = lax.optimization_barrier(jnp.sum(spot_mask * spatial * spatial, axis=-1))
    spot_cos = spot_a * lax.rsqrt(spot_b + eps) * lax.rsqrt(spot_c + eps)
    spot_loss = -jnp.mean(spot_cos)
    return (gene_loss + spot_loss, (gene_loss, spot_loss, predicted))

def reference(logits, cells_expr, spatial, gene_mask, slide_id, edge_weight, edge_mask):
    mask_f = gene_mask.astype(jnp.float32)
    slide_hot = (slide_id[None] == jnp.arange(2, dtype=jnp.int32)[:, None, None]).astype(jnp.float32)
    coeff = edge_weight * edge_mask.astype(jnp.float32)
    cells_f = cells_expr.astype(jnp.float32)

    def objective(logit_in, cells_in):
        return forward(logit_in, cells_in, spatial, mask_f, slide_hot, coeff)
    total, pullback, extra = jax.vjp(objective, logits, cells_f, has_aux=True)
    d_logits, d_cells = pullback(jnp.ones_like(total))
    losses = jnp.stack([extra[0], extra[1]])
    return (losses, extra[2], d_logits, d_cells)
```

```python
import jax
import jax.numpy as jnp
from jax import lax
from jax.sharding import PartitionSpec as P

eps = 1e-06
OFFSETS = ((0, 1), (0, -1), (1, 0), (-1, 0), (-1, 1), (1, -1))


def with_halo(cells, sides, width):
    for axis, dim in sides:
        count = lax.axis_size(axis)
        ends = count - 1
        head = lax.slice_in_dim(cells, 0, width, axis=dim)
        tail = lax.slice_in_dim(cells, cells.shape[dim] - width, cells.shape[dim], axis=dim)
        cells = jnp.concatenate(
            [
                lax.ppermute(tail, axis, [(i, (i + 1) % count) for i in range(ends)]),
                cells,
                lax.ppermute(head, axis, [((i + 1) % count, i) for i in range(ends)]),
            ],
            axis=dim,
        )
    return cells


def per_device(logits, cells_expr, spatial, gene_mask, slide_id, edge_weight, edge_mask):
    cell_rows, tile_rows, tile_cols = logits.shape
    gene_width = cells_expr.shape[1]
    tile_spots = tile_rows * tile_cols
    all_spots = tile_spots * lax.axis_size("sx") * lax.axis_size("sy")
    share = gene_width // lax.axis_size("cells")
    first_gene = lax.axis_index("cells") * share
    mask_all = gene_mask.astype(jnp.float32)
    count = jnp.maximum(jnp.sum(mask_all, axis=1), 1.0)
    mask_f = lax.dynamic_slice_in_dim(mask_all, first_gene, share, 1)
    truth = lax.dynamic_slice_in_dim(spatial, first_gene, share, 2)
    on_one = (slide_id == 1)[:, :, None]
    slide_hot = (slide_id[None] == jnp.arange(2, dtype=jnp.int32)[:, None, None]).astype(
        jnp.float32
    )
    coeff = edge_weight * edge_mask.astype(jnp.float32)
    exps_tile = jnp.exp(logits)
    col_total = lax.psum(jnp.sum(exps_tile, axis=0), "cells")
    mapping = exps_tile / col_total
    mapping_low = mapping.astype(jnp.bfloat16).reshape(cell_rows, tile_spots)
    partial_pred = lax.dot_general(
        mapping_low, cells_expr, (((0,), (0,)), ((), ())), preferred_element_type=jnp.float32
    )
    predicted = lax.psum_scatter(partial_pred, "cells", scatter_dimension=1, tiled=True)
    predicted = predicted.reshape(tile_rows, tile_cols, share)
    padded = with_halo(predicted, (("sx", 0), ("sy", 1)), 1)
    smooth = predicted
    for slot in range(6):
        row_off, col_off = OFFSETS[slot]
        smooth = (
            smooth
            + coeff[slot][:, :, None]
            * padded[1 + row_off : 1 + row_off + tile_rows, 1 + col_off : 1 + col_off + tile_cols]
        )
    product = smooth * truth
    squares = smooth * smooth
    truth_sq = truth * truth
    hot = slide_hot[:, :, :, None]
    gene_part = jnp.stack(
        [jnp.sum(hot * what[None], axis=(1, 2)) for what in (product, squares, truth_sq)]
    )
    spot_mask = jnp.where(on_one, mask_f[1], mask_f[0])
    spot_part = jnp.stack(
        [jnp.sum(spot_mask * what, axis=-1) for what in (product, squares, truth_sq)]
    )
    gene_all = lax.psum(gene_part, ("sx", "sy"))
    spot_part = lax.psum(spot_part, "cells")
    spot_ib = lax.rsqrt(spot_part[1] + eps)
    spot_ic = lax.rsqrt(spot_part[2] + eps)
    spot_cos = spot_part[0] * spot_ib * spot_ic
    gene_ib = lax.rsqrt(gene_all[1] + eps)
    gene_ic = lax.rsqrt(gene_all[2] + eps)
    gene_cos = gene_all[0] * gene_ib * gene_ic
    gene_loss = -jnp.sum(jnp.sum(mask_f * gene_cos, axis=1) / count) / 2.0
    gene_loss = lax.psum(gene_loss, "cells")
    spot_loss = -lax.psum(jnp.sum(spot_cos), ("sx", "sy")) / all_spots
    losses = jnp.stack([gene_loss, spot_loss])
    gene_scale = -mask_f / (2.0 * count[:, None])
    truth_by = gene_scale * gene_ib * gene_ic
    smooth_by = -gene_scale * gene_cos * gene_ib * gene_ib
    truth_coef = jnp.where(on_one, truth_by[1], truth_by[0])
    smooth_coef = jnp.where(on_one, smooth_by[1], smooth_by[0])
    spot_scale = -1.0 / all_spots
    spot_truth = (spot_scale * spot_ib * spot_ic)[:, :, None]
    spot_smooth = (-spot_scale * spot_cos * spot_ib * spot_ib)[:, :, None]
    d_smooth = (
        truth_coef * truth
        + smooth_coef * smooth
        + spot_mask * (spot_truth * truth + spot_smooth * smooth)
    )
    coeff_pad = with_halo(coeff, (("sx", 1), ("sy", 2)), 1)
    grad_pad = with_halo(d_smooth, (("sx", 0), ("sy", 1)), 1)
    d_pred = d_smooth
    for slot in range(6):
        row_off, col_off = OFFSETS[slot]
        rows_from = 1 - row_off
        cols_from = 1 - col_off
        weight_here = coeff_pad[
            slot, rows_from : rows_from + tile_rows, cols_from : cols_from + tile_cols
        ]
        d_pred = (
            d_pred
            + weight_here[:, :, None]
            * grad_pad[rows_from : rows_from + tile_rows, cols_from : cols_from + tile_cols]
        )
    d_low = d_pred.astype(jnp.bfloat16).reshape(tile_spots, share)
    column = jnp.sum(predicted.reshape(tile_spots, share) * d_low.astype(jnp.float32), axis=1)
    column = lax.psum(column, "cells").reshape(tile_rows, tile_cols)
    d_flat = lax.all_gather(d_low, "cells", axis=1, tiled=True)
    d_map = lax.dot_general(
        cells_expr, d_flat, (((1,), (1,)), ((), ())), preferred_element_type=jnp.float32
    )
    d_map = d_map.reshape(cell_rows, tile_rows, tile_cols)
    d_logits = mapping * (d_map - column)
    d_part = jnp.dot(mapping_low, d_flat, preferred_element_type=jnp.float32)
    d_cells = lax.psum_scatter(d_part, ("sx", "sy"), scatter_dimension=1, tiled=True)
    return (losses, predicted, d_logits, d_cells)


def solution(mesh):
    return jax.shard_map(
        per_device,
        mesh=mesh,
        in_specs=(
            P("cells", "sx", "sy"),
            P("cells", None),
            P("sx", "sy", None),
            P(),
            P("sx", "sy"),
            P(None, "sx", "sy"),
            P(None, "sx", "sy"),
        ),
        out_specs=(P(), P("sx", "sy", "cells"), P("cells", "sx", "sy"), P("cells", ("sx", "sy"))),
        check_vma=False,
    )
```

```python
import functools

import jax
import jax.numpy as jnp
from jax import lax
from jax.experimental import pallas as pl
from jax.experimental.pallas import tpu as pltpu
from jax.sharding import PartitionSpec as P

EPS = 1e-06
OFFSETS = ((0, 1), (0, -1), (1, 0), (-1, 0), (-1, 1), (1, -1))
LANES = 128
TOP = 32767.0
MESH = pl.DeviceIdType.MESH
F32, BF16, I16, I32 = jnp.float32, jnp.bfloat16, jnp.int16, jnp.int32
rem, div = lax.rem, lax.div


def loop(count, body):
    lax.fori_loop(0, count, lambda i, _: (body(i), 0)[1], 0)


def remote(src, dst, sent, got, to):
    return pltpu.make_async_remote_copy(
        src_ref=src, dst_ref=dst, send_sem=sent, recv_sem=got, device_id=to, device_id_type=MESH
    )


def wait(ref, sem):
    pltpu.make_async_copy(ref, ref, sem).wait()


def spread(row):
    parts = [
        jnp.broadcast_to(row[:, at : at + LANES], (LANES, LANES)).T
        for at in range(0, row.shape[1], LANES)
    ]
    return jnp.concatenate(parts, axis=0)


def fold(x):
    return jnp.sum(x.reshape(x.shape[0] // 8, 8, x.shape[1]), axis=0)


def kernel(names, sizes, *refs):
    n, nsx, nsy, share, all_spots = sizes
    o = dict(zip(names, refs, strict=True))
    lg, cells, spat, gmask, slide, ew, em = (o[k] for k in names[:7])
    losses, gp, dlog, dcell = (o[k] for k in names[7:11])
    xs, mm, mt, dm, srow, ab, sc, tt = (o[k] for k in names[11:19])
    gg, sm, sp, pad, hg, hs, hd, hq = (o[k] for k in names[19:27])
    es, er, cf, cb, hot, con, cor, acc = (o[k] for k in names[27:35])
    gs, gr, spx, gc, spr, dd, fm = (o[k] for k in names[35:42])
    pss, rs1, rs2, rs3, dcv, gpr, gps = (o[k] for k in names[42:49])

    c_rows, t_rows, width = lg.shape
    spots = t_rows * width
    nb = cells.shape[1] // 2 // LANES
    wl = width // LANES
    wb = gpr.shape[0]
    nplane = nsx * nsy
    half = nb // 2
    bpg = nb // 4
    tile = LANES
    tiles = c_rows // tile
    quarter = c_rows // t_rows
    sub = min(64, width)
    mid = slice(8, 8 + width)

    sx, sy, cz = (lax.axis_index(a) for a in ("sx", "sy", "cells"))
    here = sx * nsy + sy
    owner = (cz == 0) | (cz == n - 1)
    od = jnp.where(cz == 0, 0, 1)
    up, down = sx > 0, sx < nsx - 1
    mate = (sx, 1 - sy, cz)

    def gene_block(d, k):
        return jnp.where(d == 0, rem(k + half, nb), nb + k)

    for r in range(t_rows):
        pltpu.make_async_copy(lg.at[:, r, :], dm.at[r], o["lg_m"].at[r]).start()

    def load_cells(b):
        at = pl.ds(pl.multiple_of(b * LANES, LANES), LANES)
        return pltpu.make_async_copy(cells.at[:, at], xs.at[b], o["xs_m"].at[b])

    loop(2 * nb, lambda b: load_cells(b).start())

    def load_truth(k):
        at = pl.ds(pl.multiple_of(gene_block(od, k) * LANES, LANES), LANES)
        return pltpu.make_async_copy(spat.at[:, :, at], sp.at[k], o["sp_m"].at[k])

    @pl.when(owner)
    def _():
        loop(nb, lambda k: load_truth(k).start())

    barrier = pltpu.get_barrier_semaphore()

    def greet_line(j):
        to = (sx, sy, rem(cz + j + 1, n))
        pl.semaphore_signal(barrier, inc=1, device_id=to, device_id_type=MESH)

    def greet_plane(j):
        t = rem(here + j + 1, nplane)
        to = (div(t, nsy), rem(t, nsy), cz)
        pl.semaphore_signal(barrier, inc=1, device_id=to, device_id_type=MESH)

    loop(n - 1, greet_line)
    loop(nplane - 1, greet_plane)

    for r in range(t_rows):
        pltpu.make_async_copy(lg.at[:, r, :], dm.at[r], o["lg_m"].at[r]).wait()

        def exps(i, s, r=r):
            at = pl.ds(i * tile, tile)
            x = jnp.exp(dm[r, at, :])
            dm[r, at, :] = x
            return s + fold(x)

        s = lax.fori_loop(0, c_rows // tile, exps, jnp.zeros((8, width), F32))
        s = jnp.sum(s, axis=0, keepdims=True)
        for h in range(wl):
            srow[cz, pl.ds(r * wl + h, 1), :] = s[:, h * LANES : (h + 1) * LANES]

    pl.semaphore_wait(barrier, n - 1 + nplane - 1)

    def send_sums(j):
        to = (sx, sy, rem(cz + j + 1, n))
        remote(srow.at[cz], srow.at[cz], o["s_s"].at[j], o["s_r"].at[cz], to).start()

    loop(n - 1, send_sums)

    def turn(dst, first):
        def each(i):
            for r in range(t_rows):
                at = pl.ds(pl.multiple_of((i + first) * LANES, LANES), LANES)
                dst[i, r] = dm[r, at, :].T

        return each

    turned = ((gg, 0, min(tiles, nb)), (sm, nb, max(tiles - nb, 0)))
    for dst, first, count in turned:
        loop(count, turn(dst, first))

    def wait_sums(j):
        z = rem(cz + j + 1, n)
        wait(srow.at[z], o["s_r"].at[z])

    loop(n - 1, wait_sums)
    total = srow[0]
    for z in range(1, n):
        total = total + srow[z]
    inv = 1.0 / total
    inv_rows = [
        jnp.concatenate([inv[r * wl + h : r * wl + h + 1] for h in range(wl)], axis=1)
        for r in range(t_rows)
    ]
    for r in range(t_rows):
        tt[0, 0, r] = spread(inv_rows[r])

    for dst, first, count in turned:
        def scale(i, dst=dst, first=first):
            at = pl.ds(pl.multiple_of((i + first) * LANES, LANES), LANES)
            for r in range(t_rows):
                mt[r, :, at] = (dst[i, r] * tt[0, 0, r]).astype(BF16)

        loop(count, scale)

    def keep_mapping():
        for r in range(t_rows):
            def each(i, r=r):
                at = pl.ds(pl.multiple_of(i * LANES, LANES), LANES)
                mm[at, r * width : (r + 1) * width] = (dm[r, at, :] * inv_rows[r]).astype(BF16)
                dm[r, at, :] = jnp.zeros((LANES, width), F32)

            loop(tiles, each)

    loop(2 * nb, lambda b: load_cells(b).wait())

    def coef_routes():
        return (
            (0, down, (sx + 1, sy, cz)),
            (1, up, (sx - 1, sy, cz)),
            (2, sx >= 0, mate),
            (3, down, (sx + 1, 1 - sy, cz)),
            (4, up, (sx - 1, 1 - sy, cz)),
        )

    def predict(d, k, r):
        tt[d, rem(k, 2), r] = jnp.dot(mt[r], xs[gene_block(d, k)], preferred_element_type=F32)

    def put(d, k, r, t):
        top = jnp.maximum(jnp.max(jnp.abs(t), axis=0, keepdims=True), 1e-30)
        ab[d, k, r] = jnp.round(t * (TOP / top)).astype(I32).astype(I16)
        sc[d, k, r] = top * (1.0 / TOP)

    def pass_on(d, k, r):
        to = (sx, sy, cz + 2 * d - 1)
        remote(ab.at[d, k, r], ab.at[d, k, r], o["a_s"].at[d, k, r], o["a_r"].at[d, k, r], to).start()
        remote(sc.at[d, k, r], sc.at[d, k, r], o["c_s"].at[d, k, r], o["c_r"].at[d, k, r], to).start()

    def chunk_of(q):
        return div(q, t_rows), rem(rem(q, t_rows) * (t_rows - 1), t_rows)

    @pl.when(owner)
    def _():
        d = 1 - od

        def first(q):
            k, r = chunk_of(q)
            predict(d, k, r)
            put(d, k, r, tt[d, rem(k, 2), r])
            pass_on(d, k, r)

        loop(nb * t_rows, first)

        for r in range(t_rows):
            rows = [ew[j, r : r + 1, :] * em[j, r : r + 1, :].astype(F32) for j in range(6)]
            con[r] = jnp.concatenate(rows + [jnp.zeros((2, width), F32)], axis=0)
            for j in range(6):
                cf[j, r] = spread(rows[j])
            hot[r] = spread(slide[r : r + 1, :].astype(F32))
        acc[...] = jnp.zeros(acc.shape, F32)

        for slot, ok, to in coef_routes():
            @pl.when(ok)
            def _(slot=slot, to=to):
                remote(con, cor.at[slot], o["co_s"].at[slot], o["co_r"].at[slot], to).start()

        loop(nb, lambda k: load_truth(k).wait())

    def back_coefs():
        for slot, ok in ((0, up), (1, down), (2, sx >= 0), (3, up), (4, down)):
            @pl.when(ok)
            def _(slot=slot):
                wait(cor.at[slot], o["co_r"].at[slot])

        lane = lax.broadcasted_iota(I32, (8, width), 1)
        for j, (dr, dc) in enumerate(OFFSETS):
            for r in range(t_rows):
                at = r - dr
                if at < 0:
                    base, side, ok = cor[0, t_rows - 1], cor[3, t_rows - 1], up
                elif at >= t_rows:
                    base, side, ok = cor[1, 0], cor[4, 0], down
                else:
                    base, side, ok = con[at], cor[2, at], sx >= 0
                base = jnp.where(ok, base, 0.0)
                if dc:
                    by, edge = (1, 0) if dc == 1 else (width - 1, width - 1)
                    side = jnp.where(ok & (sy == (1 if dc == 1 else 0)), side, 0.0)
                    base = jnp.where(lane == edge, pltpu.roll(side, by, 1), pltpu.roll(base, by, 1))
                cb[j, r] = spread(base[j : j + 1]).astype(BF16)

    def send_edges(slot, which, k, rows):
        parts = [
            jnp.where(sy == 1, pad[slot, row, 8:9, :], pad[slot, row, 7 + width : 8 + width, :])
            for row in rows
        ]
        parts.append(jnp.zeros((8 - len(parts), LANES), F32))
        es[which, k] = jnp.concatenate(parts, axis=0)
        remote(es.at[which, k], er.at[which, k], o["e_s"].at[which, k], o["e_r"].at[which, k], mate).start()

    def take_edges(slot, which, k, rows):
        wait(er.at[which, k], o["e_r"].at[which, k])
        for i, row in enumerate(rows):
            edge = er[which, k, i : i + 1, :]
            pad[slot, row, 8 + width : 9 + width, :] = jnp.where(sy == 0, edge, 0.0)
            pad[slot, row, 7:8, :] = jnp.where(sy == 1, edge, 0.0)

    sides = ((0, up, 0), (1, down, t_rows + 1))

    def prepare(k):
        for side, ok, row in sides:
            @pl.when(ok)
            def _(side=side, row=row):
                wait(hg.at[side, k], o["hg_r"].at[side, k])
                wait(hs.at[side, k], o["hs_r"].at[side, k])
                pad[0, row, mid, :] = hg[side, k].astype(I32).astype(F32) * hs[side, k]

            @pl.when(jnp.logical_not(ok))
            def _(row=row):
                pad[0, row, mid, :] = jnp.zeros((width, LANES), F32)

        def rows(r):
            pad[0, r + 1, mid, :] = gg[k, r]

        loop(t_rows, rows)
        send_edges(0, 0, k, range(t_rows + 2))

    def smoothing(k):
        take_edges(0, 0, k, range(t_rows + 2))
        at = pl.ds(pl.multiple_of(gene_block(od, k) * LANES, LANES), LANES)
        mask = gmask[:, at].astype(F32)
        m0, m1 = mask[0:1], mask[1:2]

        def rows(r, sums):
            sums = list(sums)
            for u in range(0, width, sub):
                here_u = slice(u, u + sub)
                a = pad[0, r + 1, 8 + u : 8 + u + sub, :]
                for j, (dr, dc) in enumerate(OFFSETS):
                    a = a + cf[j, r, here_u, :] * pad[0, r + 1 + dr, 8 + dc + u : 8 + dc + u + sub, :]
                sm[k, r, here_u, :] = a
                t = sp[k, r, here_u, :]
                h = hot[r, here_u, :]
                mk = m0 + h * (m1 - m0)
                for i, x in enumerate((a * t, a * a, t * t)):
                    sums[2 * i] = sums[2 * i] + fold(x)
                    sums[2 * i + 1] = sums[2 * i + 1] + fold(x * h)
                    acc[i, r, here_u, :] = acc[i, r, here_u, :] + x * mk
            return tuple(sums)

        sums = lax.fori_loop(0, t_rows, rows, (jnp.zeros((8, LANES), F32),) * 6)
        parts = []
        for i in range(3):
            both = jnp.sum(sums[2 * i], axis=0, keepdims=True)
            one = jnp.sum(sums[2 * i + 1], axis=0, keepdims=True)
            parts += [both - one, one]
        gs[k] = jnp.concatenate(parts + [jnp.zeros((2, LANES), F32)], axis=0)

    def own_block(t, i):
        b = div(t * share, LANES) + i - od * nb
        return jnp.where(od == 0, rem(b + half, nb), b)

    def pred_copies(i, j):
        t = jnp.where(od == 0, j + 1, n - 2 - j)
        k = own_block(t, i)
        to = (sx, sy, t)
        return (
            remote(ab.at[od, k], gpr.at[i], o["gp_s"].at[j, i], o["gp_r"].at[i], to),
            remote(sc.at[od, k], gps.at[i], o["gq_s"].at[j, i], o["gq_r"].at[i], to),
        )

    def send_pred(i):
        def each(j):
            for copy in pred_copies(i, j):
                copy.start()

        loop(n // 2 - 1, each)

    early_pred = wb - 1 if n == 4 else 0

    lead = max(n - 3, 0)

    def sum_step(s):
        def direction(d):
            own, first = cz == d * (n - 1), cz == (1 - d) * (n - 1)
            off = jnp.where(owner, 0, jnp.where(d == 1, 2 * (cz - 1), 2 * (n - 2 - cz)))
            q = s - off

            @pl.when(jnp.logical_not(first) & (q >= 0) & (q < nb * t_rows))
            def _():
                k, r = chunk_of(q)
                wait(ab.at[d, k, r], o["a_r"].at[d, k, r])
                wait(sc.at[d, k, r], o["c_r"].at[d, k, r])
                got = ab[d, k, r].astype(I32).astype(F32) * sc[d, k, r]
                t = tt[d, rem(k, 2), r] + got
                put(d, k, r, t)

                @pl.when(jnp.logical_not(own))
                def _():
                    pass_on(d, k, r)

                @pl.when(own)
                def _():
                    gg[k, r] = t
                    for side, ok, row, to in halo_routes():
                        @pl.when(ok & (r == row))
                        def _(side=side, row=row, to=to):
                            remote(ab.at[d, k, row], hg.at[side, k], o["hg_s"].at[side, k], o["hg_r"].at[side, k], to).start()
                            remote(sc.at[d, k, row], hs.at[side, k], o["hs_s"].at[side, k], o["hs_r"].at[side, k], to).start()

                    i = rem(q, t_rows)

                    @pl.when((k > 0) & (i == 1))
                    def _():
                        prepare(k - 1)

                    @pl.when((k > 0) & (i == t_rows - 1))
                    def _():
                        smoothing(k - 1)

                    if early_pred:
                        @pl.when(q == 3 * nb * t_rows // 4)
                        def _():
                            for i in range(early_pred):
                                send_pred(i)

                @pl.when(k + 1 < nb)
                def _():
                    predict(d, k + 1, r)

        loop(2, direction)

        @pl.when(owner & (s == half * t_rows))
        def _():
            back_coefs()

    def halo_routes():
        return ((1, up, 0, (sx - 1, sy, cz)), (0, down, t_rows - 1, (sx + 1, sy, cz)))

    keep_mapping()

    def first_block(d):
        @pl.when(cz != (1 - d) * (n - 1))
        def _():
            loop(t_rows, lambda r: predict(d, 0, r))

    loop(2, first_block)
    loop(nb * t_rows + 2 * lead, sum_step)

    def diff_inside(k):
        slot = rem(k, 2)
        tc0, tc1, sc0, sc1, m0, m1 = (gc[k, i : i + 1, :] for i in range(6))

        def rows(r):
            for u in range(0, width, sub):
                here_u = slice(u, u + sub)
                h = hot[r, here_u, :]
                mk = m0 + h * (m1 - m0)
                by_truth = tc0 + h * (tc1 - tc0) + mk * acc[1, r, here_u, :]
                by_smooth = sc0 + h * (sc1 - sc0) + mk * acc[2, r, here_u, :]
                pad[slot, r + 1, 8 + u : 8 + u + sub, :] = (
                    by_truth * sp[k, r, here_u, :] + by_smooth * sm[k, r, here_u, :]
                )

        loop(t_rows, rows)
        for side, ok, row, to in halo_routes():
            @pl.when(ok)
            def _(side=side, row=row, to=to):
                hq[side, k] = pad[slot, row + 1, mid, :].astype(BF16)
                remote(hq.at[side, k], hd.at[side, k], o["hd_s"].at[side, k], o["hd_r"].at[side, k], to).start()

        send_edges(slot, 1, k, range(1, t_rows + 1))

    def diff_border(k):
        slot = rem(k, 2)
        for side, ok, row in sides:
            @pl.when(ok)
            def _(side=side, row=row):
                wait(hd.at[side, k], o["hd_r"].at[side, k])
                pad[slot, row, mid, :] = hd[side, k].astype(F32)

            @pl.when(jnp.logical_not(ok))
            def _(row=row):
                pad[slot, row, mid, :] = jnp.zeros((width, LANES), F32)

        send_edges(slot, 2, k, (0, t_rows + 1))

    back = cz + 1 - 2 * od

    def diff_pred(k, rows):
        slot = rem(k, 2)
        for r in rows:
            for u in range(0, width, sub):
                here_u = slice(u, u + sub)
                a = pad[slot, r + 1, 8 + u : 8 + u + sub, :]
                for j, (dr, dc) in enumerate(OFFSETS):
                    w = cb[j, r, here_u, :].astype(F32)
                    a = a + w * pad[slot, r + 1 - dr, 8 - dc + u : 8 - dc + u + sub, :]
                low = a.astype(BF16)
                dd[od, k, r, here_u, :] = low
                acc[0, r, here_u, :] = acc[0, r, here_u, :] + gg[k, r, here_u, :] * low.astype(F32)
            at = dd.at[od, k, r]
            remote(at, at, o["d_s"].at[od, k, r], o["d_r"].at[od, k, r], (sx, sy, back)).start()

    def back_chunk(q):
        i = rem(q, t_rows)
        return div(q, t_rows), jnp.where(i < t_rows - 2, i + 1, jnp.where(i == t_rows - 2, 0, i))

    def spot_rows(i):
        return [
            jnp.sum(acc[i, r, h * LANES : (h + 1) * LANES, :].T, axis=0, keepdims=True)
            for r in range(t_rows)
            for h in range(wl)
        ]

    def plane_peer(j):
        t = rem(here + j + 1, nplane)
        return t, (div(t, nsy), rem(t, nsy), cz)

    def put_own(i):
        k = own_block(cz, i)
        return pltpu.make_async_copy(gg.at[k], gp.at[:, :, i * LANES : (i + 1) * LANES], o["gp_m"].at[i])

    @pl.when(owner)
    def _():
        prepare(nb - 1)
        smoothing(nb - 1)

        def send_genes(j):
            _, to = plane_peer(j)
            remote(gs, gr.at[here], o["g_s"].at[j], o["g_r"].at[here], to).start()

        loop(nplane - 1, send_genes)
        for i in range(3):
            for at, row in enumerate(spot_rows(i)):
                spx[0, i, at : at + 1, :] = row
        remote(spx.at[0], spx.at[1], o["x_s"].at[0], o["x_r"].at[0], (sx, sy, n - 1 - cz)).start()
        if early_pred:
            for i in range(early_pred, wb):
                send_pred(i)
        gr[here] = gs[...]
        for i in range(wb):
            put_own(i).start()

        def wait_genes(j):
            t, _ = plane_peer(j)
            wait(gr.at[t], o["g_r"].at[t])

        loop(nplane - 1, wait_genes)
        count = jnp.maximum(jnp.sum(gmask[...].astype(F32), axis=1, keepdims=True), 1.0)

        def genes(k, gl):
            tot = gr[0, k]
            for t in range(1, nplane):
                tot = tot + gr[t, k]
            ib, ic = lax.rsqrt(tot[2:4] + EPS), lax.rsqrt(tot[4:6] + EPS)
            cos = tot[0:2] * ib * ic
            at = pl.ds(pl.multiple_of(gene_block(od, k) * LANES, LANES), LANES)
            mask = gmask[:, at].astype(F32)
            scale = -mask / (2.0 * count)
            gc[k, 0:2, :] = scale * ib * ic
            gc[k, 2:4, :] = -scale * cos * ib * ib
            gc[k, 4:6, :] = mask
            return gl + mask * cos / count

        gl = lax.fori_loop(0, nb, genes, jnp.zeros((2, LANES), F32))
        gene_part = jnp.sum(jnp.sum(gl, axis=0, keepdims=True), axis=1, keepdims=True)

        wait(spx.at[1], o["x_r"].at[0])
        a, b, c = (spx[0, i] + spx[1, i] for i in range(3))
        ib, ic = lax.rsqrt(b + EPS), lax.rsqrt(c + EPS)
        cos = a * ib * ic
        by_truth = (-1.0 / all_spots) * ib * ic
        by_smooth = (1.0 / all_spots) * cos * ib * ib
        for r in range(t_rows):
            for h in range(wl):
                at, i = slice(h * LANES, (h + 1) * LANES), r * wl + h
                acc[1, r, at, :] = spread(by_truth[i : i + 1])
                acc[2, r, at, :] = spread(by_smooth[i : i + 1])
        acc[0] = jnp.zeros(acc.shape[1:], F32)
        spot_part = jnp.sum(jnp.sum(cos, axis=0, keepdims=True), axis=1, keepdims=True)
        spr[here] = jnp.broadcast_to(spot_part, (8, LANES))

        def send_spot(j):
            _, to = plane_peer(j)
            remote(spr.at[here], spr.at[here], o["p_s"].at[j], o["p_r"].at[here], to).start()

        diff_inside(0)
        loop(nplane - 1, send_spot)

        def produce(k):
            take_edges(rem(k, 2), 1, k, range(1, t_rows + 1))
            diff_pred(k, range(1, t_rows - 1))

            @pl.when(k + 1 < nb)
            def _():
                diff_inside(k + 1)

            diff_border(k)
            take_edges(rem(k, 2), 2, k, (0, t_rows + 1))
            diff_pred(k, (0, t_rows - 1))

        loop(nb, produce)

        def wait_spot(j):
            t, _ = plane_peer(j)
            wait(spr.at[t], o["p_r"].at[t])

        loop(nplane - 1, wait_spot)
        spot_all = spr[0, 0:1, :]
        for t in range(1, nplane):
            spot_all = spot_all + spr[t, 0:1, :]
        rows = spot_rows(0)
        if len(rows) < 8:
            rows.append(jnp.zeros((8 - len(rows), LANES), F32))
        fm[od, 0] = jnp.concatenate(rows, axis=0)
        last = [jnp.broadcast_to(gene_part, (1, LANES)), spot_all, jnp.zeros((6, LANES), F32)]
        fm[od, 1] = jnp.concatenate(last, axis=0)
        remote(fm.at[od], fm.at[od], o["f_s"].at[od], o["f_r"].at[od], (sx, sy, back)).start()
        if not early_pred:
            for i in range(wb):
                send_pred(i)


    sy_bit, sx_bit = div(sx, 2), rem(sx, 2)
    over_y, over_x = (sx + 2 - 4 * sy_bit, sy, cz), (sx + 1 - 2 * sx_bit, sy, cz)

    def place(k):
        jj = div(k, bpg)
        hi = div(jj, 2)
        return rem(jj, 2) == sy, hi * bpg + rem(k, bpg), jnp.where(sy_bit == 0, 1 - hi, hi) == sx_bit

    halves = (pl.ds(0, c_rows // 2), pl.ds(c_rows // 2, c_rows // 2))

    def add_rows(dst, a, b):
        count = dst.shape[0] // 2

        def rows(i):
            at = pl.ds(pl.multiple_of(i * count, 8), count)
            dst[at, :] = (a[at, :].astype(F32) + b[at, :].astype(F32)).astype(dst.dtype)

        loop(2, rows)

    def scatter_0(k):
        mine, at, _ = place(k)

        @pl.when(jnp.logical_not(mine))
        def _():
            for d in range(2):
                remote(pss.at[rem(k, 2), d], rs1.at[d, at], o["r1_s"].at[d, at], o["r1_r"].at[d, at], mate).start()

    def stays(final):
        return sy_bit, jnp.where(final, sy_bit, 1 - sy_bit)

    def scatter_1(k):
        mine, at, final = place(k)

        @pl.when(mine)
        def _():
            def each(d):
                wait(rs1.at[d, at], o["r1_r"].at[d, at])
                add_rows(rs1.at[d, at], pss.at[rem(k, 2), d], rs1.at[d, at])

            loop(2, each)
            for h, (d, to) in enumerate(zip(stays(final), (over_y, over_x), strict=True)):
                src, dst = rs1.at[1 - d, at, halves[h]], rs2.at[at, halves[h]]
                remote(src, dst, o["r2_s"].at[h, at], o["r2_r"].at[h, at], to).start()

        @pl.when(jnp.logical_not(mine))
        def _():
            for d in range(2):
                wait(pss.at[rem(k, 2), d], o["r1_s"].at[d, at])

    def scatter_2(k):
        mine, at, final = place(k)

        @pl.when(mine)
        def _():
            i = rem(k, bpg)
            for h, (d, to) in enumerate(zip(stays(final), (over_x, over_y), strict=True)):
                part = rs2.at[at, halves[h]]
                wait(part, o["r2_r"].at[h, at])
                add_rows(part, rs1.at[d, at, halves[h]], part)

                @pl.when(jnp.logical_not(final))
                def _(h=h, part=part, to=to):
                    remote(part, rs3.at[i, halves[h]], o["r3_s"].at[h, i], o["r3_r"].at[h, i], to).start()

            for h, d in enumerate(stays(final)):
                wait(rs1.at[1 - d, at, halves[h]], o["r2_s"].at[h, at])

    def put_cells(i):
        at = pl.ds(pl.multiple_of(i * LANES, LANES), LANES)
        return pltpu.make_async_copy(dcv.at[i], dcell.at[:, at], o["dc_m"].at[i])

    def scatter_3(k):
        mine, at, final = place(k)
        i = rem(k, bpg)

        @pl.when(mine & final)
        def _():
            for h in range(2):
                wait(rs3.at[i, halves[h]], o["r3_r"].at[h, i])
                add_rows(dcv.at[i, halves[h]], rs2.at[at, halves[h]], rs3.at[i, halves[h]])
            put_cells(i).start()

        @pl.when(mine & jnp.logical_not(final))
        def _():
            for h in range(2):
                wait(rs2.at[at, halves[h]], o["r3_s"].at[h, i])

    def multiply(k, piece):
        x = jnp.concatenate([xs[gene_block(0, k)], xs[gene_block(1, k)]], axis=1)
        d = jnp.concatenate([dd[0, k, piece], dd[1, k, piece]], axis=1)
        dm[piece] += lax.dot_general(x, d, (((1,), (1,)), ((), ())), preferred_element_type=F32)
        at = pl.ds(pl.multiple_of(piece * quarter, 16 if quarter % 16 == 0 else 8), quarter)
        d = jnp.concatenate([dd[i, k].reshape(spots, LANES) for i in range(2)], axis=1)
        out = jnp.dot(mm[at, :], d, preferred_element_type=F32).astype(BF16)
        pss[rem(k, 2), 0, at, :] = out[:, :LANES]
        pss[rem(k, 2), 1, at, :] = out[:, LANES:]

    def put_logits(r):
        return pltpu.make_async_copy(dm.at[r], dlog.at[:, r, :], o["dl_m"].at[r])

    def finish(r):
        col = jnp.concatenate([fm[0, 0, i : i + 1] + fm[1, 0, i : i + 1] for i in range(r * wl, (r + 1) * wl)], axis=1)

        def rows(i):
            at = pl.ds(pl.multiple_of(i * tile, tile), tile)
            low = mm[at, r * width : (r + 1) * width].astype(F32)
            dm[r, at, :] = low * (dm[r, at, :] - col)

        loop(c_rows // tile, rows)
        put_logits(r).start()

    def put_pred(i):
        return pltpu.make_async_copy(gg.at[i], gp.at[:, :, i * LANES : (i + 1) * LANES], o["gp_m"].at[i])

    def take_pred(i):
        wait(gpr.at[i], o["gp_r"].at[i])
        wait(gps.at[i], o["gq_r"].at[i])

        def rows(r):
            gg[i, r] = gpr[i, r].astype(I32).astype(F32) * gps[i, r]

        loop(t_rows, rows)
        put_pred(i).start()

    lag = jnp.where(owner, 0, 2 * jnp.maximum(cz - 1, n - 2 - cz))

    def back_step(s):
        def direction(d):
            own, end = cz == d * (n - 1), cz == (1 - d) * (n - 1)
            off = jnp.where(owner, 0, jnp.where(d == 0, 2 * (cz - 1), 2 * (n - 2 - cz)))
            q = s - off
            to = (sx, sy, cz + 1 - 2 * d)

            @pl.when(jnp.logical_not(own) & (q >= 0) & (q < nb * t_rows))
            def _():
                k, r = back_chunk(q)
                at = dd.at[d, k, r]
                wait(at, o["d_r"].at[d, k, r])

                @pl.when(jnp.logical_not(end))
                def _():
                    remote(at, at, o["d_s"].at[d, k, r], o["d_r"].at[d, k, r], to).start()

            @pl.when(jnp.logical_not(own) & (q == nb * t_rows))
            def _():
                wait(fm.at[d], o["f_r"].at[d])

                @pl.when(jnp.logical_not(end))
                def _():
                    remote(fm.at[d], fm.at[d], o["f_s"].at[d], o["f_r"].at[d], to).start()

        loop(2, direction)
        w = s - lag - t_rows
        k, piece = div(w, t_rows), rem(w, t_rows)

        @pl.when((w >= 0) & (k < nb))
        def _():
            multiply(k, piece)

            @pl.when(piece == t_rows - 1)
            def _():
                scatter_0(k)

        @pl.when((w >= 0) & (k == nb))
        def _():
            for r in range(t_rows):
                @pl.when(piece == r)
                def _(r=r):
                    finish(r)

        for stage, back_by, at in ((scatter_1, 1, 0), (scatter_2, 2, 1), (scatter_3, 3, 2)):
            @pl.when((w >= 0) & (piece == at) & (k >= back_by) & (k < nb + back_by))
            def _(stage=stage, back_by=back_by):
                stage(k - back_by)

    loop(t_rows * (nb + 4) + 2 * lead, back_step)

    losses[0] = jnp.max(fm[0, 1, 0:1, :] + fm[1, 1, 0:1, :]) * -0.5
    losses[1] = jnp.max(fm[0, 1, 1:2, :]) * (-1.0 / all_spots)

    @pl.when(jnp.logical_not(owner))
    def _():
        for i in range(wb):
            take_pred(i)

    for r in range(t_rows):
        put_logits(r).wait()
    for i in range(bpg):
        put_cells(i).wait()
    loop(n - 1, lambda j: wait(srow.at[cz], o["s_s"].at[j]))

    def sent(d):
        own, end = cz == d * (n - 1), cz == (1 - d) * (n - 1)

        @pl.when(jnp.logical_not(own))
        def _():
            def each(q):
                k, r = div(q, t_rows), rem(q, t_rows)
                wait(ab.at[d, k, r], o["a_s"].at[d, k, r])
                wait(sc.at[d, k, r], o["c_s"].at[d, k, r])

            loop(nb * t_rows, each)

        @pl.when(jnp.logical_not(end))
        def _():
            def each(q):
                k, r = div(q, t_rows), rem(q, t_rows)
                wait(dd.at[d, k, r], o["d_s"].at[d, k, r])

            loop(nb * t_rows, each)
            wait(fm.at[d], o["f_s"].at[d])

    loop(2, sent)

    @pl.when(jnp.logical_not(owner))
    def _():
        for i in range(wb):
            put_pred(i).wait()

    @pl.when(owner)
    def _():
        for i in range(wb):
            put_own(i).wait()

            def each(j, i=i):
                for copy in pred_copies(i, j):
                    copy.wait_send()

            loop(n // 2 - 1, each)
        for slot, ok, _ in coef_routes():
            @pl.when(ok)
            def _(slot=slot):
                wait(con, o["co_s"].at[slot])

        def each(k):
            for side, ok, row, _ in halo_routes():
                @pl.when(ok)
                def _(side=side, row=row):
                    wait(ab.at[od, k, row], o["hg_s"].at[side, k])
                    wait(sc.at[od, k, row], o["hs_s"].at[side, k])
                    wait(hq.at[side, k], o["hd_s"].at[side, k])

            for which in range(3):
                wait(es.at[which, k], o["e_s"].at[which, k])

        loop(nb, each)
        wait(spx.at[0], o["x_s"].at[0])

        def each_peer(j):
            wait(gs, o["g_s"].at[j])
            wait(spr.at[here], o["p_s"].at[j])

        loop(nplane - 1, each_peer)


def per_device(logits, cells_expr, spatial, gene_mask, slide_id, edge_weight, edge_mask):
    c_rows, t_rows, width = logits.shape
    genes = cells_expr.shape[1]
    n, nsx, nsy = (lax.axis_size(a) for a in ("cells", "sx", "sy"))
    spots = t_rows * width
    share = genes // n
    wide = max(share, LANES)
    wb = wide // LANES
    nb = genes // 2 // LANES
    nplane = nsx * nsy
    grid = (t_rows, width, LANES)
    vm, dma = pltpu.VMEM, pltpu.SemaphoreType.DMA
    scratch = dict(
        xs=vm((2 * nb, c_rows, LANES), BF16),
        mm=vm((c_rows, spots), BF16),
        mt=vm((t_rows, width, c_rows), BF16),
        dm=vm((t_rows, c_rows, width), F32),
        srow=vm((n, spots // LANES, LANES), F32),
        ab=vm((2, nb, *grid), I16),
        sc=vm((2, nb, t_rows, 1, LANES), F32),
        tt=vm((2, 2, *grid), F32),
        gg=vm((nb, *grid), F32),
        sm=vm((nb, *grid), F32),
        sp=vm((nb, *grid), F32),
        pad=vm((2, t_rows + 2, width + 16, LANES), F32),
        hg=vm((2, nb, width, LANES), I16),
        hs=vm((2, nb, 1, LANES), F32),
        hd=vm((2, nb, width, LANES), BF16),
        hq=vm((2, nb, width, LANES), BF16),
        es=vm((3, nb, 8, LANES), F32),
        er=vm((3, nb, 8, LANES), F32),
        cf=vm((6, *grid), F32),
        cb=vm((6, *grid), BF16),
        hot=vm(grid, F32),
        con=vm((t_rows, 8, width), F32),
        cor=vm((5, t_rows, 8, width), F32),
        acc=vm((3, *grid), F32),
        gs=vm((nb, 8, LANES), F32),
        gr=vm((nplane, nb, 8, LANES), F32),
        spx=vm((2, 3, spots // LANES, LANES), F32),
        gc=vm((nb, 8, LANES), F32),
        spr=vm((nplane, 8, LANES), F32),
        dd=vm((2, nb, *grid), BF16),
        fm=vm((2, 2, 8, LANES), F32),
        pss=vm((2, 2, c_rows, LANES), BF16),
        rs1=vm((2, nb // 2, c_rows, LANES), BF16),
        rs2=vm((nb // 2, c_rows, LANES), BF16),
        rs3=vm((nb // 4, c_rows, LANES), BF16),
        dcv=vm((nb // 4, c_rows, LANES), F32),
        gpr=vm((wb, *grid), I16),
        gps=vm((wb, t_rows, 1, LANES), F32),
        lg_m=dma((t_rows,)),
        xs_m=dma((2 * nb,)),
        sp_m=dma((nb,)),
        s_s=dma((n,)),
        s_r=dma((n,)),
        a_s=dma((2, nb, t_rows)),
        a_r=dma((2, nb, t_rows)),
        c_s=dma((2, nb, t_rows)),
        c_r=dma((2, nb, t_rows)),
        hg_s=dma((2, nb)),
        hg_r=dma((2, nb)),
        hs_s=dma((2, nb)),
        hs_r=dma((2, nb)),
        hd_s=dma((2, nb)),
        hd_r=dma((2, nb)),
        e_s=dma((3, nb)),
        e_r=dma((3, nb)),
        co_s=dma((5,)),
        co_r=dma((5,)),
        g_s=dma((nplane,)),
        g_r=dma((nplane,)),
        p_s=dma((nplane,)),
        p_r=dma((nplane,)),
        x_s=dma((1,)),
        x_r=dma((1,)),
        d_s=dma((2, nb, t_rows)),
        d_r=dma((2, nb, t_rows)),
        f_s=dma((2,)),
        f_r=dma((2,)),
        r1_s=dma((2, nb // 2)),
        r1_r=dma((2, nb // 2)),
        r2_s=dma((2, nb // 2)),
        r2_r=dma((2, nb // 2)),
        r3_s=dma((2, nb // 4)),
        r3_r=dma((2, nb // 4)),
        gp_s=dma((max(n // 2 - 1, 1), wb)),
        gp_r=dma((wb,)),
        gq_s=dma((max(n // 2 - 1, 1), wb)),
        gq_r=dma((wb,)),
        gp_m=dma((wb,)),
        dl_m=dma((t_rows,)),
        dc_m=dma((nb // 4,)),
    )
    names = ("lg", "cells", "spat", "gmask", "slide", "ew", "em", "losses", "gp", "dlog", "dcell")
    names += tuple(scratch)
    sizes = (n, nsx, nsy, share, spots * nplane)
    anywhere, local = pl.BlockSpec(memory_space=pl.ANY), pl.BlockSpec(memory_space=pltpu.VMEM)
    losses, pred, d_logits, d_cells = pl.pallas_call(
        functools.partial(kernel, names, sizes),
        out_shape=(
            jax.ShapeDtypeStruct((2,), F32),
            jax.ShapeDtypeStruct((t_rows, width, wide), F32),
            jax.ShapeDtypeStruct(logits.shape, F32),
            jax.ShapeDtypeStruct((c_rows, genes // nplane), F32),
        ),
        in_specs=[anywhere] * 3 + [local] * 4,
        out_specs=(pl.BlockSpec(memory_space=pltpu.SMEM), anywhere, anywhere, anywhere),
        scratch_shapes=list(scratch.values()),
        compiler_params=pltpu.CompilerParams(
            collective_id=0, has_side_effects=True, vmem_limit_bytes=VMEM
        ),
        cost_estimate=pl.CostEstimate(
            flops=6 * c_rows * spots * genes, bytes_accessed=32 << 20, transcendentals=c_rows * spots
        ),
    )(logits, cells_expr, spatial, gene_mask, slide_id, edge_weight, edge_mask)
    if wide > share:
        pred = lax.dynamic_slice_in_dim(pred, rem(lax.axis_index("cells") * share, wide), share, 2)
    return (losses, pred, d_logits, d_cells)


VMEM = 64 * 1024 * 1024 - 512 * 1024


def solution(mesh):
    return jax.shard_map(
        per_device,
        mesh=mesh,
        in_specs=(
            P("cells", "sx", "sy"),
            P("cells", None),
            P("sx", "sy", None),
            P(),
            P("sx", "sy"),
            P(None, "sx", "sy"),
            P(None, "sx", "sy"),
        ),
        out_specs=(P(), P("sx", "sy", "cells"), P("cells", "sx", "sy"), P("cells", ("sx", "sy"))),
        check_vma=False,
    )
```

```python
import functools

import jax
import jax.numpy as jnp
from jax import lax
from jax.experimental import pallas as pl
from jax.experimental.pallas import tpu as pltpu
from jax.sharding import PartitionSpec as P

EPS = 1e-06
OFFSETS = ((0, 1), (0, -1), (1, 0), (-1, 0), (-1, 1), (1, -1))
LANES = 128
TOP = 32767.0
MESH = pl.DeviceIdType.MESH
F32, BF16, I16, I32 = jnp.float32, jnp.bfloat16, jnp.int16, jnp.int32
rem, div = lax.rem, lax.div


def loop(count, body):
    lax.fori_loop(0, count, lambda i, _: (body(i), 0)[1], 0)


def remote(src, dst, sent, got, to):
    return pltpu.make_async_remote_copy(
        src_ref=src, dst_ref=dst, send_sem=sent, recv_sem=got, device_id=to, device_id_type=MESH
    )


def wait(ref, sem):
    pltpu.make_async_copy(ref, ref, sem).wait()


def spread(row):
    parts = [
        jnp.broadcast_to(row[:, at : at + LANES], (LANES, LANES)).T
        for at in range(0, row.shape[1], LANES)
    ]
    return jnp.concatenate(parts, axis=0)


def fold(x):
    return jnp.sum(x.reshape(x.shape[0] // 8, 8, x.shape[1]), axis=0)


def kernel(names, sizes, *refs):
    n, nsx, nsy, share, all_spots = sizes
    o = dict(zip(names, refs, strict=True))
    lg, cells, spat, gmask, slide, ew, em = (o[k] for k in names[:7])
    losses, gp, dlog, dcell = (o[k] for k in names[7:11])
    xs, mm, mt, dm, srow, ab, sc, tt = (o[k] for k in names[11:19])
    gg, sm, sp, pad, hg, hs, hd, hq = (o[k] for k in names[19:27])
    es, er, cf, cb, hot, con, cor, acc = (o[k] for k in names[27:35])
    gs, gr, spx, gc, spr, dd, fm = (o[k] for k in names[35:42])
    pss, rs1, rs2, rs3, dcv, gpr, gps = (o[k] for k in names[42:49])

    c_rows, t_rows, width = lg.shape
    spots = t_rows * width
    nb = cells.shape[1] // 2 // LANES
    wl = width // LANES
    wb = gpr.shape[0]
    nplane = nsx * nsy
    half = nb // 2
    bpg = nb // 4
    tile = LANES
    tiles = c_rows // tile
    quarter = c_rows // t_rows
    sub = min(64, width)
    mid = slice(8, 8 + width)

    sx, sy, cz = (lax.axis_index(a) for a in ("sx", "sy", "cells"))
    here = sx * nsy + sy
    owner = (cz == 0) | (cz == n - 1)
    od = jnp.where(cz == 0, 0, 1)
    up, down = sx > 0, sx < nsx - 1
    mate = (sx, 1 - sy, cz)

    def gene_block(d, k):
        return jnp.where(d == 0, rem(k + half, nb), nb + k)

    for r in range(t_rows):
        pltpu.make_async_copy(lg.at[:, r, :], dm.at[r], o["lg_m"].at[r]).start()

    def load_cells(b):
        at = pl.ds(pl.multiple_of(b * LANES, LANES), LANES)
        return pltpu.make_async_copy(cells.at[:, at], xs.at[b], o["xs_m"].at[b])

    loop(2 * nb, lambda b: load_cells(b).start())

    def load_truth(k):
        at = pl.ds(pl.multiple_of(gene_block(od, k) * LANES, LANES), LANES)
        return pltpu.make_async_copy(spat.at[:, :, at], sp.at[k], o["sp_m"].at[k])

    @pl.when(owner)
    def _():
        loop(nb, lambda k: load_truth(k).start())

    barrier = pltpu.get_barrier_semaphore()

    def greet_line(j):
        to = (sx, sy, rem(cz + j + 1, n))
        pl.semaphore_signal(barrier, inc=1, device_id=to, device_id_type=MESH)

    def greet_plane(j):
        t = rem(here + j + 1, nplane)
        to = (div(t, nsy), rem(t, nsy), cz)
        pl.semaphore_signal(barrier, inc=1, device_id=to, device_id_type=MESH)

    loop(n - 1, greet_line)
    loop(nplane - 1, greet_plane)

    for r in range(t_rows):
        pltpu.make_async_copy(lg.at[:, r, :], dm.at[r], o["lg_m"].at[r]).wait()

        def exps(i, s, r=r):
            at = pl.ds(i * tile, tile)
            x = jnp.exp(dm[r, at, :])
            dm[r, at, :] = x
            return s + fold(x)

        s = lax.fori_loop(0, c_rows // tile, exps, jnp.zeros((8, width), F32))
        s = jnp.sum(s, axis=0, keepdims=True)
        for h in range(wl):
            srow[cz, pl.ds(r * wl + h, 1), :] = s[:, h * LANES : (h + 1) * LANES]

    pl.semaphore_wait(barrier, n - 1 + nplane - 1)

    def send_sums(j):
        to = (sx, sy, rem(cz + j + 1, n))
        remote(srow.at[cz], srow.at[cz], o["s_s"].at[j], o["s_r"].at[cz], to).start()

    loop(n - 1, send_sums)

    def turn(dst, first):
        def each(i):
            for r in range(t_rows):
                at = pl.ds(pl.multiple_of((i + first) * LANES, LANES), LANES)
                dst[i, r] = dm[r, at, :].T

        return each

    turned = ((gg, 0, min(tiles, nb)), (sm, nb, max(tiles - nb, 0)))
    for dst, first, count in turned:
        loop(count, turn(dst, first))

    def wait_sums(j):
        z = rem(cz + j + 1, n)
        wait(srow.at[z], o["s_r"].at[z])

    loop(n - 1, wait_sums)
    total = srow[0]
    for z in range(1, n):
        total = total + srow[z]
    inv = 1.0 / total
    inv_rows = [
        jnp.concatenate([inv[r * wl + h : r * wl + h + 1] for h in range(wl)], axis=1)
        for r in range(t_rows)
    ]
    for r in range(t_rows):
        acc[0, r] = spread(inv_rows[r])

    for dst, first, count in turned:
        def scale(i, dst=dst, first=first):
            at = pl.ds(pl.multiple_of((i + first) * LANES, LANES), LANES)
            for r in range(t_rows):
                mt[r, :, at] = (dst[i, r] * acc[0, r]).astype(BF16)

        loop(count, scale)

    def keep_mapping():
        for r in range(t_rows):
            def each(i, r=r):
                at = pl.ds(pl.multiple_of(i * LANES, LANES), LANES)
                mm[at, r * width : (r + 1) * width] = (dm[r, at, :] * inv_rows[r]).astype(BF16)

            loop(tiles, each)

    loop(2 * nb, lambda b: load_cells(b).wait())
    keep_mapping()

    def coef_routes():
        return (
            (0, down, (sx + 1, sy, cz)),
            (1, up, (sx - 1, sy, cz)),
            (2, sx >= 0, mate),
            (3, down, (sx + 1, 1 - sy, cz)),
            (4, up, (sx - 1, 1 - sy, cz)),
        )

    ahead = dm if tt.shape[0] == 1 else tt

    def predict(d, pair, r):
        g = gene_block(d, 2 * pair)
        w = jnp.concatenate([xs[g], xs[g + 1]], axis=1)
        at = pl.ds(pl.multiple_of((2 * d + rem(pair, 2)) * width, 8), width)
        ahead[r, at, :] = jnp.dot(mt[r], w, preferred_element_type=F32)

    def predicted(d, k, r):
        at = pl.ds(pl.multiple_of((2 * d + rem(div(k, 2), 2)) * width, 8), width)
        return ahead[r, at, pl.ds(pl.multiple_of(rem(k, 2) * LANES, LANES), LANES)]

    def put(d, k, r, t):
        top = jnp.maximum(jnp.max(jnp.abs(t), axis=0, keepdims=True), 1e-30)
        ab[d, k, r] = jnp.round(t * (TOP / top)).astype(I32).astype(I16)
        sc[d, k, r] = top * (1.0 / TOP)

    def pass_on(d, k, r):
        to = (sx, sy, cz + 2 * d - 1)
        remote(ab.at[d, k, r], ab.at[d, k, r], o["a_s"].at[d, k, r], o["a_r"].at[d, k, r], to).start()
        remote(sc.at[d, k, r], sc.at[d, k, r], o["c_s"].at[d, k, r], o["c_r"].at[d, k, r], to).start()

    def chunk_of(q):
        return div(q, t_rows), rem(rem(q, t_rows) * (t_rows - 1), t_rows)

    @pl.when(owner)
    def _():
        d = 1 - od

        def first(q):
            k, r = chunk_of(q)

            @pl.when(rem(k, 2) == 0)
            def _():
                predict(d, div(k, 2), r)

            put(d, k, r, predicted(d, k, r))
            pass_on(d, k, r)

        loop(nb * t_rows, first)

        for r in range(t_rows):
            rows = [ew[j, r : r + 1, :] * em[j, r : r + 1, :].astype(F32) for j in range(6)]
            con[r] = jnp.concatenate(rows + [jnp.zeros((2, width), F32)], axis=0)
            for j in range(6):
                cf[j, r] = spread(rows[j])
            hot[r] = spread(slide[r : r + 1, :].astype(F32))
        acc[...] = jnp.zeros(acc.shape, F32)

        for slot, ok, to in coef_routes():
            @pl.when(ok)
            def _(slot=slot, to=to):
                remote(con, cor.at[slot], o["co_s"].at[slot], o["co_r"].at[slot], to).start()

        loop(nb, lambda k: load_truth(k).wait())

    def back_coefs():
        for slot, ok in ((0, up), (1, down), (2, sx >= 0), (3, up), (4, down)):
            @pl.when(ok)
            def _(slot=slot):
                wait(cor.at[slot], o["co_r"].at[slot])

        lane = lax.broadcasted_iota(I32, (8, width), 1)
        for j, (dr, dc) in enumerate(OFFSETS):
            for r in range(t_rows):
                at = r - dr
                if at < 0:
                    base, side, ok = cor[0, t_rows - 1], cor[3, t_rows - 1], up
                elif at >= t_rows:
                    base, side, ok = cor[1, 0], cor[4, 0], down
                else:
                    base, side, ok = con[at], cor[2, at], sx >= 0
                base = jnp.where(ok, base, 0.0)
                if dc:
                    by, edge = (1, 0) if dc == 1 else (width - 1, width - 1)
                    side = jnp.where(ok & (sy == (1 if dc == 1 else 0)), side, 0.0)
                    base = jnp.where(lane == edge, pltpu.roll(side, by, 1), pltpu.roll(base, by, 1))
                cb[j, r] = spread(base[j : j + 1]).astype(BF16)

    def send_edges(slot, which, k, rows):
        parts = [
            jnp.where(sy == 1, pad[slot, row, 8:9, :], pad[slot, row, 7 + width : 8 + width, :])
            for row in rows
        ]
        parts.append(jnp.zeros((8 - len(parts), LANES), F32))
        es[which, k] = jnp.concatenate(parts, axis=0)
        remote(es.at[which, k], er.at[which, k], o["e_s"].at[which, k], o["e_r"].at[which, k], mate).start()

    def take_edges(slot, which, k, rows):
        wait(er.at[which, k], o["e_r"].at[which, k])
        for i, row in enumerate(rows):
            edge = er[which, k, i : i + 1, :]
            pad[slot, row, 8 + width : 9 + width, :] = jnp.where(sy == 0, edge, 0.0)
            pad[slot, row, 7:8, :] = jnp.where(sy == 1, edge, 0.0)

    sides = ((0, up, 0), (1, down, t_rows + 1))

    def prepare(k):
        for side, ok, row in sides:
            @pl.when(ok)
            def _(side=side, row=row):
                wait(hg.at[side, k], o["hg_r"].at[side, k])
                wait(hs.at[side, k], o["hs_r"].at[side, k])
                pad[0, row, mid, :] = hg[side, k].astype(I32).astype(F32) * hs[side, k]

            @pl.when(jnp.logical_not(ok))
            def _(row=row):
                pad[0, row, mid, :] = jnp.zeros((width, LANES), F32)

        def rows(r):
            pad[0, r + 1, mid, :] = gg[k, r]

        loop(t_rows, rows)
        send_edges(0, 0, k, range(t_rows + 2))

    def smoothing(k):
        take_edges(0, 0, k, range(t_rows + 2))
        at = pl.ds(pl.multiple_of(gene_block(od, k) * LANES, LANES), LANES)
        mask = gmask[:, at].astype(F32)
        m0, m1 = mask[0:1], mask[1:2]

        def rows(r, sums):
            sums = list(sums)
            for u in range(0, width, sub):
                here_u = slice(u, u + sub)
                a = pad[0, r + 1, 8 + u : 8 + u + sub, :]
                for j, (dr, dc) in enumerate(OFFSETS):
                    a = a + cf[j, r, here_u, :] * pad[0, r + 1 + dr, 8 + dc + u : 8 + dc + u + sub, :]
                sm[k, r, here_u, :] = a
                t = sp[k, r, here_u, :]
                h = hot[r, here_u, :]
                mk = m0 + h * (m1 - m0)
                for i, x in enumerate((a * t, a * a, t * t)):
                    sums[2 * i] = sums[2 * i] + fold(x)
                    sums[2 * i + 1] = sums[2 * i + 1] + fold(x * h)
                    acc[i, r, here_u, :] = acc[i, r, here_u, :] + x * mk
            return tuple(sums)

        sums = lax.fori_loop(0, t_rows, rows, (jnp.zeros((8, LANES), F32),) * 6)
        parts = []
        for i in range(3):
            both = jnp.sum(sums[2 * i], axis=0, keepdims=True)
            one = jnp.sum(sums[2 * i + 1], axis=0, keepdims=True)
            parts += [both - one, one]
        gs[k] = jnp.concatenate(parts + [jnp.zeros((2, LANES), F32)], axis=0)

    def own_block(t, i):
        b = div(t * share, LANES) + i - od * nb
        return jnp.where(od == 0, rem(b + half, nb), b)

    def pred_copies(i, j):
        t = jnp.where(od == 0, j + 1, n - 2 - j)
        k = own_block(t, i)
        to = (sx, sy, t)
        return (
            remote(ab.at[od, k], gpr.at[i], o["gp_s"].at[j, i], o["gp_r"].at[i], to),
            remote(sc.at[od, k], gps.at[i], o["gq_s"].at[j, i], o["gq_r"].at[i], to),
        )

    def send_pred(i):
        def each(j):
            for copy in pred_copies(i, j):
                copy.start()

        loop(n // 2 - 1, each)

    early_pred = 1 if n == 4 else 0

    def plane_peer(j):
        t = rem(here + j + 1, nplane)
        return t, (div(t, nsy), rem(t, nsy), cz)

    gene_parts = (pl.ds(0, nb - 1), pl.ds(nb - 1, 1))

    def send_genes(part):
        at = gene_parts[part]

        def each(j):
            _, to = plane_peer(j)
            sems = o["g_s"].at[part, j], o["g_r"].at[part, here]
            remote(gs.at[at], gr.at[here, at], *sems, to).start()

        loop(nplane - 1, each)

    lead = max(n - 3, 0)

    def sum_step(s):
        def direction(d):
            own, first = cz == d * (n - 1), cz == (1 - d) * (n - 1)
            off = jnp.where(owner, 0, LAG_SUM * jnp.where(d == 1, cz - 1, n - 2 - cz))
            q = s - off

            @pl.when(jnp.logical_not(first) & (q >= 0) & (q < nb * t_rows))
            def _():
                k, r = chunk_of(q)
                wait(ab.at[d, k, r], o["a_r"].at[d, k, r])
                wait(sc.at[d, k, r], o["c_r"].at[d, k, r])
                got = ab[d, k, r].astype(I32).astype(F32) * sc[d, k, r]
                t = predicted(d, k, r) + got
                put(d, k, r, t)

                @pl.when(jnp.logical_not(own))
                def _():
                    pass_on(d, k, r)

                @pl.when(own)
                def _():
                    gg[k, r] = t
                    for side, ok, row, to in halo_routes():
                        @pl.when(ok & (r == row))
                        def _(side=side, row=row, to=to):
                            remote(ab.at[d, k, row], hg.at[side, k], o["hg_s"].at[side, k], o["hg_r"].at[side, k], to).start()
                            remote(sc.at[d, k, row], hs.at[side, k], o["hs_s"].at[side, k], o["hs_r"].at[side, k], to).start()

                    i = rem(q, t_rows)

                    @pl.when((k > 0) & (i == 1))
                    def _():
                        prepare(k - 1)

                    @pl.when((k > 0) & (i == t_rows - 1))
                    def _():
                        smoothing(k - 1)

                    @pl.when((k == nb - 1) & (i == t_rows - 1))
                    def _():
                        send_genes(0)

                    if early_pred:
                        @pl.when(q == 3 * nb * t_rows // 4)
                        def _():
                            for i in range(early_pred):
                                send_pred(i)

                @pl.when((rem(k, 2) == d) & (k + 2 - rem(k, 2) < nb))
                def _():
                    predict(d, div(k, 2) + 1, r)

        loop(2, direction)

        @pl.when(owner & (s == half * t_rows))
        def _():
            back_coefs()

    def halo_routes():
        return ((1, up, 0, (sx - 1, sy, cz)), (0, down, t_rows - 1, (sx + 1, sy, cz)))

    def first_block(d):
        @pl.when(cz != (1 - d) * (n - 1))
        def _():
            loop(t_rows, lambda r: predict(d, 0, r))

    loop(2, first_block)
    loop(nb * t_rows + LAG_SUM * lead, sum_step)

    def diff_smooth(k, r, at):
        tc0, tc1, sc0, sc1, m0, m1 = (gc[k, i : i + 1, :] for i in range(6))
        h = hot[r, at, :]
        mk = m0 + h * (m1 - m0)
        by_truth = tc0 + h * (tc1 - tc0) + mk * acc[1, r, at, :]
        by_smooth = sc0 + h * (sc1 - sc0) + mk * acc[2, r, at, :]
        return by_truth * sp[k, r, at, :] + by_smooth * sm[k, r, at, :]

    def send_borders(k):
        for side, ok, row, to in halo_routes():
            @pl.when(ok)
            def _(side=side, row=row, to=to):
                for u in range(0, width, sub):
                    hq[side, k, u : u + sub, :] = diff_smooth(k, row, slice(u, u + sub)).astype(BF16)
                remote(hq.at[side, k], hd.at[side, k], o["hd_s"].at[side, k], o["hd_r"].at[side, k], to).start()

    def diff_inside(k):
        slot = rem(k, 2)

        def rows(r):
            for u in range(0, width, sub):
                pad[slot, r + 1, 8 + u : 8 + u + sub, :] = diff_smooth(k, r, slice(u, u + sub))

        loop(t_rows, rows)
        send_edges(slot, 1, k, range(1, t_rows + 1))

    def diff_border(k):
        slot = rem(k, 2)
        for side, ok, row in sides:
            @pl.when(ok)
            def _(side=side, row=row):
                wait(hd.at[side, k], o["hd_r"].at[side, k])
                pad[slot, row, mid, :] = hd[side, k].astype(F32)

            @pl.when(jnp.logical_not(ok))
            def _(row=row):
                pad[slot, row, mid, :] = jnp.zeros((width, LANES), F32)

        send_edges(slot, 2, k, (0, t_rows + 1))

    back = cz + 1 - 2 * od

    def diff_pred(k, rows):
        slot = rem(k, 2)
        for r in rows:
            for u in range(0, width, sub):
                here_u = slice(u, u + sub)
                a = pad[slot, r + 1, 8 + u : 8 + u + sub, :]
                for j, (dr, dc) in enumerate(OFFSETS):
                    w = cb[j, r, here_u, :].astype(F32)
                    a = a + w * pad[slot, r + 1 - dr, 8 - dc + u : 8 - dc + u + sub, :]
                low = a.astype(BF16)
                dd[od, k, r, here_u, :] = low
                acc[0, r, here_u, :] = acc[0, r, here_u, :] + gg[k, r, here_u, :] * low.astype(F32)
            at = dd.at[od, k, r]
            remote(at, at, o["d_s"].at[od, k, r], o["d_r"].at[od, k, r], (sx, sy, back)).start()

    def back_chunk(q):
        i = rem(q, t_rows)
        return div(q, t_rows), jnp.where(i < t_rows - 2, i + 1, jnp.where(i == t_rows - 2, 0, i))

    def diff_inner(k):
        take_edges(rem(k, 2), 1, k, range(1, t_rows + 1))
        diff_pred(k, range(1, t_rows - 1))
        diff_border(k)

    def diff_outer(k):
        take_edges(rem(k, 2), 2, k, (0, t_rows + 1))
        diff_pred(k, (0, t_rows - 1))

    def spot_rows(i):
        return [
            jnp.sum(acc[i, r, h * LANES : (h + 1) * LANES, :].T, axis=0, keepdims=True)
            for r in range(t_rows)
            for h in range(wl)
        ]

    def put_own(i):
        k = own_block(cz, i)
        return pltpu.make_async_copy(gg.at[k], gp.at[:, :, i * LANES : (i + 1) * LANES], o["gp_m"].at[i])

    @pl.when(owner)
    def _():
        prepare(nb - 1)
        smoothing(nb - 1)

        send_genes(1)
        for i in range(3):
            for at, row in enumerate(spot_rows(i)):
                spx[0, i, at : at + 1, :] = row
        remote(spx.at[0], spx.at[1], o["x_s"].at[0], o["x_r"].at[0], (sx, sy, n - 1 - cz)).start()
        gr[here] = gs[...]
        for i in range(wb):
            put_own(i).start()

        def wait_genes(j):
            t, _ = plane_peer(j)
            for part, at in enumerate(gene_parts):
                wait(gr.at[t, at], o["g_r"].at[part, t])

        loop(nplane - 1, wait_genes)
        count = jnp.maximum(jnp.sum(gmask[...].astype(F32), axis=1, keepdims=True), 1.0)

        def genes(k, gl):
            tot = gr[0, k]
            for t in range(1, nplane):
                tot = tot + gr[t, k]
            ib, ic = lax.rsqrt(tot[2:4] + EPS), lax.rsqrt(tot[4:6] + EPS)
            cos = tot[0:2] * ib * ic
            at = pl.ds(pl.multiple_of(gene_block(od, k) * LANES, LANES), LANES)
            mask = gmask[:, at].astype(F32)
            scale = -mask / (2.0 * count)
            gc[k, 0:2, :] = scale * ib * ic
            gc[k, 2:4, :] = -scale * cos * ib * ib
            gc[k, 4:6, :] = mask
            return gl + mask * cos / count

        gl = lax.fori_loop(0, nb, genes, jnp.zeros((2, LANES), F32))
        gene_part = jnp.sum(jnp.sum(gl, axis=0, keepdims=True), axis=1, keepdims=True)

        wait(spx.at[1], o["x_r"].at[0])
        a, b, c = (spx[0, i] + spx[1, i] for i in range(3))
        ib, ic = lax.rsqrt(b + EPS), lax.rsqrt(c + EPS)
        cos = a * ib * ic
        by_truth = (-1.0 / all_spots) * ib * ic
        by_smooth = (1.0 / all_spots) * cos * ib * ib
        for r in range(t_rows):
            for h in range(wl):
                at, i = slice(h * LANES, (h + 1) * LANES), r * wl + h
                acc[1, r, at, :] = spread(by_truth[i : i + 1])
                acc[2, r, at, :] = spread(by_smooth[i : i + 1])
        acc[0] = jnp.zeros(acc.shape[1:], F32)
        spot_part = jnp.sum(jnp.sum(cos, axis=0, keepdims=True), axis=1, keepdims=True)
        spr[here] = jnp.broadcast_to(spot_part, (8, LANES))
        fm[od, 1] = jnp.broadcast_to(gene_part, (8, LANES))

        def send_spot(j):
            _, to = plane_peer(j)
            remote(spr.at[here], spr.at[here], o["p_s"].at[j], o["p_r"].at[here], to).start()

        send_borders(0)
        diff_inside(0)
        send_borders(1)
        take_edges(0, 1, 0, range(1, t_rows + 1))
        diff_pred(0, range(1, t_rows - 1))
        loop(nb - 2, lambda k: send_borders(k + 2))
        loop(nplane - 1, send_spot)
        diff_border(0)

    def send_last():
        def wait_spot(j):
            t, _ = plane_peer(j)
            wait(spr.at[t], o["p_r"].at[t])

        loop(nplane - 1, wait_spot)
        spot_all = spr[0, 0:1, :]
        for t in range(1, nplane):
            spot_all = spot_all + spr[t, 0:1, :]
        rows = spot_rows(0)
        if len(rows) < 8:
            rows.append(jnp.zeros((8 - len(rows), LANES), F32))
        fm[od, 0] = jnp.concatenate(rows, axis=0)
        fm[od, 1, 1:2, :] = spot_all
        remote(fm.at[od], fm.at[od], o["f_s"].at[od], o["f_r"].at[od], (sx, sy, back)).start()
        for i in range(early_pred, wb):
            send_pred(i)


    sy_bit, sx_bit = div(sx, 2), rem(sx, 2)
    over_y, over_x = (sx + 2 - 4 * sy_bit, sy, cz), (sx + 1 - 2 * sx_bit, sy, cz)

    def place(k):
        jj = div(k, bpg)
        hi = div(jj, 2)
        return rem(jj, 2) == sy, hi * bpg + rem(k, bpg), jnp.where(sy_bit == 0, 1 - hi, hi) == sx_bit

    halves = (pl.ds(0, c_rows // 2), pl.ds(c_rows // 2, c_rows // 2))

    def add_rows(dst, a, b):
        count = dst.shape[0] // 2

        def rows(i):
            at = pl.ds(pl.multiple_of(i * count, 8), count)
            dst[at, :] = (a[at, :].astype(F32) + b[at, :].astype(F32)).astype(dst.dtype)

        loop(2, rows)

    def scatter_0(k):
        mine, at, _ = place(k)

        @pl.when(jnp.logical_not(mine))
        def _():
            for d in range(2):
                remote(pss.at[rem(k, 2), d], rs1.at[d, at], o["r1_s"].at[d, at], o["r1_r"].at[d, at], mate).start()

    def stays(final):
        return sy_bit, jnp.where(final, sy_bit, 1 - sy_bit)

    def scatter_1(k):
        mine, at, final = place(k)

        @pl.when(mine)
        def _():
            def each(d):
                wait(rs1.at[d, at], o["r1_r"].at[d, at])
                add_rows(rs1.at[d, at], pss.at[rem(k, 2), d], rs1.at[d, at])

            loop(2, each)
            for h, (d, to) in enumerate(zip(stays(final), (over_y, over_x), strict=True)):
                src, dst = rs1.at[1 - d, at, halves[h]], rs2.at[at, halves[h]]
                remote(src, dst, o["r2_s"].at[h, at], o["r2_r"].at[h, at], to).start()

        @pl.when(jnp.logical_not(mine))
        def _():
            for d in range(2):
                wait(pss.at[rem(k, 2), d], o["r1_s"].at[d, at])

    def scatter_2(k):
        mine, at, final = place(k)

        @pl.when(mine)
        def _():
            i = rem(k, bpg)
            for h, (d, to) in enumerate(zip(stays(final), (over_x, over_y), strict=True)):
                part = rs2.at[at, halves[h]]
                wait(part, o["r2_r"].at[h, at])
                add_rows(part, rs1.at[d, at, halves[h]], part)

                @pl.when(jnp.logical_not(final))
                def _(h=h, part=part, to=to):
                    remote(part, rs3.at[i, halves[h]], o["r3_s"].at[h, i], o["r3_r"].at[h, i], to).start()

            for h, d in enumerate(stays(final)):
                wait(rs1.at[1 - d, at, halves[h]], o["r2_s"].at[h, at])

    def put_cells(i):
        at = pl.ds(pl.multiple_of(i * LANES, LANES), LANES)
        return pltpu.make_async_copy(dcv.at[i], dcell.at[:, at], o["dc_m"].at[i])

    def scatter_3(k):
        mine, at, final = place(k)
        i = rem(k, bpg)

        @pl.when(mine & final)
        def _():
            for h in range(2):
                wait(rs3.at[i, halves[h]], o["r3_r"].at[h, i])
                add_rows(dcv.at[i, halves[h]], rs2.at[at, halves[h]], rs3.at[i, halves[h]])
            put_cells(i).start()

        @pl.when(mine & jnp.logical_not(final))
        def _():
            for h in range(2):
                wait(rs2.at[at, halves[h]], o["r3_s"].at[h, i])

    def add_map(k, r):
        x = jnp.concatenate([xs[gene_block(0, k)], xs[gene_block(1, k)]], axis=1)
        d = jnp.concatenate([dd[0, k, r], dd[1, k, r]], axis=1)
        new = lax.dot_general(x, d, (((1,), (1,)), ((), ())), preferred_element_type=F32)
        dm[r] = jnp.where(k == 0, 0.0, dm[r]) + new

    def multiply(k, piece):
        d = jnp.concatenate([dd[i, k].reshape(spots, LANES) for i in range(2)], axis=1)
        out = jnp.dot(mm[...], d, preferred_element_type=F32).astype(BF16)
        pss[rem(k, 2), 0] = out[:, :LANES]
        pss[rem(k, 2), 1] = out[:, LANES:]

    def put_logits(r):
        return pltpu.make_async_copy(dm.at[r], dlog.at[:, r, :], o["dl_m"].at[r])

    def finish(r):
        col = jnp.concatenate([fm[0, 0, i : i + 1] + fm[1, 0, i : i + 1] for i in range(r * wl, (r + 1) * wl)], axis=1)

        def rows(i):
            at = pl.ds(pl.multiple_of(i * tile, tile), tile)
            low = mm[at, r * width : (r + 1) * width].astype(F32)
            dm[r, at, :] = low * (dm[r, at, :] - col)

        loop(c_rows // tile, rows)
        put_logits(r).start()

    def put_pred(i):
        return pltpu.make_async_copy(gg.at[i], gp.at[:, :, i * LANES : (i + 1) * LANES], o["gp_m"].at[i])

    def take_pred(i):
        wait(gpr.at[i], o["gp_r"].at[i])
        wait(gps.at[i], o["gq_r"].at[i])

        def rows(r):
            gg[i, r] = gpr[i, r].astype(I32).astype(F32) * gps[i, r]

        loop(t_rows, rows)
        put_pred(i).start()

    behind = BEHIND * t_rows
    lag = jnp.where(owner, behind, LAG_BACK * jnp.maximum(cz - 1, n - 2 - cz))

    def produce(k, piece):
        @pl.when(piece == 0)
        def _():
            diff_outer(k)

        @pl.when((piece == 1) & (k + 1 < nb))
        def _():
            diff_inside(k + 1)

        @pl.when((piece == 2) & (k + 1 < nb))
        def _():
            diff_inner(k + 1)

        @pl.when((piece == 1) & (k + 1 == nb))
        def _():
            send_last()

    def back_step(s):
        @pl.when(owner & (s < nb * t_rows))
        def _():
            produce(div(s, t_rows), rem(s, t_rows))

        def direction(d):
            own, end = cz == d * (n - 1), cz == (1 - d) * (n - 1)
            off = jnp.where(owner, behind, LAG_BACK * jnp.where(d == 0, cz - 1, n - 2 - cz))
            q = s - off
            to = (sx, sy, cz + 1 - 2 * d)

            @pl.when(jnp.logical_not(own) & (q >= 0) & (q < nb * t_rows))
            def _():
                k, r = back_chunk(q)
                at = dd.at[d, k, r]
                wait(at, o["d_r"].at[d, k, r])

                @pl.when(jnp.logical_not(end))
                def _():
                    remote(at, at, o["d_s"].at[d, k, r], o["d_r"].at[d, k, r], to).start()

            @pl.when(jnp.logical_not(own) & (q == nb * t_rows))
            def _():
                wait(fm.at[d], o["f_r"].at[d])

                @pl.when(jnp.logical_not(end))
                def _():
                    remote(fm.at[d], fm.at[d], o["f_s"].at[d], o["f_r"].at[d], to).start()

        loop(2, direction)
        q = s - lag

        @pl.when((q >= 0) & (q < nb * t_rows))
        def _():
            add_map(*back_chunk(q))

        w = q - t_rows
        k, piece = div(w, t_rows), rem(w, t_rows)

        @pl.when((w >= 0) & (k < nb))
        def _():
            @pl.when(piece == 0)
            def _():
                multiply(k, piece)
                scatter_0(k)

        @pl.when((w >= 0) & (k == nb))
        def _():
            for r in range(t_rows):
                @pl.when(piece == r)
                def _(r=r):
                    finish(r)

        for stage, back_by, at in ((scatter_1, 0, 2), (scatter_2, 1, 2), (scatter_3, 2, 2)):
            @pl.when((w >= 0) & (piece == at) & (k >= back_by) & (k < nb + back_by))
            def _(stage=stage, back_by=back_by):
                stage(k - back_by)

    loop(t_rows * (nb + 4) + max(LAG_BACK * lead, behind), back_step)

    losses[0] = jnp.max(fm[0, 1, 0:1, :] + fm[1, 1, 0:1, :]) * -0.5
    losses[1] = jnp.max(fm[0, 1, 1:2, :]) * (-1.0 / all_spots)

    @pl.when(jnp.logical_not(owner))
    def _():
        for i in range(wb):
            take_pred(i)

    for r in range(t_rows):
        put_logits(r).wait()
    for i in range(bpg):
        put_cells(i).wait()
    loop(n - 1, lambda j: wait(srow.at[cz], o["s_s"].at[j]))

    def sent(d):
        own, end = cz == d * (n - 1), cz == (1 - d) * (n - 1)

        @pl.when(jnp.logical_not(own))
        def _():
            def each(q):
                k, r = div(q, t_rows), rem(q, t_rows)
                wait(ab.at[d, k, r], o["a_s"].at[d, k, r])
                wait(sc.at[d, k, r], o["c_s"].at[d, k, r])

            loop(nb * t_rows, each)

        @pl.when(jnp.logical_not(end))
        def _():
            def each(q):
                k, r = div(q, t_rows), rem(q, t_rows)
                wait(dd.at[d, k, r], o["d_s"].at[d, k, r])

            loop(nb * t_rows, each)
            wait(fm.at[d], o["f_s"].at[d])

    loop(2, sent)

    @pl.when(jnp.logical_not(owner))
    def _():
        for i in range(wb):
            put_pred(i).wait()

    @pl.when(owner)
    def _():
        for i in range(wb):
            put_own(i).wait()

            def each(j, i=i):
                for copy in pred_copies(i, j):
                    copy.wait_send()

            loop(n // 2 - 1, each)
        for slot, ok, _ in coef_routes():
            @pl.when(ok)
            def _(slot=slot):
                wait(con, o["co_s"].at[slot])

        def each(k):
            for side, ok, row, _ in halo_routes():
                @pl.when(ok)
                def _(side=side, row=row):
                    wait(ab.at[od, k, row], o["hg_s"].at[side, k])
                    wait(sc.at[od, k, row], o["hs_s"].at[side, k])
                    wait(hq.at[side, k], o["hd_s"].at[side, k])

            for which in range(3):
                wait(es.at[which, k], o["e_s"].at[which, k])

        loop(nb, each)
        wait(spx.at[0], o["x_s"].at[0])

        def each_peer(j):
            for part, at in enumerate(gene_parts):
                wait(gs.at[at], o["g_s"].at[part, j])
            wait(spr.at[here], o["p_s"].at[j])

        loop(nplane - 1, each_peer)


def per_device(logits, cells_expr, spatial, gene_mask, slide_id, edge_weight, edge_mask):
    c_rows, t_rows, width = logits.shape
    genes = cells_expr.shape[1]
    n, nsx, nsy = (lax.axis_size(a) for a in ("cells", "sx", "sy"))
    spots = t_rows * width
    share = genes // n
    wide = max(share, LANES)
    wb = wide // LANES
    nb = genes // 2 // LANES
    nplane = nsx * nsy
    grid = (t_rows, width, LANES)
    vm, dma = pltpu.VMEM, pltpu.SemaphoreType.DMA
    fits = width == 2 * LANES and c_rows >= 4 * width
    scratch = dict(
        xs=vm((2 * nb, c_rows, LANES), BF16),
        mm=vm((c_rows, spots), BF16),
        mt=vm((t_rows, width, c_rows), BF16),
        dm=vm((t_rows, c_rows, width), F32),
        srow=vm((n, spots // LANES, LANES), F32),
        ab=vm((2, nb, *grid), I16),
        sc=vm((2, nb, t_rows, 1, LANES), F32),
        tt=vm((1, 8, LANES) if fits else (t_rows, 4 * width, 2 * LANES), F32),
        gg=vm((nb, *grid), F32),
        sm=vm((nb, *grid), F32),
        sp=vm((nb, *grid), F32),
        pad=vm((2, t_rows + 2, width + 16, LANES), F32),
        hg=vm((2, nb, width, LANES), I16),
        hs=vm((2, nb, 1, LANES), F32),
        hd=vm((2, nb, width, LANES), BF16),
        hq=vm((2, nb, width, LANES), BF16),
        es=vm((3, nb, 8, LANES), F32),
        er=vm((3, nb, 8, LANES), F32),
        cf=vm((6, *grid), F32),
        cb=vm((6, *grid), BF16),
        hot=vm(grid, F32),
        con=vm((t_rows, 8, width), F32),
        cor=vm((5, t_rows, 8, width), F32),
        acc=vm((3, *grid), F32),
        gs=vm((nb, 8, LANES), F32),
        gr=vm((nplane, nb, 8, LANES), F32),
        spx=vm((2, 3, spots // LANES, LANES), F32),
        gc=vm((nb, 8, LANES), F32),
        spr=vm((nplane, 8, LANES), F32),
        dd=vm((2, nb, *grid), BF16),
        fm=vm((2, 2, 8, LANES), F32),
        pss=vm((2, 2, c_rows, LANES), BF16),
        rs1=vm((2, nb // 2, c_rows, LANES), BF16),
        rs2=vm((nb // 2, c_rows, LANES), BF16),
        rs3=vm((nb // 4, c_rows, LANES), BF16),
        dcv=vm((nb // 4, c_rows, LANES), F32),
        gpr=vm((wb, *grid), I16),
        gps=vm((wb, t_rows, 1, LANES), F32),
        lg_m=dma((t_rows,)),
        xs_m=dma((2 * nb,)),
        sp_m=dma((nb,)),
        s_s=dma((n,)),
        s_r=dma((n,)),
        a_s=dma((2, nb, t_rows)),
        a_r=dma((2, nb, t_rows)),
        c_s=dma((2, nb, t_rows)),
        c_r=dma((2, nb, t_rows)),
        hg_s=dma((2, nb)),
        hg_r=dma((2, nb)),
        hs_s=dma((2, nb)),
        hs_r=dma((2, nb)),
        hd_s=dma((2, nb)),
        hd_r=dma((2, nb)),
        e_s=dma((3, nb)),
        e_r=dma((3, nb)),
        co_s=dma((5,)),
        co_r=dma((5,)),
        g_s=dma((2, nplane)),
        g_r=dma((2, nplane)),
        p_s=dma((nplane,)),
        p_r=dma((nplane,)),
        x_s=dma((1,)),
        x_r=dma((1,)),
        d_s=dma((2, nb, t_rows)),
        d_r=dma((2, nb, t_rows)),
        f_s=dma((2,)),
        f_r=dma((2,)),
        r1_s=dma((2, nb // 2)),
        r1_r=dma((2, nb // 2)),
        r2_s=dma((2, nb // 2)),
        r2_r=dma((2, nb // 2)),
        r3_s=dma((2, nb // 4)),
        r3_r=dma((2, nb // 4)),
        gp_s=dma((max(n // 2 - 1, 1), wb)),
        gp_r=dma((wb,)),
        gq_s=dma((max(n // 2 - 1, 1), wb)),
        gq_r=dma((wb,)),
        gp_m=dma((wb,)),
        dl_m=dma((t_rows,)),
        dc_m=dma((nb // 4,)),
    )
    names = ("lg", "cells", "spat", "gmask", "slide", "ew", "em", "losses", "gp", "dlog", "dcell")
    names += tuple(scratch)
    sizes = (n, nsx, nsy, share, spots * nplane)
    anywhere, local = pl.BlockSpec(memory_space=pl.ANY), pl.BlockSpec(memory_space=pltpu.VMEM)
    losses, pred, d_logits, d_cells = pl.pallas_call(
        functools.partial(kernel, names, sizes),
        out_shape=(
            jax.ShapeDtypeStruct((2,), F32),
            jax.ShapeDtypeStruct((t_rows, width, wide), F32),
            jax.ShapeDtypeStruct(logits.shape, F32),
            jax.ShapeDtypeStruct((c_rows, genes // nplane), F32),
        ),
        in_specs=[anywhere] * 3 + [local] * 4,
        out_specs=(pl.BlockSpec(memory_space=pltpu.SMEM), anywhere, anywhere, anywhere),
        scratch_shapes=list(scratch.values()),
        compiler_params=pltpu.CompilerParams(
            collective_id=0, has_side_effects=True, vmem_limit_bytes=VMEM
        ),
        cost_estimate=pl.CostEstimate(
            flops=6 * c_rows * spots * genes, bytes_accessed=32 << 20, transcendentals=c_rows * spots
        ),
    )(logits, cells_expr, spatial, gene_mask, slide_id, edge_weight, edge_mask)
    if wide > share:
        pred = lax.dynamic_slice_in_dim(pred, rem(lax.axis_index("cells") * share, wide), share, 2)
    return (losses, pred, d_logits, d_cells)


BEHIND = 3
LAG_SUM = 3
LAG_BACK = 3
VMEM = 64 * 1024 * 1024 - 512 * 1024


def solution(mesh):
    return jax.shard_map(
        per_device,
        mesh=mesh,
        in_specs=(
            P("cells", "sx", "sy"),
            P("cells", None),
            P("sx", "sy", None),
            P(),
            P("sx", "sy"),
            P(None, "sx", "sy"),
            P(None, "sx", "sy"),
        ),
        out_specs=(P(), P("sx", "sy", "cells"), P("cells", "sx", "sy"), P("cells", ("sx", "sy"))),
        check_vma=False,
    )
```

```python
import functools

import jax
import jax.numpy as jnp
from jax import lax
from jax.experimental import pallas as pl
from jax.experimental.pallas import tpu as pltpu
from jax.sharding import PartitionSpec as P

EPS = 1e-06
OFFSETS = ((0, 1), (0, -1), (1, 0), (-1, 0), (-1, 1), (1, -1))
LANES = 128
TOP = 32767.0
MESH = pl.DeviceIdType.MESH
F32, BF16, I16, I32 = jnp.float32, jnp.bfloat16, jnp.int16, jnp.int32
rem, div = lax.rem, lax.div


def loop(count, body):
    lax.fori_loop(0, count, lambda i, _: (body(i), 0)[1], 0)


def remote(src, dst, sent, got, to):
    return pltpu.make_async_remote_copy(
        src_ref=src, dst_ref=dst, send_sem=sent, recv_sem=got, device_id=to, device_id_type=MESH
    )


def wait(ref, sem):
    pltpu.make_async_copy(ref, ref, sem).wait()


def spread(row):
    parts = [
        jnp.broadcast_to(row[:, at : at + LANES], (LANES, LANES)).T
        for at in range(0, row.shape[1], LANES)
    ]
    return jnp.concatenate(parts, axis=0)


def fold(x):
    return jnp.sum(x.reshape(x.shape[0] // 8, 8, x.shape[1]), axis=0)


def kernel(names, sizes, *refs):
    n, nsx, nsy, share, all_spots = sizes
    o = dict(zip(names, refs, strict=True))
    lg, cells, spat, gmask, slide, ew, em = (o[k] for k in names[:7])
    losses, gp, dlog, dcell = (o[k] for k in names[7:11])
    xs, mm, mt, dm, srow, ab, sc, tt = (o[k] for k in names[11:19])
    gg, sm, sp, pad, hg, hs, hd, hq = (o[k] for k in names[19:27])
    es, er, cf, cb, hot, con, cor, acc = (o[k] for k in names[27:35])
    gs, gr, spx, gc, spr, dd, fm = (o[k] for k in names[35:42])
    pss, rs1, rs2, rs3, dcv, gpr, gps, gpb = (o[k] for k in names[42:50])

    c_rows, t_rows, width = lg.shape
    spots = t_rows * width
    nb = cells.shape[1] // 2 // LANES
    wl = width // LANES
    wb = gpr.shape[0]
    nplane = nsx * nsy
    half = nb // 2
    bpg = nb // 4
    tile = LANES
    tiles = c_rows // tile
    quarter = c_rows // t_rows
    sub = min(64, width)
    mid = slice(8, 8 + width)

    sx, sy, cz = (lax.axis_index(a) for a in ("sx", "sy", "cells"))
    here = sx * nsy + sy
    owner = (cz == 0) | (cz == n - 1)
    od = jnp.where(cz == 0, 0, 1)
    up, down = sx > 0, sx < nsx - 1
    mate = (sx, 1 - sy, cz)

    def gene_block(d, k):
        return jnp.where(d == 0, rem(k + half, nb), nb + k)

    for r in range(t_rows):
        pltpu.make_async_copy(lg.at[:, r, :], dm.at[r], o["lg_m"].at[r]).start()

    def load_cells(b):
        at = pl.ds(pl.multiple_of(b * LANES, LANES), LANES)
        return pltpu.make_async_copy(cells.at[:, at], xs.at[b], o["xs_m"].at[b])

    loop(2 * nb, lambda b: load_cells(b).start())

    def load_truth(k):
        at = pl.ds(pl.multiple_of(gene_block(od, k) * LANES, LANES), LANES)
        return pltpu.make_async_copy(spat.at[:, :, at], sp.at[k], o["sp_m"].at[k])

    @pl.when(owner)
    def _():
        loop(nb, lambda k: load_truth(k).start())

    barrier = pltpu.get_barrier_semaphore()

    def greet_line(j):
        to = (sx, sy, rem(cz + j + 1, n))
        pl.semaphore_signal(barrier, inc=1, device_id=to, device_id_type=MESH)

    def greet_plane(j):
        t = rem(here + j + 1, nplane)
        to = (div(t, nsy), rem(t, nsy), cz)
        pl.semaphore_signal(barrier, inc=1, device_id=to, device_id_type=MESH)

    loop(n - 1, greet_line)
    loop(nplane - 1, greet_plane)

    for r in range(t_rows):
        pltpu.make_async_copy(lg.at[:, r, :], dm.at[r], o["lg_m"].at[r]).wait()

        def exps(i, s, r=r):
            at = pl.ds(i * tile, tile)
            x = jnp.exp(dm[r, at, :])
            dm[r, at, :] = x
            return s + fold(x)

        s = lax.fori_loop(0, c_rows // tile, exps, jnp.zeros((8, width), F32))
        s = jnp.sum(s, axis=0, keepdims=True)
        for h in range(wl):
            srow[cz, pl.ds(r * wl + h, 1), :] = s[:, h * LANES : (h + 1) * LANES]

    pl.semaphore_wait(barrier, n - 1 + nplane - 1)

    def send_sums(j):
        to = (sx, sy, rem(cz + j + 1, n))
        remote(srow.at[cz], srow.at[cz], o["s_s"].at[j], o["s_r"].at[cz], to).start()

    loop(n - 1, send_sums)

    def turn(dst, first):
        def each(i):
            for r in range(t_rows):
                at = pl.ds(pl.multiple_of((i + first) * LANES, LANES), LANES)
                dst[i, r] = dm[r, at, :].T

        return each

    turned = ((gg, 0, min(tiles, nb)), (sm, nb, max(tiles - nb, 0)))
    for dst, first, count in turned:
        loop(count, turn(dst, first))

    def wait_sums(j):
        z = rem(cz + j + 1, n)
        wait(srow.at[z], o["s_r"].at[z])

    loop(n - 1, wait_sums)
    total = srow[0]
    for z in range(1, n):
        total = total + srow[z]
    inv = 1.0 / total
    inv_rows = [
        jnp.concatenate([inv[r * wl + h : r * wl + h + 1] for h in range(wl)], axis=1)
        for r in range(t_rows)
    ]
    for r in range(t_rows):
        acc[0, r] = spread(inv_rows[r])

    for dst, first, count in turned:
        def scale(i, dst=dst, first=first):
            at = pl.ds(pl.multiple_of((i + first) * LANES, LANES), LANES)
            for r in range(t_rows):
                mt[r, :, at] = (dst[i, r] * acc[0, r]).astype(BF16)

        loop(count, scale)

    def keep_mapping():
        for r in range(t_rows):
            def each(i, r=r):
                at = pl.ds(pl.multiple_of(i * LANES, LANES), LANES)
                mm[at, r * width : (r + 1) * width] = (dm[r, at, :] * inv_rows[r]).astype(BF16)

            loop(tiles, each)

    loop(2 * nb, lambda b: load_cells(b).wait())

    def coef_routes():
        return (
            (0, down, (sx + 1, sy, cz)),
            (1, up, (sx - 1, sy, cz)),
            (2, sx >= 0, mate),
            (3, down, (sx + 1, 1 - sy, cz)),
            (4, up, (sx - 1, 1 - sy, cz)),
        )


    def predict(d, pair, r):
        g = gene_block(d, 2 * pair)
        w = jnp.concatenate([xs[g], xs[g + 1]], axis=1)
        at = pl.ds(pl.multiple_of((2 * d + rem(pair, 2)) * width, 8), width)
        tt[r, at, :] = jnp.dot(mt[r], w, preferred_element_type=F32)

    def predicted(d, k, r):
        at = pl.ds(pl.multiple_of((2 * d + rem(div(k, 2), 2)) * width, 8), width)
        return tt[r, at, pl.ds(pl.multiple_of(rem(k, 2) * LANES, LANES), LANES)]

    def put(d, k, r, t):
        top = jnp.maximum(jnp.max(jnp.abs(t), axis=0, keepdims=True), 1e-30)
        ab[d, k, r] = jnp.round(t * (TOP / top)).astype(I32).astype(I16)
        sc[d, k, r] = top * (1.0 / TOP)

    def pass_on(d, k, r):
        to = (sx, sy, cz + 2 * d - 1)
        remote(ab.at[d, k, r], ab.at[d, k, r], o["a_s"].at[d, k, r], o["a_r"].at[d, k, r], to).start()
        remote(sc.at[d, k, r], sc.at[d, k, r], o["c_s"].at[d, k, r], o["c_r"].at[d, k, r], to).start()

    def chunk_of(q):
        return div(q, t_rows), rem(rem(q, t_rows) * (t_rows - 1), t_rows)

    @pl.when(owner)
    def _():
        d = 1 - od

        def first(q):
            k, r = chunk_of(q)

            @pl.when(rem(k, 2) == 0)
            def _():
                predict(d, div(k, 2), r)

            put(d, k, r, predicted(d, k, r))
            pass_on(d, k, r)

        loop(nb * t_rows, first)

        for r in range(t_rows):
            rows = [ew[j, r : r + 1, :] * em[j, r : r + 1, :].astype(F32) for j in range(6)]
            con[r] = jnp.concatenate(rows + [jnp.zeros((2, width), F32)], axis=0)
            for j in range(6):
                cf[j, r] = spread(rows[j])
            hot[r] = spread(slide[r : r + 1, :].astype(F32))
        acc[...] = jnp.zeros(acc.shape, F32)

        for slot, ok, to in coef_routes():
            @pl.when(ok)
            def _(slot=slot, to=to):
                remote(con, cor.at[slot], o["co_s"].at[slot], o["co_r"].at[slot], to).start()

        loop(nb, lambda k: load_truth(k).wait())

    def back_coefs():
        for slot, ok in ((0, up), (1, down), (2, sx >= 0), (3, up), (4, down)):
            @pl.when(ok)
            def _(slot=slot):
                wait(cor.at[slot], o["co_r"].at[slot])

        lane = lax.broadcasted_iota(I32, (8, width), 1)
        for j, (dr, dc) in enumerate(OFFSETS):
            for r in range(t_rows):
                at = r - dr
                if at < 0:
                    base, side, ok = cor[0, t_rows - 1], cor[3, t_rows - 1], up
                elif at >= t_rows:
                    base, side, ok = cor[1, 0], cor[4, 0], down
                else:
                    base, side, ok = con[at], cor[2, at], sx >= 0
                base = jnp.where(ok, base, 0.0)
                if dc:
                    by, edge = (1, 0) if dc == 1 else (width - 1, width - 1)
                    side = jnp.where(ok & (sy == (1 if dc == 1 else 0)), side, 0.0)
                    base = jnp.where(lane == edge, pltpu.roll(side, by, 1), pltpu.roll(base, by, 1))
                cb[j, r] = spread(base[j : j + 1]).astype(BF16)

    def send_edges(slot, which, k, rows):
        parts = [
            jnp.where(sy == 1, pad[slot, row, 8:9, :], pad[slot, row, 7 + width : 8 + width, :])
            for row in rows
        ]
        parts.append(jnp.zeros((8 - len(parts), LANES), F32))
        es[which, k] = jnp.concatenate(parts, axis=0)
        remote(es.at[which, k], er.at[which, k], o["e_s"].at[which, k], o["e_r"].at[which, k], mate).start()

    def take_edges(slot, which, k, rows):
        wait(er.at[which, k], o["e_r"].at[which, k])
        for i, row in enumerate(rows):
            edge = er[which, k, i : i + 1, :]
            pad[slot, row, 8 + width : 9 + width, :] = jnp.where(sy == 0, edge, 0.0)
            pad[slot, row, 7:8, :] = jnp.where(sy == 1, edge, 0.0)

    sides = ((0, up, 0), (1, down, t_rows + 1))

    def prepare(k):
        for side, ok, row in sides:
            @pl.when(ok)
            def _(side=side, row=row):
                wait(hg.at[side, k], o["hg_r"].at[side, k])
                wait(hs.at[side, k], o["hs_r"].at[side, k])
                pad[0, row, mid, :] = hg[side, k].astype(I32).astype(F32) * hs[side, k]

            @pl.when(jnp.logical_not(ok))
            def _(row=row):
                pad[0, row, mid, :] = jnp.zeros((width, LANES), F32)

        def rows(r):
            pad[0, r + 1, mid, :] = gg[k, r]

        loop(t_rows, rows)
        send_edges(0, 0, k, range(t_rows + 2))

    def smoothing(k):
        take_edges(0, 0, k, range(t_rows + 2))
        at = pl.ds(pl.multiple_of(gene_block(od, k) * LANES, LANES), LANES)
        mask = gmask[:, at].astype(F32)
        m0, m1 = mask[0:1], mask[1:2]

        def rows(r, sums):
            sums = list(sums)
            for u in range(0, width, sub):
                here_u = slice(u, u + sub)
                a = pad[0, r + 1, 8 + u : 8 + u + sub, :]
                for j, (dr, dc) in enumerate(OFFSETS):
                    a = a + cf[j, r, here_u, :] * pad[0, r + 1 + dr, 8 + dc + u : 8 + dc + u + sub, :]
                sm[k, r, here_u, :] = a
                t = sp[k, r, here_u, :]
                h = hot[r, here_u, :]
                mk = m0 + h * (m1 - m0)
                for i, x in enumerate((a * t, a * a, t * t)):
                    sums[2 * i] = sums[2 * i] + fold(x)
                    sums[2 * i + 1] = sums[2 * i + 1] + fold(x * h)
                    acc[i, r, here_u, :] = acc[i, r, here_u, :] + x * mk
            return tuple(sums)

        sums = lax.fori_loop(0, t_rows, rows, (jnp.zeros((8, LANES), F32),) * 6)
        parts = []
        for i in range(3):
            both = jnp.sum(sums[2 * i], axis=0, keepdims=True)
            one = jnp.sum(sums[2 * i + 1], axis=0, keepdims=True)
            parts += [both - one, one]
        gs[k] = jnp.concatenate(parts + [jnp.zeros((2, LANES), F32)], axis=0)

    def own_block(t, i):
        b = div(t * share, LANES) + i - od * nb
        return jnp.where(od == 0, rem(b + half, nb), b)

    def pred_copies(i, j):
        t = jnp.where(od == 0, j + 1, n - 2 - j)
        k = own_block(t, i)
        to = (sx, sy, t)
        return (
            remote(ab.at[od, k], gpr.at[i], o["gp_s"].at[j, i], o["gp_r"].at[i], to),
            remote(sc.at[od, k], gps.at[i], o["gq_s"].at[j, i], o["gq_r"].at[i], to),
        )

    def send_pred(i):
        def each(j):
            for copy in pred_copies(i, j):
                copy.start()

        loop(n // 2 - 1, each)

    early_pred = 1 if n == 4 else 0

    def plane_peer(j):
        t = rem(here + j + 1, nplane)
        return t, (div(t, nsy), rem(t, nsy), cz)

    gene_parts = (pl.ds(0, nb - 1), pl.ds(nb - 1, 1))

    def send_genes(part):
        at = gene_parts[part]

        def each(j):
            _, to = plane_peer(j)
            sems = o["g_s"].at[part, j], o["g_r"].at[part, here]
            remote(gs.at[at], gr.at[here, at], *sems, to).start()

        loop(nplane - 1, each)

    lead = max(n - 3, 0)

    def sum_step(s):
        def direction(d):
            own, first = cz == d * (n - 1), cz == (1 - d) * (n - 1)
            off = jnp.where(owner, 0, LAG_SUM * jnp.where(d == 1, cz - 1, n - 2 - cz))
            q = s - off

            @pl.when(jnp.logical_not(first) & (q >= 0) & (q < nb * t_rows))
            def _():
                k, r = chunk_of(q)
                wait(ab.at[d, k, r], o["a_r"].at[d, k, r])
                wait(sc.at[d, k, r], o["c_r"].at[d, k, r])
                got = ab[d, k, r].astype(I32).astype(F32) * sc[d, k, r]
                t = predicted(d, k, r) + got
                put(d, k, r, t)

                @pl.when(jnp.logical_not(own))
                def _():
                    pass_on(d, k, r)

                @pl.when(own)
                def _():
                    gg[k, r] = t
                    for side, ok, row, to in halo_routes():
                        @pl.when(ok & (r == row))
                        def _(side=side, row=row, to=to):
                            remote(ab.at[d, k, row], hg.at[side, k], o["hg_s"].at[side, k], o["hg_r"].at[side, k], to).start()
                            remote(sc.at[d, k, row], hs.at[side, k], o["hs_s"].at[side, k], o["hs_r"].at[side, k], to).start()

                    i = rem(q, t_rows)

                    @pl.when((k > 0) & (i == 1))
                    def _():
                        prepare(k - 1)

                    @pl.when((k > 0) & (i == t_rows - 1))
                    def _():
                        smoothing(k - 1)

                    @pl.when((k == nb - 1) & (i == t_rows - 1))
                    def _():
                        send_genes(0)

                    if early_pred:
                        @pl.when(q == 3 * nb * t_rows // 4)
                        def _():
                            for i in range(early_pred):
                                send_pred(i)

                @pl.when((rem(k, 2) == d) & (k + 2 - rem(k, 2) < nb))
                def _():
                    predict(d, div(k, 2) + 1, r)

        loop(2, direction)

        @pl.when(owner & (s == half * t_rows))
        def _():
            back_coefs()

    def halo_routes():
        return ((1, up, 0, (sx - 1, sy, cz)), (0, down, t_rows - 1, (sx + 1, sy, cz)))

    def first_block(d):
        @pl.when(cz != (1 - d) * (n - 1))
        def _():
            loop(t_rows, lambda r: predict(d, 0, r))

    loop(2, first_block)
    keep_mapping()
    loop(nb * t_rows + LAG_SUM * lead, sum_step)

    def diff_smooth(k, r, at):
        tc0, tc1, sc0, sc1, m0, m1 = (gc[k, i : i + 1, :] for i in range(6))
        h = hot[r, at, :]
        mk = m0 + h * (m1 - m0)
        by_truth = tc0 + h * (tc1 - tc0) + mk * acc[1, r, at, :]
        by_smooth = sc0 + h * (sc1 - sc0) + mk * acc[2, r, at, :]
        return by_truth * sp[k, r, at, :] + by_smooth * sm[k, r, at, :]

    def send_borders(k):
        for side, ok, row, to in halo_routes():
            @pl.when(ok)
            def _(side=side, row=row, to=to):
                for u in range(0, width, sub):
                    hq[side, k, u : u + sub, :] = diff_smooth(k, row, slice(u, u + sub)).astype(BF16)
                remote(hq.at[side, k], hd.at[side, k], o["hd_s"].at[side, k], o["hd_r"].at[side, k], to).start()

    def diff_inside(k):
        slot = rem(k, 2)

        def rows(r):
            for u in range(0, width, sub):
                pad[slot, r + 1, 8 + u : 8 + u + sub, :] = diff_smooth(k, r, slice(u, u + sub))

        loop(t_rows, rows)
        send_edges(slot, 1, k, range(1, t_rows + 1))

    def diff_border(k):
        slot = rem(k, 2)
        for side, ok, row in sides:
            @pl.when(ok)
            def _(side=side, row=row):
                wait(hd.at[side, k], o["hd_r"].at[side, k])
                pad[slot, row, mid, :] = hd[side, k].astype(F32)

            @pl.when(jnp.logical_not(ok))
            def _(row=row):
                pad[slot, row, mid, :] = jnp.zeros((width, LANES), F32)

        send_edges(slot, 2, k, (0, t_rows + 1))

    back = cz + 1 - 2 * od

    def diff_pred(k, rows):
        slot = rem(k, 2)
        for r in rows:
            for u in range(0, width, sub):
                here_u = slice(u, u + sub)
                a = pad[slot, r + 1, 8 + u : 8 + u + sub, :]
                for j, (dr, dc) in enumerate(OFFSETS):
                    w = cb[j, r, here_u, :].astype(F32)
                    a = a + w * pad[slot, r + 1 - dr, 8 - dc + u : 8 - dc + u + sub, :]
                low = a.astype(BF16)
                dd[od, k, r, here_u, :] = low
                acc[0, r, here_u, :] = acc[0, r, here_u, :] + gg[k, r, here_u, :] * low.astype(F32)
            at = dd.at[od, k, r]
            remote(at, at, o["d_s"].at[od, k, r], o["d_r"].at[od, k, r], (sx, sy, back)).start()

    def back_chunk(q):
        i = rem(q, t_rows)
        return div(q, t_rows), jnp.where(i < t_rows - 2, i + 1, jnp.where(i == t_rows - 2, 0, i))

    def diff_inner(k):
        take_edges(rem(k, 2), 1, k, range(1, t_rows + 1))
        diff_pred(k, range(1, t_rows - 1))
        diff_border(k)

    def diff_outer(k):
        take_edges(rem(k, 2), 2, k, (0, t_rows + 1))
        diff_pred(k, (0, t_rows - 1))

    def spot_rows(i):
        return [
            jnp.sum(acc[i, r, h * LANES : (h + 1) * LANES, :].T, axis=0, keepdims=True)
            for r in range(t_rows)
            for h in range(wl)
        ]

    def put_pred(i):
        at = slice(i * LANES, (i + 1) * LANES)
        return pltpu.make_async_copy(gpb.at[i], gp.at[:, :, at], o["gp_m"].at[i])

    def put_own(i):
        k = own_block(cz, i)

        def rows(r):
            gpb[i, r] = gg[k, r].astype(BF16)

        loop(t_rows, rows)
        put_pred(i).start()

    @pl.when(owner)
    def _():
        prepare(nb - 1)
        smoothing(nb - 1)

        send_genes(1)
        for i in range(3):
            for at, row in enumerate(spot_rows(i)):
                spx[0, i, at : at + 1, :] = row
        remote(spx.at[0], spx.at[1], o["x_s"].at[0], o["x_r"].at[0], (sx, sy, n - 1 - cz)).start()
        gr[here] = gs[...]
        def wait_genes(j):
            t, _ = plane_peer(j)
            for part, at in enumerate(gene_parts):
                wait(gr.at[t, at], o["g_r"].at[part, t])

        loop(nplane - 1, wait_genes)
        count = jnp.maximum(jnp.sum(gmask[...].astype(F32), axis=1, keepdims=True), 1.0)

        def genes(k, gl):
            tot = gr[0, k]
            for t in range(1, nplane):
                tot = tot + gr[t, k]
            ib, ic = lax.rsqrt(tot[2:4] + EPS), lax.rsqrt(tot[4:6] + EPS)
            cos = tot[0:2] * ib * ic
            at = pl.ds(pl.multiple_of(gene_block(od, k) * LANES, LANES), LANES)
            mask = gmask[:, at].astype(F32)
            scale = -mask / (2.0 * count)
            gc[k, 0:2, :] = scale * ib * ic
            gc[k, 2:4, :] = -scale * cos * ib * ib
            gc[k, 4:6, :] = mask
            return gl + mask * cos / count

        gl = lax.fori_loop(0, nb, genes, jnp.zeros((2, LANES), F32))
        gene_part = jnp.sum(jnp.sum(gl, axis=0, keepdims=True), axis=1, keepdims=True)

        wait(spx.at[1], o["x_r"].at[0])
        a, b, c = (spx[0, i] + spx[1, i] for i in range(3))
        ib, ic = lax.rsqrt(b + EPS), lax.rsqrt(c + EPS)
        cos = a * ib * ic
        by_truth = (-1.0 / all_spots) * ib * ic
        by_smooth = (1.0 / all_spots) * cos * ib * ib
        for r in range(t_rows):
            for h in range(wl):
                at, i = slice(h * LANES, (h + 1) * LANES), r * wl + h
                acc[1, r, at, :] = spread(by_truth[i : i + 1])
                acc[2, r, at, :] = spread(by_smooth[i : i + 1])
        acc[0] = jnp.zeros(acc.shape[1:], F32)
        spot_part = jnp.sum(jnp.sum(cos, axis=0, keepdims=True), axis=1, keepdims=True)
        spr[here] = jnp.broadcast_to(spot_part, (8, LANES))
        fm[od, 1] = jnp.broadcast_to(gene_part, (8, LANES))

        def send_spot(j):
            _, to = plane_peer(j)
            remote(spr.at[here], spr.at[here], o["p_s"].at[j], o["p_r"].at[here], to).start()

        send_borders(0)
        diff_inside(0)
        send_borders(1)
        take_edges(0, 1, 0, range(1, t_rows + 1))
        diff_pred(0, range(1, t_rows - 1))
        loop(nb - 2, lambda k: send_borders(k + 2))
        loop(nplane - 1, send_spot)
        diff_border(0)

    def send_last():
        def wait_spot(j):
            t, _ = plane_peer(j)
            wait(spr.at[t], o["p_r"].at[t])

        loop(nplane - 1, wait_spot)
        spot_all = spr[0, 0:1, :]
        for t in range(1, nplane):
            spot_all = spot_all + spr[t, 0:1, :]
        rows = spot_rows(0)
        if len(rows) < 8:
            rows.append(jnp.zeros((8 - len(rows), LANES), F32))
        fm[od, 0] = jnp.concatenate(rows, axis=0)
        fm[od, 1, 1:2, :] = spot_all
        remote(fm.at[od], fm.at[od], o["f_s"].at[od], o["f_r"].at[od], (sx, sy, back)).start()
        for i in range(early_pred, wb):
            send_pred(i)


    sy_bit, sx_bit = div(sx, 2), rem(sx, 2)
    over_y, over_x = (sx + 2 - 4 * sy_bit, sy, cz), (sx + 1 - 2 * sx_bit, sy, cz)

    def place(k):
        jj = div(k, bpg)
        hi = div(jj, 2)
        return rem(jj, 2) == sy, hi * bpg + rem(k, bpg), jnp.where(sy_bit == 0, 1 - hi, hi) == sx_bit

    halves = (pl.ds(0, c_rows // 2), pl.ds(c_rows // 2, c_rows // 2))

    def add_rows(dst, a, b):
        count = dst.shape[0] // 2

        def rows(i):
            at = pl.ds(pl.multiple_of(i * count, 8), count)
            dst[at, :] = (a[at, :].astype(F32) + b[at, :].astype(F32)).astype(dst.dtype)

        loop(2, rows)

    def scatter_0(k):
        mine, at, _ = place(k)

        @pl.when(jnp.logical_not(mine))
        def _():
            for d in range(2):
                remote(pss.at[rem(k, 2), d], rs1.at[d, at], o["r1_s"].at[d, at], o["r1_r"].at[d, at], mate).start()

    def stays(final):
        return sy_bit, jnp.where(final, sy_bit, 1 - sy_bit)

    def scatter_1(k):
        mine, at, final = place(k)

        @pl.when(mine)
        def _():
            def each(d):
                wait(rs1.at[d, at], o["r1_r"].at[d, at])
                add_rows(rs1.at[d, at], pss.at[rem(k, 2), d], rs1.at[d, at])

            loop(2, each)
            for h, (d, to) in enumerate(zip(stays(final), (over_y, over_x), strict=True)):
                src, dst = rs1.at[1 - d, at, halves[h]], rs2.at[at, halves[h]]
                remote(src, dst, o["r2_s"].at[h, at], o["r2_r"].at[h, at], to).start()

        @pl.when(jnp.logical_not(mine))
        def _():
            for d in range(2):
                wait(pss.at[rem(k, 2), d], o["r1_s"].at[d, at])

    def scatter_2(k):
        mine, at, final = place(k)

        @pl.when(mine)
        def _():
            i = rem(k, bpg)
            for h, (d, to) in enumerate(zip(stays(final), (over_x, over_y), strict=True)):
                part = rs2.at[at, halves[h]]
                wait(part, o["r2_r"].at[h, at])
                add_rows(part, rs1.at[d, at, halves[h]], part)

                @pl.when(jnp.logical_not(final))
                def _(h=h, part=part, to=to):
                    remote(part, rs3.at[i, halves[h]], o["r3_s"].at[h, i], o["r3_r"].at[h, i], to).start()

            for h, d in enumerate(stays(final)):
                wait(rs1.at[1 - d, at, halves[h]], o["r2_s"].at[h, at])

    def put_cells(i):
        at = pl.ds(pl.multiple_of(i * LANES, LANES), LANES)
        return pltpu.make_async_copy(dcv.at[i], dcell.at[:, at], o["dc_m"].at[i])

    def scatter_3(k):
        mine, at, final = place(k)
        i = rem(k, bpg)

        @pl.when(mine & final)
        def _():
            for h in range(2):
                wait(rs3.at[i, halves[h]], o["r3_r"].at[h, i])
                add_rows(dcv.at[i, halves[h]], rs2.at[at, halves[h]], rs3.at[i, halves[h]])
            put_cells(i).start()

        @pl.when(mine & jnp.logical_not(final))
        def _():
            for h in range(2):
                wait(rs2.at[at, halves[h]], o["r3_s"].at[h, i])

    def add_map(k, r):
        x = jnp.concatenate([xs[gene_block(0, k)], xs[gene_block(1, k)]], axis=1)
        d = jnp.concatenate([dd[0, k, r], dd[1, k, r]], axis=1)
        new = lax.dot_general(x, d, (((1,), (1,)), ((), ())), preferred_element_type=F32)
        dm[r] = jnp.where(k == 0, 0.0, dm[r]) + new

    def multiply(k, piece):
        d = jnp.concatenate([dd[i, k].reshape(spots, LANES) for i in range(2)], axis=1)
        out = jnp.dot(mm[...], d, preferred_element_type=F32).astype(BF16)
        pss[rem(k, 2), 0] = out[:, :LANES]
        pss[rem(k, 2), 1] = out[:, LANES:]

    def put_logits(r):
        return pltpu.make_async_copy(mm.at[:, r * width : (r + 1) * width], dlog.at[r], o["dl_m"].at[r])

    def finish(r):
        col = jnp.concatenate([fm[0, 0, i : i + 1] + fm[1, 0, i : i + 1] for i in range(r * wl, (r + 1) * wl)], axis=1)

        def rows(i):
            at = pl.ds(pl.multiple_of(i * tile, tile), tile)
            cols = slice(r * width, (r + 1) * width)
            low = mm[at, cols].astype(F32)
            mm[at, cols] = (low * (dm[r, at, :] - col)).astype(BF16)

        loop(c_rows // tile, rows)
        put_logits(r).start()

    def take_pred(i):
        wait(gpr.at[i], o["gp_r"].at[i])
        wait(gps.at[i], o["gq_r"].at[i])

        def rows(r):
            gpb[i, r] = (gpr[i, r].astype(I32).astype(F32) * gps[i, r]).astype(BF16)

        loop(t_rows, rows)
        put_pred(i).start()

    behind = BEHIND * t_rows
    lag = jnp.where(owner, behind, LAG_BACK * jnp.maximum(cz - 1, n - 2 - cz))

    def produce(k, piece):
        @pl.when(piece == 0)
        def _():
            diff_outer(k)

        @pl.when((piece == 1) & (k + 1 < nb))
        def _():
            diff_inside(k + 1)

        @pl.when((piece == 2) & (k + 1 < nb))
        def _():
            diff_inner(k + 1)

        @pl.when((piece == 1) & (k + 1 == nb))
        def _():
            send_last()

    def drain():
        loop(n - 1, lambda j: wait(srow.at[cz], o["s_s"].at[j]))

        def sent(d):
            own, end = cz == d * (n - 1), cz == (1 - d) * (n - 1)

            @pl.when(jnp.logical_not(own))
            def _():
                def each(q):
                    k, r = div(q, t_rows), rem(q, t_rows)
                    wait(ab.at[d, k, r], o["a_s"].at[d, k, r])
                    wait(sc.at[d, k, r], o["c_s"].at[d, k, r])

                loop(nb * t_rows, each)

            @pl.when(jnp.logical_not(end))
            def _():
                def each(q):
                    k, r = div(q, t_rows), rem(q, t_rows)
                    wait(dd.at[d, k, r], o["d_s"].at[d, k, r])

                loop(nb * t_rows, each)
                wait(fm.at[d], o["f_s"].at[d])

        loop(2, sent)

        @pl.when(owner)
        def _():
            for i in range(wb):
                def each(j, i=i):
                    for copy in pred_copies(i, j):
                        copy.wait_send()

                loop(n // 2 - 1, each)
            for slot, ok, _ in coef_routes():
                @pl.when(ok)
                def _(slot=slot):
                    wait(con, o["co_s"].at[slot])

            def each(k):
                for side, ok, row, _ in halo_routes():
                    @pl.when(ok)
                    def _(side=side, row=row):
                        wait(ab.at[od, k, row], o["hg_s"].at[side, k])
                        wait(sc.at[od, k, row], o["hs_s"].at[side, k])
                        wait(hq.at[side, k], o["hd_s"].at[side, k])

                for which in range(3):
                    wait(es.at[which, k], o["e_s"].at[which, k])

            loop(nb, each)
            wait(spx.at[0], o["x_s"].at[0])

            def each_peer(j):
                for part, at in enumerate(gene_parts):
                    wait(gs.at[at], o["g_s"].at[part, j])
                wait(spr.at[here], o["p_s"].at[j])

            loop(nplane - 1, each_peer)

    def back_step(s):
        for i in range(wb):
            @pl.when(owner & (s == 2 * i + 1))
            def _(i=i):
                put_own(i)

        @pl.when(owner & (s < nb * t_rows))
        def _():
            produce(div(s, t_rows), rem(s, t_rows))

        def direction(d):
            own, end = cz == d * (n - 1), cz == (1 - d) * (n - 1)
            off = jnp.where(owner, behind, LAG_BACK * jnp.where(d == 0, cz - 1, n - 2 - cz))
            q = s - off
            to = (sx, sy, cz + 1 - 2 * d)

            @pl.when(jnp.logical_not(own) & (q >= 0) & (q < nb * t_rows))
            def _():
                k, r = back_chunk(q)
                at = dd.at[d, k, r]
                wait(at, o["d_r"].at[d, k, r])

                @pl.when(jnp.logical_not(end))
                def _():
                    remote(at, at, o["d_s"].at[d, k, r], o["d_r"].at[d, k, r], to).start()

            @pl.when(jnp.logical_not(own) & (q == nb * t_rows + 2))
            def _():
                wait(fm.at[d], o["f_r"].at[d])

                @pl.when(jnp.logical_not(end))
                def _():
                    remote(fm.at[d], fm.at[d], o["f_s"].at[d], o["f_r"].at[d], to).start()

        loop(2, direction)
        q = s - lag

        @pl.when((q >= 0) & (q < nb * t_rows))
        def _():
            add_map(*back_chunk(q))

        w = q - t_rows
        k, piece = div(w, t_rows), rem(w, t_rows)

        @pl.when((w >= 0) & (k < nb))
        def _():
            @pl.when(piece == 0)
            def _():
                multiply(k, piece)
                scatter_0(k)

        @pl.when((w >= 0) & (k == nb))
        def _():
            for r in range(t_rows):
                @pl.when(piece == r)
                def _(r=r):
                    finish(r)

        for stage, back_by, at in ((scatter_1, 0, 2), (scatter_2, 1, 2), (scatter_3, 2, 2)):
            @pl.when((w >= 0) & (piece == at) & (k >= back_by) & (k < nb + back_by))
            def _(stage=stage, back_by=back_by):
                stage(k - back_by)

        @pl.when(w == nb * t_rows + t_rows - 1)
        def _():
            drain()

        @pl.when((w == (nb + 1) * t_rows) & jnp.logical_not(owner))
        def _():
            for i in range(wb):
                take_pred(i)

    loop(t_rows * (nb + 4) + max(LAG_BACK * lead, behind), back_step)

    losses[0] = jnp.max(fm[0, 1, 0:1, :] + fm[1, 1, 0:1, :]) * -0.5
    losses[1] = jnp.max(fm[0, 1, 1:2, :]) * (-1.0 / all_spots)

    for r in range(t_rows):
        put_logits(r).wait()
    for i in range(bpg):
        put_cells(i).wait()

    for i in range(wb):
        put_pred(i).wait()


def cells_first(x, out):
    for r in range(x.shape[0]):
        out[:, r, :] = x[r].astype(F32)


def per_device(logits, cells_expr, spatial, gene_mask, slide_id, edge_weight, edge_mask):
    c_rows, t_rows, width = logits.shape
    genes = cells_expr.shape[1]
    n, nsx, nsy = (lax.axis_size(a) for a in ("cells", "sx", "sy"))
    spots = t_rows * width
    share = genes // n
    wide = max(share, LANES)
    wb = wide // LANES
    nb = genes // 2 // LANES
    nplane = nsx * nsy
    grid = (t_rows, width, LANES)
    vm, dma = pltpu.VMEM, pltpu.SemaphoreType.DMA
    scratch = dict(
        xs=vm((2 * nb, c_rows, LANES), BF16),
        mm=vm((c_rows, spots), BF16),
        mt=vm((t_rows, width, c_rows), BF16),
        dm=vm((t_rows, c_rows, width), F32),
        srow=vm((n, spots // LANES, LANES), F32),
        ab=vm((2, nb, *grid), I16),
        sc=vm((2, nb, t_rows, 1, LANES), F32),
        tt=vm((t_rows, 4 * width, 2 * LANES), F32),
        gg=vm((nb, *grid), F32),
        sm=vm((nb, *grid), F32),
        sp=vm((nb, *grid), F32),
        pad=vm((2, t_rows + 2, width + 16, LANES), F32),
        hg=vm((2, nb, width, LANES), I16),
        hs=vm((2, nb, 1, LANES), F32),
        hd=vm((2, nb, width, LANES), BF16),
        hq=vm((2, nb, width, LANES), BF16),
        es=vm((3, nb, 8, LANES), F32),
        er=vm((3, nb, 8, LANES), F32),
        cf=vm((6, *grid), F32),
        cb=vm((6, *grid), BF16),
        hot=vm(grid, F32),
        con=vm((t_rows, 8, width), F32),
        cor=vm((5, t_rows, 8, width), F32),
        acc=vm((3, *grid), F32),
        gs=vm((nb, 8, LANES), F32),
        gr=vm((nplane, nb, 8, LANES), F32),
        spx=vm((2, 3, spots // LANES, LANES), F32),
        gc=vm((nb, 8, LANES), F32),
        spr=vm((nplane, 8, LANES), F32),
        dd=vm((2, nb, *grid), BF16),
        fm=vm((2, 2, 8, LANES), F32),
        pss=vm((2, 2, c_rows, LANES), BF16),
        rs1=vm((2, nb // 2, c_rows, LANES), BF16),
        rs2=vm((nb // 2, c_rows, LANES), BF16),
        rs3=vm((nb // 4, c_rows, LANES), BF16),
        dcv=vm((nb // 4, c_rows, LANES), BF16),
        gpr=vm((wb, *grid), I16),
        gps=vm((wb, t_rows, 1, LANES), F32),
        gpb=vm((wb, *grid), BF16),
        lg_m=dma((t_rows,)),
        xs_m=dma((2 * nb,)),
        sp_m=dma((nb,)),
        s_s=dma((n,)),
        s_r=dma((n,)),
        a_s=dma((2, nb, t_rows)),
        a_r=dma((2, nb, t_rows)),
        c_s=dma((2, nb, t_rows)),
        c_r=dma((2, nb, t_rows)),
        hg_s=dma((2, nb)),
        hg_r=dma((2, nb)),
        hs_s=dma((2, nb)),
        hs_r=dma((2, nb)),
        hd_s=dma((2, nb)),
        hd_r=dma((2, nb)),
        e_s=dma((3, nb)),
        e_r=dma((3, nb)),
        co_s=dma((5,)),
        co_r=dma((5,)),
        g_s=dma((2, nplane)),
        g_r=dma((2, nplane)),
        p_s=dma((nplane,)),
        p_r=dma((nplane,)),
        x_s=dma((1,)),
        x_r=dma((1,)),
        d_s=dma((2, nb, t_rows)),
        d_r=dma((2, nb, t_rows)),
        f_s=dma((2,)),
        f_r=dma((2,)),
        r1_s=dma((2, nb // 2)),
        r1_r=dma((2, nb // 2)),
        r2_s=dma((2, nb // 2)),
        r2_r=dma((2, nb // 2)),
        r3_s=dma((2, nb // 4)),
        r3_r=dma((2, nb // 4)),
        gp_s=dma((max(n // 2 - 1, 1), wb)),
        gp_r=dma((wb,)),
        gq_s=dma((max(n // 2 - 1, 1), wb)),
        gq_r=dma((wb,)),
        gp_m=dma((wb,)),
        dl_m=dma((t_rows,)),
        dc_m=dma((nb // 4,)),
    )
    names = ("lg", "cells", "spat", "gmask", "slide", "ew", "em", "losses", "gp", "dlog", "dcell")
    names += tuple(scratch)
    sizes = (n, nsx, nsy, share, spots * nplane)
    anywhere, local = pl.BlockSpec(memory_space=pl.ANY), pl.BlockSpec(memory_space=pltpu.VMEM)
    losses, pred, d_logits, d_cells = pl.pallas_call(
        functools.partial(kernel, names, sizes),
        out_shape=(
            jax.ShapeDtypeStruct((2,), F32),
            jax.ShapeDtypeStruct((t_rows, width, wide), BF16),
            jax.ShapeDtypeStruct((t_rows, c_rows, width), BF16),
            jax.ShapeDtypeStruct((c_rows, genes // nplane), BF16),
        ),
        in_specs=[anywhere] * 3 + [local] * 4,
        out_specs=(pl.BlockSpec(memory_space=pltpu.SMEM), anywhere, anywhere, anywhere),
        scratch_shapes=list(scratch.values()),
        compiler_params=pltpu.CompilerParams(
            collective_id=0, has_side_effects=True, vmem_limit_bytes=VMEM
        ),
        cost_estimate=pl.CostEstimate(
            flops=6 * c_rows * spots * genes, bytes_accessed=32 << 20, transcendentals=c_rows * spots
        ),
    )(logits, cells_expr, spatial, gene_mask, slide_id, edge_weight, edge_mask)
    if wide > share:
        pred = lax.dynamic_slice_in_dim(pred, rem(lax.axis_index("cells") * share, wide), share, 2)
    tile = c_rows // 2 if c_rows % 64 == 0 else c_rows
    d_logits = pl.pallas_call(
        cells_first,
        grid=(c_rows // tile,),
        out_shape=jax.ShapeDtypeStruct(logits.shape, F32),
        in_specs=[pl.BlockSpec((t_rows, tile, width), lambda i: (0, i, 0))],
        out_specs=pl.BlockSpec((tile, t_rows, width), lambda i: (i, 0, 0)),
        compiler_params=pltpu.CompilerParams(vmem_limit_bytes=60 * 1024 * 1024),
    )(d_logits)
    return (losses, pred.astype(F32), d_logits, d_cells.astype(F32))


BEHIND = 3
LAG_SUM = 3
LAG_BACK = 3
VMEM = 64 * 1024 * 1024 - 512 * 1024


def solution(mesh):
    return jax.shard_map(
        per_device,
        mesh=mesh,
        in_specs=(
            P("cells", "sx", "sy"),
            P("cells", None),
            P("sx", "sy", None),
            P(),
            P("sx", "sy"),
            P(None, "sx", "sy"),
            P(None, "sx", "sy"),
        ),
        out_specs=(P(), P("sx", "sy", "cells"), P("cells", "sx", "sy"), P("cells", ("sx", "sy"))),
        check_vma=False,
    )
```

```python
import functools

import jax
import jax.numpy as jnp
from jax import lax
from jax.experimental import pallas as pl
from jax.experimental.pallas import tpu as pltpu
from jax.sharding import PartitionSpec as P

EPS = 1e-06
OFFSETS = ((0, 1), (0, -1), (1, 0), (-1, 0), (-1, 1), (1, -1))
LANES = 128
TOP = 32767.0
MESH = pl.DeviceIdType.MESH
F32, BF16, I16, I32 = jnp.float32, jnp.bfloat16, jnp.int16, jnp.int32
rem, div = lax.rem, lax.div


def loop(count, body):
    lax.fori_loop(0, count, lambda i, _: (body(i), 0)[1], 0)


def remote(src, dst, sent, got, to):
    return pltpu.make_async_remote_copy(
        src_ref=src, dst_ref=dst, send_sem=sent, recv_sem=got, device_id=to, device_id_type=MESH
    )


def wait(ref, sem):
    pltpu.make_async_copy(ref, ref, sem).wait()


def spread(row):
    parts = [
        jnp.broadcast_to(row[:, at : at + LANES], (LANES, LANES)).T
        for at in range(0, row.shape[1], LANES)
    ]
    return jnp.concatenate(parts, axis=0)


def fold(x):
    return jnp.sum(x.reshape(x.shape[0] // 8, 8, x.shape[1]), axis=0)


def kernel(names, sizes, *refs):
    n, nsx, nsy, share, all_spots = sizes
    o = dict(zip(names, refs, strict=True))
    lg, cells, spat, gmask, slide, ew, em = (o[k] for k in names[:7])
    losses, gp, dlog, dcell = (o[k] for k in names[7:11])
    xs, mm, mt, dm, srow, ab, sc, tt = (o[k] for k in names[11:19])
    gg, sm, sp, pad, hg, hs, hd, hq = (o[k] for k in names[19:27])
    es, er, cf, cb, hot, con, cor, acc = (o[k] for k in names[27:35])
    gs, gr, spx, gc, spr, dd, fm = (o[k] for k in names[35:42])
    pss, rs1, rs2, rs3, dcv, gpr, gps, gpb = (o[k] for k in names[42:50])

    c_rows, t_rows, width = lg.shape
    spots = t_rows * width
    nb = cells.shape[1] // 2 // LANES
    wl = width // LANES
    wb = gpr.shape[0]
    nplane = nsx * nsy
    half = nb // 2
    bpg = nb // 4
    tile = LANES
    tiles = c_rows // tile
    quarter = c_rows // t_rows
    sub = min(64, width)
    mid = slice(8, 8 + width)

    sx, sy, cz = (lax.axis_index(a) for a in ("sx", "sy", "cells"))
    here = sx * nsy + sy
    owner = (cz == 0) | (cz == n - 1)
    od = jnp.where(cz == 0, 0, 1)
    up, down = sx > 0, sx < nsx - 1
    mate = (sx, 1 - sy, cz)

    def gene_block(d, k):
        return jnp.where(d == 0, rem(k + half, nb), nb + k)

    for r in range(t_rows):
        pltpu.make_async_copy(lg.at[:, r, :], dm.at[r], o["lg_m"].at[r]).start()

    def load_cells(b):
        at = pl.ds(pl.multiple_of(b * LANES, LANES), LANES)
        return pltpu.make_async_copy(cells.at[:, at], xs.at[b], o["xs_m"].at[b])

    loop(2 * nb, lambda b: load_cells(b).start())

    def load_truth(k):
        at = pl.ds(pl.multiple_of(gene_block(od, k) * LANES, LANES), LANES)
        return pltpu.make_async_copy(spat.at[:, :, at], sp.at[k], o["sp_m"].at[k])

    @pl.when(owner)
    def _():
        loop(nb, lambda k: load_truth(k).start())

    barrier = pltpu.get_barrier_semaphore()

    def greet_line(j):
        to = (sx, sy, rem(cz + j + 1, n))
        pl.semaphore_signal(barrier, inc=1, device_id=to, device_id_type=MESH)

    def greet_plane(j):
        t = rem(here + j + 1, nplane)
        to = (div(t, nsy), rem(t, nsy), cz)
        pl.semaphore_signal(barrier, inc=1, device_id=to, device_id_type=MESH)

    loop(n - 1, greet_line)
    loop(nplane - 1, greet_plane)

    for r in range(t_rows):
        pltpu.make_async_copy(lg.at[:, r, :], dm.at[r], o["lg_m"].at[r]).wait()

        def exps(i, s, r=r):
            at = pl.ds(i * tile, tile)
            x = jnp.exp(dm[r, at, :])
            dm[r, at, :] = x
            return s + fold(x)

        s = lax.fori_loop(0, c_rows // tile, exps, jnp.zeros((8, width), F32))
        s = jnp.sum(s, axis=0, keepdims=True)
        for h in range(wl):
            srow[cz, pl.ds(r * wl + h, 1), :] = s[:, h * LANES : (h + 1) * LANES]

    pl.semaphore_wait(barrier, n - 1 + nplane - 1)

    def send_sums(j):
        to = (sx, sy, rem(cz + j + 1, n))
        remote(srow.at[cz], srow.at[cz], o["s_s"].at[j], o["s_r"].at[cz], to).start()

    loop(n - 1, send_sums)

    def turn(dst, first):
        def each(i):
            for r in range(t_rows):
                at = pl.ds(pl.multiple_of((i + first) * LANES, LANES), LANES)
                dst[i, r] = dm[r, at, :].T

        return each

    turned = ((gg, 0, min(tiles, nb)), (sm, nb, max(tiles - nb, 0)))
    for dst, first, count in turned:
        loop(count, turn(dst, first))

    def wait_sums(j):
        z = rem(cz + j + 1, n)
        wait(srow.at[z], o["s_r"].at[z])

    loop(n - 1, wait_sums)
    total = srow[0]
    for z in range(1, n):
        total = total + srow[z]
    inv = 1.0 / total
    inv_rows = [
        jnp.concatenate([inv[r * wl + h : r * wl + h + 1] for h in range(wl)], axis=1)
        for r in range(t_rows)
    ]
    for r in range(t_rows):
        acc[0, r] = spread(inv_rows[r])

    for dst, first, count in turned:
        def scale(i, dst=dst, first=first):
            at = pl.ds(pl.multiple_of((i + first) * LANES, LANES), LANES)
            for r in range(t_rows):
                mt[r, :, at] = (dst[i, r] * acc[0, r]).astype(BF16)

        loop(count, scale)

    def keep_mapping():
        for r in range(t_rows):
            def each(i, r=r):
                at = pl.ds(pl.multiple_of(i * LANES, LANES), LANES)
                mm[at, r * width : (r + 1) * width] = (dm[r, at, :] * inv_rows[r]).astype(BF16)

            loop(tiles, each)

    loop(2 * nb, lambda b: load_cells(b).wait())

    def coef_routes():
        return (
            (0, down, (sx + 1, sy, cz)),
            (1, up, (sx - 1, sy, cz)),
            (2, sx >= 0, mate),
            (3, down, (sx + 1, 1 - sy, cz)),
            (4, up, (sx - 1, 1 - sy, cz)),
        )


    def predict(d, pair, r):
        g = gene_block(d, 2 * pair)
        w = jnp.concatenate([xs[g], xs[g + 1]], axis=1)
        at = pl.ds(pl.multiple_of((2 * d + rem(pair, 2)) * width, 8), width)
        tt[r, at, :] = jnp.dot(mt[r], w, preferred_element_type=F32)

    def predicted(d, k, r):
        at = pl.ds(pl.multiple_of((2 * d + rem(div(k, 2), 2)) * width, 8), width)
        return tt[r, at, pl.ds(pl.multiple_of(rem(k, 2) * LANES, LANES), LANES)]

    def put(d, k, r, t):
        top = jnp.maximum(jnp.max(jnp.abs(t), axis=0, keepdims=True), 1e-30)
        ab[d, k, r] = jnp.round(t * (TOP / top)).astype(I32).astype(I16)
        sc[d, k, r] = top * (1.0 / TOP)

    def pass_on(d, k, r):
        to = (sx, sy, cz + 2 * d - 1)
        remote(ab.at[d, k, r], ab.at[d, k, r], o["a_s"].at[d, k, r], o["a_r"].at[d, k, r], to).start()
        remote(sc.at[d, k, r], sc.at[d, k, r], o["c_s"].at[d, k, r], o["c_r"].at[d, k, r], to).start()

    def chunk_of(q):
        return div(q, t_rows), rem(rem(q, t_rows) * (t_rows - 1), t_rows)

    @pl.when(owner)
    def _():
        d = 1 - od

        def first(q):
            k, r = chunk_of(q)

            @pl.when(rem(k, 2) == 0)
            def _():
                predict(d, div(k, 2), r)

            put(d, k, r, predicted(d, k, r))
            pass_on(d, k, r)

        loop(nb * t_rows, first)

        for r in range(t_rows):
            rows = [ew[j, r : r + 1, :] * em[j, r : r + 1, :].astype(F32) for j in range(6)]
            con[r] = jnp.concatenate(rows + [jnp.zeros((2, width), F32)], axis=0)
            for j in range(6):
                cf[j, r] = spread(rows[j])
            hot[r] = spread(slide[r : r + 1, :].astype(F32))
        acc[...] = jnp.zeros(acc.shape, F32)

        for slot, ok, to in coef_routes():
            @pl.when(ok)
            def _(slot=slot, to=to):
                remote(con, cor.at[slot], o["co_s"].at[slot], o["co_r"].at[slot], to).start()

        loop(nb, lambda k: load_truth(k).wait())

    def back_coefs():
        for slot, ok in ((0, up), (1, down), (2, sx >= 0), (3, up), (4, down)):
            @pl.when(ok)
            def _(slot=slot):
                wait(cor.at[slot], o["co_r"].at[slot])

        lane = lax.broadcasted_iota(I32, (8, width), 1)
        for j, (dr, dc) in enumerate(OFFSETS):
            for r in range(t_rows):
                at = r - dr
                if at < 0:
                    base, side, ok = cor[0, t_rows - 1], cor[3, t_rows - 1], up
                elif at >= t_rows:
                    base, side, ok = cor[1, 0], cor[4, 0], down
                else:
                    base, side, ok = con[at], cor[2, at], sx >= 0
                base = jnp.where(ok, base, 0.0)
                if dc:
                    by, edge = (1, 0) if dc == 1 else (width - 1, width - 1)
                    side = jnp.where(ok & (sy == (1 if dc == 1 else 0)), side, 0.0)
                    base = jnp.where(lane == edge, pltpu.roll(side, by, 1), pltpu.roll(base, by, 1))
                cb[j, r] = spread(base[j : j + 1]).astype(BF16)

    def send_edges(slot, which, k, rows):
        parts = [
            jnp.where(sy == 1, pad[slot, row, 8:9, :], pad[slot, row, 7 + width : 8 + width, :])
            for row in rows
        ]
        parts.append(jnp.zeros((8 - len(parts), LANES), F32))
        es[which, k] = jnp.concatenate(parts, axis=0)
        remote(es.at[which, k], er.at[which, k], o["e_s"].at[which, k], o["e_r"].at[which, k], mate).start()

    def take_edges(slot, which, k, rows):
        wait(er.at[which, k], o["e_r"].at[which, k])
        for i, row in enumerate(rows):
            edge = er[which, k, i : i + 1, :]
            pad[slot, row, 8 + width : 9 + width, :] = jnp.where(sy == 0, edge, 0.0)
            pad[slot, row, 7:8, :] = jnp.where(sy == 1, edge, 0.0)

    sides = ((0, up, 0), (1, down, t_rows + 1))

    def prepare(k):
        for side, ok, row in sides:
            @pl.when(ok)
            def _(side=side, row=row):
                wait(hg.at[side, k], o["hg_r"].at[side, k])
                wait(hs.at[side, k], o["hs_r"].at[side, k])
                pad[0, row, mid, :] = hg[side, k].astype(I32).astype(F32) * hs[side, k]

            @pl.when(jnp.logical_not(ok))
            def _(row=row):
                pad[0, row, mid, :] = jnp.zeros((width, LANES), F32)

        def rows(r):
            pad[0, r + 1, mid, :] = gg[k, r]

        loop(t_rows, rows)
        send_edges(0, 0, k, range(t_rows + 2))

    def smoothing(k):
        take_edges(0, 0, k, range(t_rows + 2))
        at = pl.ds(pl.multiple_of(gene_block(od, k) * LANES, LANES), LANES)
        mask = gmask[:, at].astype(F32)
        m0, m1 = mask[0:1], mask[1:2]

        def rows(r, sums):
            sums = list(sums)
            for u in range(0, width, sub):
                here_u = slice(u, u + sub)
                a = pad[0, r + 1, 8 + u : 8 + u + sub, :]
                for j, (dr, dc) in enumerate(OFFSETS):
                    a = a + cf[j, r, here_u, :] * pad[0, r + 1 + dr, 8 + dc + u : 8 + dc + u + sub, :]
                sm[k, r, here_u, :] = a
                t = sp[k, r, here_u, :]
                h = hot[r, here_u, :]
                mk = m0 + h * (m1 - m0)
                for i, x in enumerate((a * t, a * a, t * t)):
                    sums[2 * i] = sums[2 * i] + fold(x)
                    sums[2 * i + 1] = sums[2 * i + 1] + fold(x * h)
                    acc[i, r, here_u, :] = acc[i, r, here_u, :] + x * mk
            return tuple(sums)

        sums = lax.fori_loop(0, t_rows, rows, (jnp.zeros((8, LANES), F32),) * 6)
        parts = []
        for i in range(3):
            both = jnp.sum(sums[2 * i], axis=0, keepdims=True)
            one = jnp.sum(sums[2 * i + 1], axis=0, keepdims=True)
            parts += [both - one, one]
        gs[k] = jnp.concatenate(parts + [jnp.zeros((2, LANES), F32)], axis=0)

    def own_block(t, i):
        b = div(t * share, LANES) + i - od * nb
        return jnp.where(od == 0, rem(b + half, nb), b)

    def pred_copies(i, j):
        t = jnp.where(od == 0, j + 1, n - 2 - j)
        k = own_block(t, i)
        to = (sx, sy, t)
        return (
            remote(ab.at[od, k], gpr.at[i], o["gp_s"].at[j, i], o["gp_r"].at[i], to),
            remote(sc.at[od, k], gps.at[i], o["gq_s"].at[j, i], o["gq_r"].at[i], to),
        )

    def send_pred(i):
        def each(j):
            for copy in pred_copies(i, j):
                copy.start()

        loop(n // 2 - 1, each)

    early_pred = 1 if n == 4 else 0

    def plane_peer(j):
        t = rem(here + j + 1, nplane)
        return t, (div(t, nsy), rem(t, nsy), cz)

    gene_parts = (pl.ds(0, nb - 1), pl.ds(nb - 1, 1))

    def send_genes(part):
        at = gene_parts[part]

        def each(j):
            _, to = plane_peer(j)
            sems = o["g_s"].at[part, j], o["g_r"].at[part, here]
            remote(gs.at[at], gr.at[here, at], *sems, to).start()

        loop(nplane - 1, each)

    lead = max(n - 3, 0)

    def sum_step(s):
        def direction(d):
            own, first = cz == d * (n - 1), cz == (1 - d) * (n - 1)
            off = jnp.where(owner, 0, LAG_SUM * jnp.where(d == 1, cz - 1, n - 2 - cz))
            q = s - off

            @pl.when(jnp.logical_not(first) & (q >= 0) & (q < nb * t_rows))
            def _():
                k, r = chunk_of(q)
                wait(ab.at[d, k, r], o["a_r"].at[d, k, r])
                wait(sc.at[d, k, r], o["c_r"].at[d, k, r])
                got = ab[d, k, r].astype(I32).astype(F32) * sc[d, k, r]
                t = predicted(d, k, r) + got
                put(d, k, r, t)

                @pl.when(jnp.logical_not(own))
                def _():
                    pass_on(d, k, r)

                @pl.when(own)
                def _():
                    gg[k, r] = t
                    for side, ok, row, to in halo_routes():
                        @pl.when(ok & (r == row))
                        def _(side=side, row=row, to=to):
                            remote(ab.at[d, k, row], hg.at[side, k], o["hg_s"].at[side, k], o["hg_r"].at[side, k], to).start()
                            remote(sc.at[d, k, row], hs.at[side, k], o["hs_s"].at[side, k], o["hs_r"].at[side, k], to).start()

                    i = rem(q, t_rows)

                    @pl.when((k > 0) & (i == 1))
                    def _():
                        prepare(k - 1)

                    @pl.when((k > 0) & (i == t_rows - 1))
                    def _():
                        smoothing(k - 1)

                    @pl.when((k == nb - 1) & (i == t_rows - 1))
                    def _():
                        send_genes(0)

                    if early_pred:
                        @pl.when(q == 3 * nb * t_rows // 4)
                        def _():
                            for i in range(early_pred):
                                send_pred(i)

                @pl.when((rem(k, 2) == d) & (k + 2 - rem(k, 2) < nb))
                def _():
                    predict(d, div(k, 2) + 1, r)

        loop(2, direction)

        @pl.when(owner & (s == half * t_rows))
        def _():
            back_coefs()

    def halo_routes():
        return ((1, up, 0, (sx - 1, sy, cz)), (0, down, t_rows - 1, (sx + 1, sy, cz)))

    def first_block(d):
        @pl.when(cz != (1 - d) * (n - 1))
        def _():
            loop(t_rows, lambda r: predict(d, 0, r))

    loop(2, first_block)
    keep_mapping()
    loop(nb * t_rows + LAG_SUM * lead, sum_step)

    def diff_smooth(k, r, at):
        tc0, tc1, sc0, sc1, m0, m1 = (gc[k, i : i + 1, :] for i in range(6))
        h = hot[r, at, :]
        mk = m0 + h * (m1 - m0)
        by_truth = tc0 + h * (tc1 - tc0) + mk * acc[1, r, at, :]
        by_smooth = sc0 + h * (sc1 - sc0) + mk * acc[2, r, at, :]
        return by_truth * sp[k, r, at, :] + by_smooth * sm[k, r, at, :]

    def send_borders(k):
        for side, ok, row, to in halo_routes():
            @pl.when(ok)
            def _(side=side, row=row, to=to):
                for u in range(0, width, sub):
                    hq[side, k, u : u + sub, :] = diff_smooth(k, row, slice(u, u + sub)).astype(BF16)
                remote(hq.at[side, k], hd.at[side, k], o["hd_s"].at[side, k], o["hd_r"].at[side, k], to).start()

    def diff_inside(k):
        slot = rem(k, 2)

        def rows(r):
            for u in range(0, width, sub):
                pad[slot, r + 1, 8 + u : 8 + u + sub, :] = diff_smooth(k, r, slice(u, u + sub))

        loop(t_rows, rows)
        send_edges(slot, 1, k, range(1, t_rows + 1))

    def diff_border(k):
        slot = rem(k, 2)
        for side, ok, row in sides:
            @pl.when(ok)
            def _(side=side, row=row):
                wait(hd.at[side, k], o["hd_r"].at[side, k])
                pad[slot, row, mid, :] = hd[side, k].astype(F32)

            @pl.when(jnp.logical_not(ok))
            def _(row=row):
                pad[slot, row, mid, :] = jnp.zeros((width, LANES), F32)

        send_edges(slot, 2, k, (0, t_rows + 1))

    back = cz + 1 - 2 * od

    def diff_pred(k, rows):
        slot = rem(k, 2)
        for r in rows:
            for u in range(0, width, sub):
                here_u = slice(u, u + sub)
                a = pad[slot, r + 1, 8 + u : 8 + u + sub, :]
                for j, (dr, dc) in enumerate(OFFSETS):
                    w = cb[j, r, here_u, :].astype(F32)
                    a = a + w * pad[slot, r + 1 - dr, 8 - dc + u : 8 - dc + u + sub, :]
                low = a.astype(BF16)
                dd[od, k, r, here_u, :] = low
                acc[0, r, here_u, :] = acc[0, r, here_u, :] + gg[k, r, here_u, :] * low.astype(F32)
            at = dd.at[od, k, r]
            remote(at, at, o["d_s"].at[od, k, r], o["d_r"].at[od, k, r], (sx, sy, back)).start()

    def back_chunk(q):
        i = rem(q, t_rows)
        return div(q, t_rows), jnp.where(i < t_rows - 2, i + 1, jnp.where(i == t_rows - 2, 0, i))

    def diff_inner(k):
        take_edges(rem(k, 2), 1, k, range(1, t_rows + 1))
        diff_pred(k, range(1, t_rows - 1))
        diff_border(k)

    def diff_outer(k):
        take_edges(rem(k, 2), 2, k, (0, t_rows + 1))
        diff_pred(k, (0, t_rows - 1))

    def spot_rows(i):
        return [
            jnp.sum(acc[i, r, h * LANES : (h + 1) * LANES, :].T, axis=0, keepdims=True)
            for r in range(t_rows)
            for h in range(wl)
        ]

    def put_pred(i):
        at = slice(i * LANES, (i + 1) * LANES)
        return pltpu.make_async_copy(gpb.at[i], gp.at[:, :, at], o["gp_m"].at[i])

    def put_own(i):
        k = own_block(cz, i)

        def rows(r):
            gpb[i, r] = gg[k, r].astype(BF16)

        loop(t_rows, rows)
        put_pred(i).start()

    @pl.when(owner)
    def _():
        prepare(nb - 1)
        smoothing(nb - 1)

        send_genes(1)
        for i in range(3):
            for at, row in enumerate(spot_rows(i)):
                spx[0, i, at : at + 1, :] = row
        remote(spx.at[0], spx.at[1], o["x_s"].at[0], o["x_r"].at[0], (sx, sy, n - 1 - cz)).start()
        gr[here] = gs[...]
        def wait_genes(j):
            t, _ = plane_peer(j)
            for part, at in enumerate(gene_parts):
                wait(gr.at[t, at], o["g_r"].at[part, t])

        loop(nplane - 1, wait_genes)
        count = jnp.maximum(jnp.sum(gmask[...].astype(F32), axis=1, keepdims=True), 1.0)

        def genes(k, gl):
            tot = gr[0, k]
            for t in range(1, nplane):
                tot = tot + gr[t, k]
            ib, ic = lax.rsqrt(tot[2:4] + EPS), lax.rsqrt(tot[4:6] + EPS)
            cos = tot[0:2] * ib * ic
            at = pl.ds(pl.multiple_of(gene_block(od, k) * LANES, LANES), LANES)
            mask = gmask[:, at].astype(F32)
            scale = -mask / (2.0 * count)
            gc[k, 0:2, :] = scale * ib * ic
            gc[k, 2:4, :] = -scale * cos * ib * ib
            gc[k, 4:6, :] = mask
            return gl + mask * cos / count

        gl = lax.fori_loop(0, nb, genes, jnp.zeros((2, LANES), F32))
        gene_part = jnp.sum(jnp.sum(gl, axis=0, keepdims=True), axis=1, keepdims=True)

        wait(spx.at[1], o["x_r"].at[0])
        a, b, c = (spx[0, i] + spx[1, i] for i in range(3))
        ib, ic = lax.rsqrt(b + EPS), lax.rsqrt(c + EPS)
        cos = a * ib * ic
        by_truth = (-1.0 / all_spots) * ib * ic
        by_smooth = (1.0 / all_spots) * cos * ib * ib
        for r in range(t_rows):
            for h in range(wl):
                at, i = slice(h * LANES, (h + 1) * LANES), r * wl + h
                acc[1, r, at, :] = spread(by_truth[i : i + 1])
                acc[2, r, at, :] = spread(by_smooth[i : i + 1])
        acc[0] = jnp.zeros(acc.shape[1:], F32)
        spot_part = jnp.sum(jnp.sum(cos, axis=0, keepdims=True), axis=1, keepdims=True)
        spr[here] = jnp.broadcast_to(spot_part, (8, LANES))
        fm[od, 1] = jnp.broadcast_to(gene_part, (8, LANES))

        def send_spot(j):
            _, to = plane_peer(j)
            remote(spr.at[here], spr.at[here], o["p_s"].at[j], o["p_r"].at[here], to).start()

        send_borders(0)
        diff_inside(0)
        send_borders(1)
        take_edges(0, 1, 0, range(1, t_rows + 1))
        diff_pred(0, range(1, t_rows - 1))
        loop(nb - 2, lambda k: send_borders(k + 2))
        loop(nplane - 1, send_spot)
        diff_border(0)

    def send_last():
        def wait_spot(j):
            t, _ = plane_peer(j)
            wait(spr.at[t], o["p_r"].at[t])

        loop(nplane - 1, wait_spot)
        spot_all = spr[0, 0:1, :]
        for t in range(1, nplane):
            spot_all = spot_all + spr[t, 0:1, :]
        rows = spot_rows(0)
        if len(rows) < 8:
            rows.append(jnp.zeros((8 - len(rows), LANES), F32))
        fm[od, 0] = jnp.concatenate(rows, axis=0)
        fm[od, 1, 1:2, :] = spot_all
        remote(fm.at[od], fm.at[od], o["f_s"].at[od], o["f_r"].at[od], (sx, sy, back)).start()
        for i in range(early_pred, wb):
            send_pred(i)


    sy_bit, sx_bit = div(sx, 2), rem(sx, 2)
    over_y, over_x = (sx + 2 - 4 * sy_bit, sy, cz), (sx + 1 - 2 * sx_bit, sy, cz)

    def place(k):
        jj = div(k, bpg)
        hi = div(jj, 2)
        return rem(jj, 2) == sy, hi * bpg + rem(k, bpg), jnp.where(sy_bit == 0, 1 - hi, hi) == sx_bit

    halves = (pl.ds(0, c_rows // 2), pl.ds(c_rows // 2, c_rows // 2))

    def add_rows(dst, *terms):
        count = dst.shape[0] // 2

        def rows(i):
            at = pl.ds(pl.multiple_of(i * count, 8), count)
            dst[at, :] = sum(t[at, :].astype(F32) for t in terms).astype(dst.dtype)

        loop(2, rows)

    def multiply(k):
        mine, at, _ = place(k)
        slot = rem(k, 2)
        block = jnp.concatenate([dd[i, k].reshape(spots, LANES) for i in range(2)], axis=1)
        out = jnp.dot(mm[...], block, preferred_element_type=F32).astype(BF16)
        pss[slot, 0] = out[:, :LANES]
        pss[slot, 1] = out[:, LANES:]

        @pl.when(jnp.logical_not(mine))
        def _():
            for h, half in enumerate(halves):
                for d in range(2):
                    src, dst = pss.at[slot, d, half], rs1.at[d, at, half]
                    remote(src, dst, o["r1_s"].at[d, at, h], o["r1_r"].at[d, at, h], mate).start()

    def stays(final):
        return sy_bit, jnp.where(final, sy_bit, 1 - sy_bit)

    def scatter_1(k):
        mine, at, final = place(k)
        slot = rem(k, 2)

        @pl.when(mine)
        def _():
            for h, (stay, to) in enumerate(zip(stays(final), (over_y, over_x), strict=True)):
                d, half = 1 - stay, halves[h]
                src = rs1.at[d, at, half]
                wait(src, o["r1_r"].at[d, at, h])
                add_rows(src, pss.at[slot, d, half], src)
                remote(src, rs2.at[at, half], o["r2_s"].at[h, at], o["r2_r"].at[h, at], to).start()

        @pl.when(jnp.logical_not(mine))
        def _():
            for d in range(2):
                for h, half in enumerate(halves):
                    wait(pss.at[slot, d, half], o["r1_s"].at[d, at, h])

    def scatter_2(k):
        mine, at, final = place(k)
        slot = rem(k, 2)

        @pl.when(mine)
        def _():
            i = rem(k, bpg)
            for h, (d, to) in enumerate(zip(stays(final), (over_x, over_y), strict=True)):
                half = halves[h]
                part, first = rs2.at[at, half], rs1.at[d, at, half]
                wait(first, o["r1_r"].at[d, at, h])
                wait(part, o["r2_r"].at[h, at])
                add_rows(part, pss.at[slot, d, half], first, part)

                @pl.when(jnp.logical_not(final))
                def _(h=h, part=part, half=half, to=to):
                    remote(part, rs3.at[i, half], o["r3_s"].at[h, i], o["r3_r"].at[h, i], to).start()

            for h, d in enumerate(stays(final)):
                wait(rs1.at[1 - d, at, halves[h]], o["r2_s"].at[h, at])

    def put_cells(i):
        at = pl.ds(pl.multiple_of(i * LANES, LANES), LANES)
        return pltpu.make_async_copy(dcv.at[i], dcell.at[:, at], o["dc_m"].at[i])

    def scatter_3(k):
        mine, at, final = place(k)
        i = rem(k, bpg)

        @pl.when(mine & final)
        def _():
            for h in range(2):
                wait(rs3.at[i, halves[h]], o["r3_r"].at[h, i])
                add_rows(dcv.at[i, halves[h]], rs2.at[at, halves[h]], rs3.at[i, halves[h]])
            put_cells(i).start()

        @pl.when(mine & jnp.logical_not(final))
        def _():
            for h in range(2):
                wait(rs2.at[at, halves[h]], o["r3_s"].at[h, i])

    def add_map(k, r):
        x = jnp.concatenate([xs[gene_block(0, k)], xs[gene_block(1, k)]], axis=1)
        d = jnp.concatenate([dd[0, k, r], dd[1, k, r]], axis=1)
        new = lax.dot_general(x, d, (((1,), (1,)), ((), ())), preferred_element_type=F32)
        dm[r] = jnp.where(k == 0, 0.0, dm[r]) + new

    def put_logits(r):
        return pltpu.make_async_copy(mm.at[:, r * width : (r + 1) * width], dlog.at[r], o["dl_m"].at[r])

    def finish(r):
        col = jnp.concatenate([fm[0, 0, i : i + 1] + fm[1, 0, i : i + 1] for i in range(r * wl, (r + 1) * wl)], axis=1)

        def rows(i):
            at = pl.ds(pl.multiple_of(i * tile, tile), tile)
            cols = slice(r * width, (r + 1) * width)
            low = mm[at, cols].astype(F32)
            mm[at, cols] = (low * (dm[r, at, :] - col)).astype(BF16)

        loop(c_rows // tile, rows)
        put_logits(r).start()

    def take_pred(i):
        wait(gpr.at[i], o["gp_r"].at[i])
        wait(gps.at[i], o["gq_r"].at[i])

        def rows(r):
            gpb[i, r] = (gpr[i, r].astype(I32).astype(F32) * gps[i, r]).astype(BF16)

        loop(t_rows, rows)
        put_pred(i).start()

    behind = BEHIND * t_rows
    lag = jnp.where(owner, behind, LAG_BACK * jnp.maximum(cz - 1, n - 2 - cz))

    def produce(k, piece):
        @pl.when(piece == 0)
        def _():
            diff_outer(k)

        @pl.when((piece == 1) & (k + 1 < nb))
        def _():
            diff_inside(k + 1)

        @pl.when((piece == 2) & (k + 1 < nb))
        def _():
            diff_inner(k + 1)

        @pl.when((piece == 1) & (k + 1 == nb))
        def _():
            send_last()

    def drain():
        loop(n - 1, lambda j: wait(srow.at[cz], o["s_s"].at[j]))

        def sent(d):
            own, end = cz == d * (n - 1), cz == (1 - d) * (n - 1)

            @pl.when(jnp.logical_not(own))
            def _():
                def each(q):
                    k, r = div(q, t_rows), rem(q, t_rows)
                    wait(ab.at[d, k, r], o["a_s"].at[d, k, r])
                    wait(sc.at[d, k, r], o["c_s"].at[d, k, r])

                loop(nb * t_rows, each)

            @pl.when(jnp.logical_not(end))
            def _():
                def each(q):
                    k, r = div(q, t_rows), rem(q, t_rows)
                    wait(dd.at[d, k, r], o["d_s"].at[d, k, r])

                loop(nb * t_rows, each)
                wait(fm.at[d], o["f_s"].at[d])

        loop(2, sent)

        @pl.when(owner)
        def _():
            for i in range(wb):
                def each(j, i=i):
                    for copy in pred_copies(i, j):
                        copy.wait_send()

                loop(n // 2 - 1, each)
            for slot, ok, _ in coef_routes():
                @pl.when(ok)
                def _(slot=slot):
                    wait(con, o["co_s"].at[slot])

            def each(k):
                for side, ok, row, _ in halo_routes():
                    @pl.when(ok)
                    def _(side=side, row=row):
                        wait(ab.at[od, k, row], o["hg_s"].at[side, k])
                        wait(sc.at[od, k, row], o["hs_s"].at[side, k])
                        wait(hq.at[side, k], o["hd_s"].at[side, k])

                for which in range(3):
                    wait(es.at[which, k], o["e_s"].at[which, k])

            loop(nb, each)
            wait(spx.at[0], o["x_s"].at[0])

            def each_peer(j):
                for part, at in enumerate(gene_parts):
                    wait(gs.at[at], o["g_s"].at[part, j])
                wait(spr.at[here], o["p_s"].at[j])

            loop(nplane - 1, each_peer)

    def back_step(s):
        for i in range(wb):
            @pl.when(owner & (s == 2 * i + 1))
            def _(i=i):
                put_own(i)

        @pl.when(owner & (s < nb * t_rows))
        def _():
            produce(div(s, t_rows), rem(s, t_rows))

        def direction(d):
            own, end = cz == d * (n - 1), cz == (1 - d) * (n - 1)
            off = jnp.where(owner, behind, LAG_BACK * jnp.where(d == 0, cz - 1, n - 2 - cz))
            q = s - off
            to = (sx, sy, cz + 1 - 2 * d)

            @pl.when(jnp.logical_not(own) & (q >= 0) & (q < nb * t_rows))
            def _():
                k, r = back_chunk(q)
                at = dd.at[d, k, r]
                wait(at, o["d_r"].at[d, k, r])

                @pl.when(jnp.logical_not(end))
                def _():
                    remote(at, at, o["d_s"].at[d, k, r], o["d_r"].at[d, k, r], to).start()

            @pl.when(jnp.logical_not(own) & (q == nb * t_rows + 2))
            def _():
                wait(fm.at[d], o["f_r"].at[d])

                @pl.when(jnp.logical_not(end))
                def _():
                    remote(fm.at[d], fm.at[d], o["f_s"].at[d], o["f_r"].at[d], to).start()

        loop(2, direction)
        q = s - lag

        @pl.when((q >= 0) & (q < nb * t_rows))
        def _():
            add_map(*back_chunk(q))

        w = q - t_rows
        k, piece = div(w, t_rows), rem(w, t_rows)

        @pl.when((w >= 0) & (k < nb))
        def _():
            @pl.when(piece == 0)
            def _():
                multiply(k)

        @pl.when((w >= 0) & (k == nb))
        def _():
            for r in range(t_rows):
                @pl.when(piece == r)
                def _(r=r):
                    finish(r)

        for stage, back_by, at in ((scatter_1, 0, 2), (scatter_2, 1, 2), (scatter_3, 2, 2)):
            @pl.when((w >= 0) & (piece == at) & (k >= back_by) & (k < nb + back_by))
            def _(stage=stage, back_by=back_by):
                stage(k - back_by)

        @pl.when(w == nb * t_rows + t_rows - 1)
        def _():
            drain()

        @pl.when((w == (nb + 1) * t_rows) & jnp.logical_not(owner))
        def _():
            for i in range(wb):
                take_pred(i)

    loop(t_rows * (nb + 4) + max(LAG_BACK * lead, behind), back_step)

    losses[0] = jnp.max(fm[0, 1, 0:1, :] + fm[1, 1, 0:1, :]) * -0.5
    losses[1] = jnp.max(fm[0, 1, 1:2, :]) * (-1.0 / all_spots)

    for r in range(t_rows):
        put_logits(r).wait()
    for i in range(bpg):
        put_cells(i).wait()

    for i in range(wb):
        put_pred(i).wait()


def cells_first(x, out):
    for r in range(x.shape[0]):
        out[:, r, :] = x[r].astype(F32)


def per_device(logits, cells_expr, spatial, gene_mask, slide_id, edge_weight, edge_mask):
    c_rows, t_rows, width = logits.shape
    genes = cells_expr.shape[1]
    n, nsx, nsy = (lax.axis_size(a) for a in ("cells", "sx", "sy"))
    spots = t_rows * width
    share = genes // n
    wide = max(share, LANES)
    wb = wide // LANES
    nb = genes // 2 // LANES
    nplane = nsx * nsy
    grid = (t_rows, width, LANES)
    vm, dma = pltpu.VMEM, pltpu.SemaphoreType.DMA
    scratch = dict(
        xs=vm((2 * nb, c_rows, LANES), BF16),
        mm=vm((c_rows, spots), BF16),
        mt=vm((t_rows, width, c_rows), BF16),
        dm=vm((t_rows, c_rows, width), F32),
        srow=vm((n, spots // LANES, LANES), F32),
        ab=vm((2, nb, *grid), I16),
        sc=vm((2, nb, t_rows, 1, LANES), F32),
        tt=vm((t_rows, 4 * width, 2 * LANES), F32),
        gg=vm((nb, *grid), F32),
        sm=vm((nb, *grid), F32),
        sp=vm((nb, *grid), F32),
        pad=vm((2, t_rows + 2, width + 16, LANES), F32),
        hg=vm((2, nb, width, LANES), I16),
        hs=vm((2, nb, 1, LANES), F32),
        hd=vm((2, nb, width, LANES), BF16),
        hq=vm((2, nb, width, LANES), BF16),
        es=vm((3, nb, 8, LANES), F32),
        er=vm((3, nb, 8, LANES), F32),
        cf=vm((6, *grid), F32),
        cb=vm((6, *grid), BF16),
        hot=vm(grid, F32),
        con=vm((t_rows, 8, width), F32),
        cor=vm((5, t_rows, 8, width), F32),
        acc=vm((3, *grid), F32),
        gs=vm((nb, 8, LANES), F32),
        gr=vm((nplane, nb, 8, LANES), F32),
        spx=vm((2, 3, spots // LANES, LANES), F32),
        gc=vm((nb, 8, LANES), F32),
        spr=vm((nplane, 8, LANES), F32),
        dd=vm((2, nb, *grid), BF16),
        fm=vm((2, 2, 8, LANES), F32),
        pss=vm((2, 2, c_rows, LANES), BF16),
        rs1=vm((2, nb // 2, c_rows, LANES), BF16),
        rs2=vm((nb // 2, c_rows, LANES), BF16),
        rs3=vm((nb // 4, c_rows, LANES), BF16),
        dcv=vm((nb // 4, c_rows, LANES), BF16),
        gpr=vm((wb, *grid), I16),
        gps=vm((wb, t_rows, 1, LANES), F32),
        gpb=vm((wb, *grid), BF16),
        lg_m=dma((t_rows,)),
        xs_m=dma((2 * nb,)),
        sp_m=dma((nb,)),
        s_s=dma((n,)),
        s_r=dma((n,)),
        a_s=dma((2, nb, t_rows)),
        a_r=dma((2, nb, t_rows)),
        c_s=dma((2, nb, t_rows)),
        c_r=dma((2, nb, t_rows)),
        hg_s=dma((2, nb)),
        hg_r=dma((2, nb)),
        hs_s=dma((2, nb)),
        hs_r=dma((2, nb)),
        hd_s=dma((2, nb)),
        hd_r=dma((2, nb)),
        e_s=dma((3, nb)),
        e_r=dma((3, nb)),
        co_s=dma((5,)),
        co_r=dma((5,)),
        g_s=dma((2, nplane)),
        g_r=dma((2, nplane)),
        p_s=dma((nplane,)),
        p_r=dma((nplane,)),
        x_s=dma((1,)),
        x_r=dma((1,)),
        d_s=dma((2, nb, t_rows)),
        d_r=dma((2, nb, t_rows)),
        f_s=dma((2,)),
        f_r=dma((2,)),
        r1_s=dma((2, nb // 2, 2)),
        r1_r=dma((2, nb // 2, 2)),
        r2_s=dma((2, nb // 2)),
        r2_r=dma((2, nb // 2)),
        r3_s=dma((2, nb // 4)),
        r3_r=dma((2, nb // 4)),
        gp_s=dma((max(n // 2 - 1, 1), wb)),
        gp_r=dma((wb,)),
        gq_s=dma((max(n // 2 - 1, 1), wb)),
        gq_r=dma((wb,)),
        gp_m=dma((wb,)),
        dl_m=dma((t_rows,)),
        dc_m=dma((nb // 4,)),
    )
    names = ("lg", "cells", "spat", "gmask", "slide", "ew", "em", "losses", "gp", "dlog", "dcell")
    names += tuple(scratch)
    sizes = (n, nsx, nsy, share, spots * nplane)
    anywhere, local = pl.BlockSpec(memory_space=pl.ANY), pl.BlockSpec(memory_space=pltpu.VMEM)
    losses, pred, d_logits, d_cells = pl.pallas_call(
        functools.partial(kernel, names, sizes),
        out_shape=(
            jax.ShapeDtypeStruct((2,), F32),
            jax.ShapeDtypeStruct((t_rows, width, wide), BF16),
            jax.ShapeDtypeStruct((t_rows, c_rows, width), BF16),
            jax.ShapeDtypeStruct((c_rows, genes // nplane), BF16),
        ),
        in_specs=[anywhere] * 3 + [local] * 4,
        out_specs=(pl.BlockSpec(memory_space=pltpu.SMEM), anywhere, anywhere, anywhere),
        scratch_shapes=list(scratch.values()),
        compiler_params=pltpu.CompilerParams(
            collective_id=0, has_side_effects=True, vmem_limit_bytes=VMEM
        ),
        cost_estimate=pl.CostEstimate(
            flops=6 * c_rows * spots * genes, bytes_accessed=32 << 20, transcendentals=c_rows * spots
        ),
    )(logits, cells_expr, spatial, gene_mask, slide_id, edge_weight, edge_mask)
    if wide > share:
        pred = lax.dynamic_slice_in_dim(pred, rem(lax.axis_index("cells") * share, wide), share, 2)
    tile = c_rows // 2 if c_rows % 64 == 0 else c_rows
    d_logits = pl.pallas_call(
        cells_first,
        grid=(c_rows // tile,),
        out_shape=jax.ShapeDtypeStruct(logits.shape, F32),
        in_specs=[pl.BlockSpec((t_rows, tile, width), lambda i: (0, i, 0))],
        out_specs=pl.BlockSpec((tile, t_rows, width), lambda i: (i, 0, 0)),
        compiler_params=pltpu.CompilerParams(vmem_limit_bytes=60 * 1024 * 1024),
    )(d_logits)
    return (losses, pred.astype(F32), d_logits, d_cells.astype(F32))


BEHIND = 3
LAG_SUM = 3
LAG_BACK = 3
VMEM = 64 * 1024 * 1024 - 512 * 1024


def solution(mesh):
    return jax.shard_map(
        per_device,
        mesh=mesh,
        in_specs=(
            P("cells", "sx", "sy"),
            P("cells", None),
            P("sx", "sy", None),
            P(),
            P("sx", "sy"),
            P(None, "sx", "sy"),
            P(None, "sx", "sy"),
        ),
        out_specs=(P(), P("sx", "sy", "cells"), P("cells", "sx", "sy"), P("cells", ("sx", "sy"))),
        check_vma=False,
    )
```

```python
import functools

import jax
import jax.numpy as jnp
from jax import lax
from jax.experimental import pallas as pl
from jax.experimental.pallas import tpu as pltpu
from jax.sharding import PartitionSpec as P

EPS = 1e-06
OFFSETS = ((0, 1), (0, -1), (1, 0), (-1, 0), (-1, 1), (1, -1))
LANES = 128
TOP = 32767.0
MESH = pl.DeviceIdType.MESH
F32, BF16, I16, I32 = jnp.float32, jnp.bfloat16, jnp.int16, jnp.int32
rem, div = lax.rem, lax.div


def loop(count, body):
    lax.fori_loop(0, count, lambda i, _: (body(i), 0)[1], 0)


def remote(src, dst, sent, got, to):
    return pltpu.make_async_remote_copy(
        src_ref=src, dst_ref=dst, send_sem=sent, recv_sem=got, device_id=to, device_id_type=MESH
    )


def wait(ref, sem):
    pltpu.make_async_copy(ref, ref, sem).wait()


def spread(row):
    parts = [
        jnp.broadcast_to(row[:, at : at + LANES], (LANES, LANES)).T
        for at in range(0, row.shape[1], LANES)
    ]
    return jnp.concatenate(parts, axis=0)


def fold(x):
    return jnp.sum(x.reshape(x.shape[0] // 8, 8, x.shape[1]), axis=0)


def kernel(names, sizes, *refs):
    n, nsx, nsy, share, all_spots = sizes
    o = dict(zip(names, refs, strict=True))
    lg, cells, spat, gmask, slide, ew, em = (o[k] for k in names[:7])
    losses, gp, dlog, dcell = (o[k] for k in names[7:11])
    xs, mm, mt, dm, srow, ab, sc, tt = (o[k] for k in names[11:19])
    gg, sm, sp, pad, hg, hs, hd, hq = (o[k] for k in names[19:27])
    es, er, cf, cb, hot, con, cor, acc = (o[k] for k in names[27:35])
    gs, gr, spx, gc, spr, dd, fm = (o[k] for k in names[35:42])
    pss, rs1, rs2, rs3, dcv, gpr, gps, gpb = (o[k] for k in names[42:50])

    c_rows, t_rows, width = lg.shape
    spots = t_rows * width
    nb = cells.shape[1] // 2 // LANES
    wl = width // LANES
    wb = gpr.shape[0]
    nplane = nsx * nsy
    half = nb // 2
    bpg = nb // 4
    tile = LANES
    tiles = c_rows // tile
    quarter = c_rows // 4
    sub = min(64, width)
    mid = slice(8, 8 + width)

    sx, sy, cz = (lax.axis_index(a) for a in ("sx", "sy", "cells"))
    here = sx * nsy + sy
    owner = (cz == 0) | (cz == n - 1)
    od = jnp.where(cz == 0, 0, 1)
    up, down = sx > 0, sx < nsx - 1
    mate = (sx, 1 - sy, cz)

    def gene_block(d, k):
        return jnp.where(d == 0, rem(k + half, nb), nb + k)

    for r in range(t_rows):
        pltpu.make_async_copy(lg.at[:, r, :], dm.at[r], o["lg_m"].at[r]).start()

    def load_cells(b):
        at = pl.ds(pl.multiple_of(b * LANES, LANES), LANES)
        return pltpu.make_async_copy(cells.at[:, at], xs.at[b], o["xs_m"].at[b])

    loop(2 * nb, lambda b: load_cells(b).start())

    def load_truth(k):
        at = pl.ds(pl.multiple_of(gene_block(od, k) * LANES, LANES), LANES)
        return pltpu.make_async_copy(spat.at[:, :, at], sp.at[k], o["sp_m"].at[k])

    @pl.when(owner)
    def _():
        loop(nb, lambda k: load_truth(k).start())

    barrier = pltpu.get_barrier_semaphore()

    def greet_line(j):
        to = (sx, sy, rem(cz + j + 1, n))
        pl.semaphore_signal(barrier, inc=1, device_id=to, device_id_type=MESH)

    def greet_plane(j):
        t = rem(here + j + 1, nplane)
        to = (div(t, nsy), rem(t, nsy), cz)
        pl.semaphore_signal(barrier, inc=1, device_id=to, device_id_type=MESH)

    loop(n - 1, greet_line)
    loop(nplane - 1, greet_plane)

    for r in range(t_rows):
        pltpu.make_async_copy(lg.at[:, r, :], dm.at[r], o["lg_m"].at[r]).wait()

        def exps(i, s, r=r):
            at = pl.ds(i * tile, tile)
            x = jnp.exp(dm[r, at, :])
            dm[r, at, :] = x
            return s + fold(x)

        s = lax.fori_loop(0, c_rows // tile, exps, jnp.zeros((8, width), F32))
        s = jnp.sum(s, axis=0, keepdims=True)
        for h in range(wl):
            srow[cz, pl.ds(r * wl + h, 1), :] = s[:, h * LANES : (h + 1) * LANES]

    pl.semaphore_wait(barrier, n - 1 + nplane - 1)

    def send_sums(j):
        to = (sx, sy, rem(cz + j + 1, n))
        remote(srow.at[cz], srow.at[cz], o["s_s"].at[j], o["s_r"].at[cz], to).start()

    loop(n - 1, send_sums)

    def turn(dst, first):
        def each(i):
            for r in range(t_rows):
                at = pl.ds(pl.multiple_of((i + first) * LANES, LANES), LANES)
                dst[i, r] = dm[r, at, :].T

        return each

    turned = ((gg, 0, min(tiles, nb)), (sm, nb, max(tiles - nb, 0)))
    for dst, first, count in turned:
        loop(count, turn(dst, first))

    def wait_sums(j):
        z = rem(cz + j + 1, n)
        wait(srow.at[z], o["s_r"].at[z])

    loop(n - 1, wait_sums)
    total = srow[0]
    for z in range(1, n):
        total = total + srow[z]
    inv = 1.0 / total
    inv_rows = [
        jnp.concatenate([inv[r * wl + h : r * wl + h + 1] for h in range(wl)], axis=1)
        for r in range(t_rows)
    ]
    for r in range(t_rows):
        acc[0, r] = spread(inv_rows[r])

    for dst, first, count in turned:
        def scale(i, dst=dst, first=first):
            at = pl.ds(pl.multiple_of((i + first) * LANES, LANES), LANES)
            for r in range(t_rows):
                mt[r, :, at] = (dst[i, r] * acc[0, r]).astype(BF16)

        loop(count, scale)

    def keep_mapping():
        for r in range(t_rows):
            def each(i, r=r):
                at = pl.ds(pl.multiple_of(i * LANES, LANES), LANES)
                mm[at, r * width : (r + 1) * width] = (dm[r, at, :] * inv_rows[r]).astype(BF16)

            loop(tiles, each)

    loop(2 * nb, lambda b: load_cells(b).wait())

    def coef_routes():
        return (
            (0, down, (sx + 1, sy, cz)),
            (1, up, (sx - 1, sy, cz)),
            (2, sx >= 0, mate),
            (3, down, (sx + 1, 1 - sy, cz)),
            (4, up, (sx - 1, 1 - sy, cz)),
        )


    def predict(d, pair, r):
        g = gene_block(d, 2 * pair)
        w = jnp.concatenate([xs[g], xs[g + 1]], axis=1)
        at = pl.ds(pl.multiple_of((2 * d + rem(pair, 2)) * width, 8), width)
        tt[r, at, :] = jnp.dot(mt[r], w, preferred_element_type=F32)

    def predicted(d, k, r):
        at = pl.ds(pl.multiple_of((2 * d + rem(div(k, 2), 2)) * width, 8), width)
        return tt[r, at, pl.ds(pl.multiple_of(rem(k, 2) * LANES, LANES), LANES)]

    def put(d, k, r, t):
        top = jnp.maximum(jnp.max(jnp.abs(t), axis=0, keepdims=True), 1e-30)
        ab[d, k, r] = jnp.round(t * (TOP / top)).astype(I32).astype(I16)
        sc[d, k, r] = top * (1.0 / TOP)

    def pass_on(d, k, r):
        to = (sx, sy, cz + 2 * d - 1)
        remote(ab.at[d, k, r], ab.at[d, k, r], o["a_s"].at[d, k, r], o["a_r"].at[d, k, r], to).start()
        remote(sc.at[d, k, r], sc.at[d, k, r], o["c_s"].at[d, k, r], o["c_r"].at[d, k, r], to).start()

    def chunk_of(q):
        return div(q, t_rows), rem(rem(q, t_rows) * (t_rows - 1), t_rows)

    @pl.when(owner)
    def _():
        d = 1 - od

        def first(q):
            k, r = chunk_of(q)

            @pl.when(rem(k, 2) == 0)
            def _():
                predict(d, div(k, 2), r)

            put(d, k, r, predicted(d, k, r))
            pass_on(d, k, r)

        loop(nb * t_rows, first)

        for r in range(t_rows):
            rows = [ew[j, r : r + 1, :] * em[j, r : r + 1, :].astype(F32) for j in range(6)]
            con[r] = jnp.concatenate(rows + [jnp.zeros((2, width), F32)], axis=0)
            for j in range(6):
                cf[j, r] = spread(rows[j])
            hot[r] = spread(slide[r : r + 1, :].astype(F32))
        acc[...] = jnp.zeros(acc.shape, F32)

        for slot, ok, to in coef_routes():
            @pl.when(ok)
            def _(slot=slot, to=to):
                remote(con, cor.at[slot], o["co_s"].at[slot], o["co_r"].at[slot], to).start()

        loop(nb, lambda k: load_truth(k).wait())

    def back_coefs():
        for slot, ok in ((0, up), (1, down), (2, sx >= 0), (3, up), (4, down)):
            @pl.when(ok)
            def _(slot=slot):
                wait(cor.at[slot], o["co_r"].at[slot])

        lane = lax.broadcasted_iota(I32, (8, width), 1)
        for j, (dr, dc) in enumerate(OFFSETS):
            for r in range(t_rows):
                at = r - dr
                if at < 0:
                    base, side, ok = cor[0, t_rows - 1], cor[3, t_rows - 1], up
                elif at >= t_rows:
                    base, side, ok = cor[1, 0], cor[4, 0], down
                else:
                    base, side, ok = con[at], cor[2, at], sx >= 0
                base = jnp.where(ok, base, 0.0)
                if dc:
                    by, edge = (1, 0) if dc == 1 else (width - 1, width - 1)
                    side = jnp.where(ok & (sy == (1 if dc == 1 else 0)), side, 0.0)
                    base = jnp.where(lane == edge, pltpu.roll(side, by, 1), pltpu.roll(base, by, 1))
                cb[j, r] = spread(base[j : j + 1]).astype(BF16)

    def send_edges(slot, which, k, rows):
        parts = [
            jnp.where(sy == 1, pad[slot, row, 8:9, :], pad[slot, row, 7 + width : 8 + width, :])
            for row in rows
        ]
        parts.append(jnp.zeros((8 - len(parts), LANES), F32))
        es[which, k] = jnp.concatenate(parts, axis=0)
        remote(es.at[which, k], er.at[which, k], o["e_s"].at[which, k], o["e_r"].at[which, k], mate).start()

    def take_edges(slot, which, k, rows):
        wait(er.at[which, k], o["e_r"].at[which, k])
        for i, row in enumerate(rows):
            edge = er[which, k, i : i + 1, :]
            pad[slot, row, 8 + width : 9 + width, :] = jnp.where(sy == 0, edge, 0.0)
            pad[slot, row, 7:8, :] = jnp.where(sy == 1, edge, 0.0)

    sides = ((0, up, 0), (1, down, t_rows + 1))

    def prepare(k):
        for side, ok, row in sides:
            @pl.when(ok)
            def _(side=side, row=row):
                wait(hg.at[side, k], o["hg_r"].at[side, k])
                wait(hs.at[side, k], o["hs_r"].at[side, k])
                pad[0, row, mid, :] = hg[side, k].astype(I32).astype(F32) * hs[side, k]

            @pl.when(jnp.logical_not(ok))
            def _(row=row):
                pad[0, row, mid, :] = jnp.zeros((width, LANES), F32)

        def rows(r):
            pad[0, r + 1, mid, :] = gg[k, r]

        loop(t_rows, rows)
        send_edges(0, 0, k, range(t_rows + 2))

    def smoothing(k):
        take_edges(0, 0, k, range(t_rows + 2))
        at = pl.ds(pl.multiple_of(gene_block(od, k) * LANES, LANES), LANES)
        mask = gmask[:, at].astype(F32)
        m0, m1 = mask[0:1], mask[1:2]

        def rows(r, sums):
            sums = list(sums)
            for u in range(0, width, sub):
                here_u = slice(u, u + sub)
                a = pad[0, r + 1, 8 + u : 8 + u + sub, :]
                for j, (dr, dc) in enumerate(OFFSETS):
                    a = a + cf[j, r, here_u, :] * pad[0, r + 1 + dr, 8 + dc + u : 8 + dc + u + sub, :]
                sm[k, r, here_u, :] = a
                t = sp[k, r, here_u, :]
                h = hot[r, here_u, :]
                mk = m0 + h * (m1 - m0)
                for i, x in enumerate((a * t, a * a, t * t)):
                    sums[2 * i] = sums[2 * i] + fold(x)
                    sums[2 * i + 1] = sums[2 * i + 1] + fold(x * h)
                    acc[i, r, here_u, :] = acc[i, r, here_u, :] + x * mk
            return tuple(sums)

        sums = lax.fori_loop(0, t_rows, rows, (jnp.zeros((8, LANES), F32),) * 6)
        parts = []
        for i in range(3):
            both = jnp.sum(sums[2 * i], axis=0, keepdims=True)
            one = jnp.sum(sums[2 * i + 1], axis=0, keepdims=True)
            parts += [both - one, one]
        gs[k] = jnp.concatenate(parts + [jnp.zeros((2, LANES), F32)], axis=0)

    def own_block(t, i):
        b = div(t * share, LANES) + i - od * nb
        return jnp.where(od == 0, rem(b + half, nb), b)

    def pred_copies(i, j):
        t = jnp.where(od == 0, j + 1, n - 2 - j)
        k = own_block(t, i)
        to = (sx, sy, t)
        return (
            remote(ab.at[od, k], gpr.at[i], o["gp_s"].at[j, i], o["gp_r"].at[i], to),
            remote(sc.at[od, k], gps.at[i], o["gq_s"].at[j, i], o["gq_r"].at[i], to),
        )

    def send_pred(i):
        def each(j):
            for copy in pred_copies(i, j):
                copy.start()

        loop(n // 2 - 1, each)

    early_pred = 2 if n == 4 else 0

    def plane_peer(j):
        t = rem(here + j + 1, nplane)
        return t, (div(t, nsy), rem(t, nsy), cz)

    gene_parts = (pl.ds(0, nb - 1), pl.ds(nb - 1, 1))

    def send_genes(part):
        at = gene_parts[part]

        def each(j):
            _, to = plane_peer(j)
            sems = o["g_s"].at[part, j], o["g_r"].at[part, here]
            remote(gs.at[at], gr.at[here, at], *sems, to).start()

        loop(nplane - 1, each)

    lead = max(n - 3, 0)

    def sum_step(s):
        def direction(d):
            own, first = cz == d * (n - 1), cz == (1 - d) * (n - 1)
            off = jnp.where(owner, 0, LAG_SUM * jnp.where(d == 1, cz - 1, n - 2 - cz))
            q = s - off

            @pl.when(jnp.logical_not(first) & (q >= 0) & (q < nb * t_rows))
            def _():
                k, r = chunk_of(q)
                wait(ab.at[d, k, r], o["a_r"].at[d, k, r])
                wait(sc.at[d, k, r], o["c_r"].at[d, k, r])
                got = ab[d, k, r].astype(I32).astype(F32) * sc[d, k, r]
                t = predicted(d, k, r) + got
                put(d, k, r, t)

                @pl.when(jnp.logical_not(own))
                def _():
                    pass_on(d, k, r)

                @pl.when(own)
                def _():
                    gg[k, r] = t
                    for side, ok, row, to in halo_routes():
                        @pl.when(ok & (r == row))
                        def _(side=side, row=row, to=to):
                            remote(ab.at[d, k, row], hg.at[side, k], o["hg_s"].at[side, k], o["hg_r"].at[side, k], to).start()
                            remote(sc.at[d, k, row], hs.at[side, k], o["hs_s"].at[side, k], o["hs_r"].at[side, k], to).start()

                    i = rem(q, t_rows)

                    @pl.when((k > 0) & (i == 1))
                    def _():
                        prepare(k - 1)

                    @pl.when((k > 0) & (i == t_rows - 1))
                    def _():
                        smoothing(k - 1)

                    @pl.when((k == nb - 1) & (i == t_rows - 1))
                    def _():
                        send_genes(0)

                    if early_pred:
                        @pl.when(q == 3 * nb * t_rows // 4)
                        def _():
                            for i in range(early_pred):
                                send_pred(i)

                @pl.when((rem(k, 2) == d) & (k + 2 - rem(k, 2) < nb))
                def _():
                    predict(d, div(k, 2) + 1, r)

        turn = cz - 1 > n - 2 - cz
        loop(2, lambda i: direction(jnp.where(turn, 1 - i, i)))

        @pl.when(owner & (s == half * t_rows))
        def _():
            back_coefs()

    def halo_routes():
        return ((1, up, 0, (sx - 1, sy, cz)), (0, down, t_rows - 1, (sx + 1, sy, cz)))

    def first_block(d):
        @pl.when(cz != (1 - d) * (n - 1))
        def _():
            loop(t_rows, lambda r: predict(d, 0, r))

    loop(2, first_block)
    keep_mapping()
    loop(nb * t_rows + LAG_SUM * lead, sum_step)

    def diff_smooth(k, r, at):
        tc0, tc1, sc0, sc1, m0, m1 = (gc[k, i : i + 1, :] for i in range(6))
        h = hot[r, at, :]
        mk = m0 + h * (m1 - m0)
        by_truth = tc0 + h * (tc1 - tc0) + mk * acc[1, r, at, :]
        by_smooth = sc0 + h * (sc1 - sc0) + mk * acc[2, r, at, :]
        return by_truth * sp[k, r, at, :] + by_smooth * sm[k, r, at, :]

    def send_borders(k):
        for side, ok, row, to in halo_routes():
            @pl.when(ok)
            def _(side=side, row=row, to=to):
                for u in range(0, width, sub):
                    hq[side, k, u : u + sub, :] = diff_smooth(k, row, slice(u, u + sub)).astype(BF16)
                remote(hq.at[side, k], hd.at[side, k], o["hd_s"].at[side, k], o["hd_r"].at[side, k], to).start()

    def diff_inside(k):
        slot = rem(k, 2)

        def rows(r):
            for u in range(0, width, sub):
                pad[slot, r + 1, 8 + u : 8 + u + sub, :] = diff_smooth(k, r, slice(u, u + sub))

        loop(t_rows, rows)
        send_edges(slot, 1, k, range(1, t_rows + 1))

    def diff_border(k):
        slot = rem(k, 2)
        for side, ok, row in sides:
            @pl.when(ok)
            def _(side=side, row=row):
                wait(hd.at[side, k], o["hd_r"].at[side, k])
                pad[slot, row, mid, :] = hd[side, k].astype(F32)

            @pl.when(jnp.logical_not(ok))
            def _(row=row):
                pad[slot, row, mid, :] = jnp.zeros((width, LANES), F32)

        send_edges(slot, 2, k, (0, t_rows + 1))

    back = cz + 1 - 2 * od

    def diff_pred(k, rows):
        slot = rem(k, 2)
        for r in rows:
            for u in range(0, width, sub):
                here_u = slice(u, u + sub)
                a = pad[slot, r + 1, 8 + u : 8 + u + sub, :]
                for j, (dr, dc) in enumerate(OFFSETS):
                    w = cb[j, r, here_u, :].astype(F32)
                    a = a + w * pad[slot, r + 1 - dr, 8 - dc + u : 8 - dc + u + sub, :]
                low = a.astype(BF16)
                dd[od, k, r, here_u, :] = low
                acc[0, r, here_u, :] = acc[0, r, here_u, :] + gg[k, r, here_u, :] * low.astype(F32)
            at = dd.at[od, k, r]
            remote(at, at, o["d_s"].at[od, k, r], o["d_r"].at[od, k, r], (sx, sy, back)).start()

    def back_chunk(q):
        i = rem(q, t_rows)
        return div(q, t_rows), jnp.where(i < t_rows - 2, i + 1, jnp.where(i == t_rows - 2, 0, i))

    def diff_inner(k):
        take_edges(rem(k, 2), 1, k, range(1, t_rows + 1))
        diff_pred(k, range(1, t_rows - 1))
        diff_border(k)

    def diff_outer(k):
        take_edges(rem(k, 2), 2, k, (0, t_rows + 1))
        diff_pred(k, (0, t_rows - 1))

    def spot_rows(i):
        return [
            jnp.sum(acc[i, r, h * LANES : (h + 1) * LANES, :].T, axis=0, keepdims=True)
            for r in range(t_rows)
            for h in range(wl)
        ]

    def put_pred(i):
        at = slice(i * LANES, (i + 1) * LANES)
        return pltpu.make_async_copy(gpb.at[i], gp.at[:, :, at], o["gp_m"].at[i])

    def put_own(i):
        k = own_block(cz, i)

        def rows(r):
            gpb[i, r] = gg[k, r].astype(BF16)

        loop(t_rows, rows)
        put_pred(i).start()

    @pl.when(owner)
    def _():
        prepare(nb - 1)
        smoothing(nb - 1)

        send_genes(1)
        for i in range(3):
            for at, row in enumerate(spot_rows(i)):
                spx[0, i, at : at + 1, :] = row
        remote(spx.at[0], spx.at[1], o["x_s"].at[0], o["x_r"].at[0], (sx, sy, n - 1 - cz)).start()
        gr[here] = gs[...]
        def wait_genes(j):
            t, _ = plane_peer(j)
            for part, at in enumerate(gene_parts):
                wait(gr.at[t, at], o["g_r"].at[part, t])

        loop(nplane - 1, wait_genes)
        count = jnp.maximum(jnp.sum(gmask[...].astype(F32), axis=1, keepdims=True), 1.0)

        def genes(k, gl):
            tot = gr[0, k]
            for t in range(1, nplane):
                tot = tot + gr[t, k]
            ib, ic = lax.rsqrt(tot[2:4] + EPS), lax.rsqrt(tot[4:6] + EPS)
            cos = tot[0:2] * ib * ic
            at = pl.ds(pl.multiple_of(gene_block(od, k) * LANES, LANES), LANES)
            mask = gmask[:, at].astype(F32)
            scale = -mask / (2.0 * count)
            gc[k, 0:2, :] = scale * ib * ic
            gc[k, 2:4, :] = -scale * cos * ib * ib
            gc[k, 4:6, :] = mask
            return gl + mask * cos / count

        gl = lax.fori_loop(0, nb, genes, jnp.zeros((2, LANES), F32))
        gene_part = jnp.sum(jnp.sum(gl, axis=0, keepdims=True), axis=1, keepdims=True)

        wait(spx.at[1], o["x_r"].at[0])
        a, b, c = (spx[0, i] + spx[1, i] for i in range(3))
        ib, ic = lax.rsqrt(b + EPS), lax.rsqrt(c + EPS)
        cos = a * ib * ic
        by_truth = (-1.0 / all_spots) * ib * ic
        by_smooth = (1.0 / all_spots) * cos * ib * ib
        for r in range(t_rows):
            for h in range(wl):
                at, i = slice(h * LANES, (h + 1) * LANES), r * wl + h
                acc[1, r, at, :] = spread(by_truth[i : i + 1])
                acc[2, r, at, :] = spread(by_smooth[i : i + 1])
        acc[0] = jnp.zeros(acc.shape[1:], F32)
        spot_part = jnp.sum(jnp.sum(cos, axis=0, keepdims=True), axis=1, keepdims=True)
        spr[here] = jnp.broadcast_to(spot_part, (8, LANES))
        fm[od, 1] = jnp.broadcast_to(gene_part, (8, LANES))

        def send_spot(j):
            _, to = plane_peer(j)
            remote(spr.at[here], spr.at[here], o["p_s"].at[j], o["p_r"].at[here], to).start()

        send_borders(0)
        diff_inside(0)
        send_borders(1)
        take_edges(0, 1, 0, range(1, t_rows + 1))
        diff_pred(0, range(1, t_rows - 1))
        loop(nb - 2, lambda k: send_borders(k + 2))
        loop(nplane - 1, send_spot)
        diff_border(0)

    def send_last():
        def wait_spot(j):
            t, _ = plane_peer(j)
            wait(spr.at[t], o["p_r"].at[t])

        loop(nplane - 1, wait_spot)
        spot_all = spr[0, 0:1, :]
        for t in range(1, nplane):
            spot_all = spot_all + spr[t, 0:1, :]
        rows = spot_rows(0)
        if len(rows) < 8:
            rows.append(jnp.zeros((8 - len(rows), LANES), F32))
        fm[od, 0] = jnp.concatenate(rows, axis=0)
        fm[od, 1, 1:2, :] = spot_all
        remote(fm.at[od], fm.at[od], o["f_s"].at[od], o["f_r"].at[od], (sx, sy, back)).start()
        for i in range(early_pred, wb):
            send_pred(i)


    sy_bit, sx_bit = div(sx, 2), rem(sx, 2)
    over_y, over_x = (sx + 2 - 4 * sy_bit, sy, cz), (sx + 1 - 2 * sx_bit, sy, cz)

    def place(k):
        jj = div(k, bpg)
        hi = div(jj, 2)
        return rem(jj, 2) == sy, hi * bpg + rem(k, bpg), jnp.where(sy_bit == 0, 1 - hi, hi) == sx_bit

    halves = (pl.ds(0, c_rows // 2), pl.ds(c_rows // 2, c_rows // 2))
    cuts = [pl.ds(i * quarter, quarter) for i in range(4)]

    def add_rows(dst, *terms):
        count = dst.shape[0] // 2

        def rows(i):
            at = pl.ds(pl.multiple_of(i * count, 8), count)
            dst[at, :] = sum(t[at, :].astype(F32) for t in terms).astype(dst.dtype)

        loop(2, rows)

    def multiply(k):
        mine, at, _ = place(k)
        slot = rem(k, 2)
        block = jnp.concatenate([dd[i, k].reshape(spots, LANES) for i in range(2)], axis=1)
        out = jnp.dot(mm[...], block, preferred_element_type=F32).astype(BF16)
        pss[slot, 0] = out[:, :LANES]
        pss[slot, 1] = out[:, LANES:]

        @pl.when(jnp.logical_not(mine))
        def _():
            for h, half in enumerate(halves):
                for d in range(2):
                    src, dst = pss.at[slot, d, half], rs1.at[d, at, half]
                    remote(src, dst, o["r1_s"].at[d, at, h], o["r1_r"].at[d, at, h], mate).start()

    def stays(final):
        return sy_bit, jnp.where(final, sy_bit, 1 - sy_bit)

    def scatter_1(k):
        mine, at, final = place(k)
        slot = rem(k, 2)

        @pl.when(mine)
        def _():
            for h, (stay, to) in enumerate(zip(stays(final), (over_y, over_x), strict=True)):
                d, half = 1 - stay, halves[h]
                wait(rs1.at[d, at, half], o["r1_r"].at[d, at, h])
                for i in (2 * h, 2 * h + 1):
                    src, sems = rs1.at[d, at, cuts[i]], (o["r2_s"].at[i, at], o["r2_r"].at[i, at])
                    add_rows(src, pss.at[slot, d, cuts[i]], src)
                    remote(src, rs2.at[at, cuts[i]], *sems, to).start()

        @pl.when(jnp.logical_not(mine))
        def _():
            for d in range(2):
                for h, half in enumerate(halves):
                    wait(pss.at[slot, d, half], o["r1_s"].at[d, at, h])

    def scatter_2(k):
        mine, at, final = place(k)
        slot = rem(k, 2)

        @pl.when(mine)
        def _():
            j = rem(k, bpg)
            for h, d in enumerate(stays(final)):
                wait(rs1.at[d, at, halves[h]], o["r1_r"].at[d, at, h])
            for i in (0, 2, 1, 3):
                h, cut = i // 2, cuts[i]
                d, to = stays(final)[h], (over_x, over_y)[h]
                part = rs2.at[at, cut]
                wait(part, o["r2_r"].at[i, at])
                add_rows(part, pss.at[slot, d, cut], rs1.at[d, at, cut], part)

                @pl.when(jnp.logical_not(final))
                def _(i=i, part=part, cut=cut, to=to):
                    remote(part, rs3.at[j, cut], o["r3_s"].at[i, j], o["r3_r"].at[i, j], to).start()

            for i in range(4):
                wait(rs1.at[1 - stays(final)[i // 2], at, cuts[i]], o["r2_s"].at[i, at])

    def put_cells(i):
        at = pl.ds(pl.multiple_of(i * LANES, LANES), LANES)
        return pltpu.make_async_copy(dcv.at[i], dcell.at[:, at], o["dc_m"].at[i])

    def scatter_3(k):
        mine, at, final = place(k)
        i = rem(k, bpg)

        @pl.when(mine & final)
        def _():
            for c in (0, 2, 1, 3):
                wait(rs3.at[i, cuts[c]], o["r3_r"].at[c, i])
                add_rows(dcv.at[i, cuts[c]], rs2.at[at, cuts[c]], rs3.at[i, cuts[c]])
            put_cells(i).start()

        @pl.when(mine & jnp.logical_not(final))
        def _():
            for c in range(4):
                wait(rs2.at[at, cuts[c]], o["r3_s"].at[c, i])

    def add_map(k, r):
        x = jnp.concatenate([xs[gene_block(0, k)], xs[gene_block(1, k)]], axis=1)
        d = jnp.concatenate([dd[0, k, r], dd[1, k, r]], axis=1)
        new = lax.dot_general(x, d, (((1,), (1,)), ((), ())), preferred_element_type=F32)
        dm[r] = jnp.where(k == 0, 0.0, dm[r]) + new

    def put_logits(r):
        return pltpu.make_async_copy(mm.at[:, r * width : (r + 1) * width], dlog.at[r], o["dl_m"].at[r])

    def finish(r):
        col = jnp.concatenate([fm[0, 0, i : i + 1] + fm[1, 0, i : i + 1] for i in range(r * wl, (r + 1) * wl)], axis=1)

        def rows(i):
            at = pl.ds(pl.multiple_of(i * tile, tile), tile)
            cols = slice(r * width, (r + 1) * width)
            low = mm[at, cols].astype(F32)
            mm[at, cols] = (low * (dm[r, at, :] - col)).astype(BF16)

        loop(c_rows // tile, rows)
        put_logits(r).start()

    def take_pred(i):
        wait(gpr.at[i], o["gp_r"].at[i])
        wait(gps.at[i], o["gq_r"].at[i])

        def rows(r):
            gpb[i, r] = (gpr[i, r].astype(I32).astype(F32) * gps[i, r]).astype(BF16)

        loop(t_rows, rows)
        put_pred(i).start()

    behind = BEHIND * t_rows
    lag = jnp.where(owner, behind, LAG_BACK * jnp.maximum(cz - 1, n - 2 - cz))

    def produce(k, piece):
        @pl.when(piece == 0)
        def _():
            diff_outer(k)

        @pl.when((piece == 1) & (k + 1 < nb))
        def _():
            diff_inside(k + 1)

        @pl.when((piece == 2) & (k + 1 < nb))
        def _():
            diff_inner(k + 1)

        @pl.when((piece == 1) & (k + 1 == nb))
        def _():
            send_last()

    def drain():
        loop(n - 1, lambda j: wait(srow.at[cz], o["s_s"].at[j]))

        def sent(d):
            own, end = cz == d * (n - 1), cz == (1 - d) * (n - 1)

            @pl.when(jnp.logical_not(own))
            def _():
                def each(q):
                    k, r = div(q, t_rows), rem(q, t_rows)
                    wait(ab.at[d, k, r], o["a_s"].at[d, k, r])
                    wait(sc.at[d, k, r], o["c_s"].at[d, k, r])

                loop(nb * t_rows, each)

            @pl.when(jnp.logical_not(end))
            def _():
                def each(q):
                    k, r = div(q, t_rows), rem(q, t_rows)
                    wait(dd.at[d, k, r], o["d_s"].at[d, k, r])

                loop(nb * t_rows, each)
                wait(fm.at[d], o["f_s"].at[d])

        loop(2, sent)

        @pl.when(owner)
        def _():
            for i in range(wb):
                def each(j, i=i):
                    for copy in pred_copies(i, j):
                        copy.wait_send()

                loop(n // 2 - 1, each)
            for slot, ok, _ in coef_routes():
                @pl.when(ok)
                def _(slot=slot):
                    wait(con, o["co_s"].at[slot])

            def each(k):
                for side, ok, row, _ in halo_routes():
                    @pl.when(ok)
                    def _(side=side, row=row):
                        wait(ab.at[od, k, row], o["hg_s"].at[side, k])
                        wait(sc.at[od, k, row], o["hs_s"].at[side, k])
                        wait(hq.at[side, k], o["hd_s"].at[side, k])

                for which in range(3):
                    wait(es.at[which, k], o["e_s"].at[which, k])

            loop(nb, each)
            wait(spx.at[0], o["x_s"].at[0])

            def each_peer(j):
                for part, at in enumerate(gene_parts):
                    wait(gs.at[at], o["g_s"].at[part, j])
                wait(spr.at[here], o["p_s"].at[j])

            loop(nplane - 1, each_peer)

    def back_step(s):
        for i in range(wb):
            @pl.when(owner & (s == 2 * i + 1))
            def _(i=i):
                put_own(i)

        @pl.when(owner & (s < nb * t_rows))
        def _():
            produce(div(s, t_rows), rem(s, t_rows))

        def direction(d):
            own, end = cz == d * (n - 1), cz == (1 - d) * (n - 1)
            off = jnp.where(owner, behind, LAG_BACK * jnp.where(d == 0, cz - 1, n - 2 - cz))
            q = s - off
            to = (sx, sy, cz + 1 - 2 * d)

            @pl.when(jnp.logical_not(own) & (q >= 0) & (q < nb * t_rows))
            def _():
                k, r = back_chunk(q)
                at = dd.at[d, k, r]
                wait(at, o["d_r"].at[d, k, r])

                @pl.when(jnp.logical_not(end))
                def _():
                    remote(at, at, o["d_s"].at[d, k, r], o["d_r"].at[d, k, r], to).start()

            @pl.when(jnp.logical_not(own) & (q == nb * t_rows + 2))
            def _():
                wait(fm.at[d], o["f_r"].at[d])

                @pl.when(jnp.logical_not(end))
                def _():
                    remote(fm.at[d], fm.at[d], o["f_s"].at[d], o["f_r"].at[d], to).start()

        turn = cz - 1 < n - 2 - cz
        loop(2, lambda i: direction(jnp.where(turn, 1 - i, i)))
        q = s - lag

        w = q - t_rows + 1
        k, piece = div(w, t_rows), rem(w, t_rows)

        @pl.when((w >= 0) & (k < nb) & (piece == 0))
        def _():
            multiply(k)

        @pl.when((q >= 0) & (q < nb * t_rows))
        def _():
            add_map(*back_chunk(q))

        @pl.when((w >= 0) & (k == nb))
        def _():
            for r in range(t_rows):
                @pl.when(piece == r)
                def _(r=r):
                    finish(r)

        for stage, back_by, at in ((scatter_1, 0, 2), (scatter_2, 1, 2), (scatter_3, 2, 2)):
            @pl.when((w >= 0) & (piece == at) & (k >= back_by) & (k < nb + back_by))
            def _(stage=stage, back_by=back_by):
                stage(k - back_by)

        @pl.when(w == nb * t_rows + t_rows - 1)
        def _():
            drain()

        @pl.when((w == (nb + 1) * t_rows) & jnp.logical_not(owner))
        def _():
            for i in range(wb):
                take_pred(i)

    loop(t_rows * (nb + 4) + max(LAG_BACK * lead, behind), back_step)

    losses[0] = jnp.max(fm[0, 1, 0:1, :] + fm[1, 1, 0:1, :]) * -0.5
    losses[1] = jnp.max(fm[0, 1, 1:2, :]) * (-1.0 / all_spots)

    for r in range(t_rows):
        put_logits(r).wait()
    for i in range(bpg):
        put_cells(i).wait()

    for i in range(wb):
        put_pred(i).wait()


def cells_first(x, out):
    for r in range(x.shape[0]):
        out[:, r, :] = x[r].astype(F32)


def per_device(logits, cells_expr, spatial, gene_mask, slide_id, edge_weight, edge_mask):
    c_rows, t_rows, width = logits.shape
    genes = cells_expr.shape[1]
    n, nsx, nsy = (lax.axis_size(a) for a in ("cells", "sx", "sy"))
    spots = t_rows * width
    share = genes // n
    wide = max(share, LANES)
    wb = wide // LANES
    nb = genes // 2 // LANES
    nplane = nsx * nsy
    grid = (t_rows, width, LANES)
    vm, dma = pltpu.VMEM, pltpu.SemaphoreType.DMA
    scratch = dict(
        xs=vm((2 * nb, c_rows, LANES), BF16),
        mm=vm((c_rows, spots), BF16),
        mt=vm((t_rows, width, c_rows), BF16),
        dm=vm((t_rows, c_rows, width), F32),
        srow=vm((n, spots // LANES, LANES), F32),
        ab=vm((2, nb, *grid), I16),
        sc=vm((2, nb, t_rows, 1, LANES), F32),
        tt=vm((t_rows, 4 * width, 2 * LANES), F32),
        gg=vm((nb, *grid), F32),
        sm=vm((nb, *grid), F32),
        sp=vm((nb, *grid), F32),
        pad=vm((2, t_rows + 2, width + 16, LANES), F32),
        hg=vm((2, nb, width, LANES), I16),
        hs=vm((2, nb, 1, LANES), F32),
        hd=vm((2, nb, width, LANES), BF16),
        hq=vm((2, nb, width, LANES), BF16),
        es=vm((3, nb, 8, LANES), F32),
        er=vm((3, nb, 8, LANES), F32),
        cf=vm((6, *grid), F32),
        cb=vm((6, *grid), BF16),
        hot=vm(grid, F32),
        con=vm((t_rows, 8, width), F32),
        cor=vm((5, t_rows, 8, width), F32),
        acc=vm((3, *grid), F32),
        gs=vm((nb, 8, LANES), F32),
        gr=vm((nplane, nb, 8, LANES), F32),
        spx=vm((2, 3, spots // LANES, LANES), F32),
        gc=vm((nb, 8, LANES), F32),
        spr=vm((nplane, 8, LANES), F32),
        dd=vm((2, nb, *grid), BF16),
        fm=vm((2, 2, 8, LANES), F32),
        pss=vm((2, 2, c_rows, LANES), BF16),
        rs1=vm((2, nb // 2, c_rows, LANES), BF16),
        rs2=vm((nb // 2, c_rows, LANES), BF16),
        rs3=vm((nb // 4, c_rows, LANES), BF16),
        dcv=vm((nb // 4, c_rows, LANES), BF16),
        gpr=vm((wb, *grid), I16),
        gps=vm((wb, t_rows, 1, LANES), F32),
        gpb=vm((wb, *grid), BF16),
        lg_m=dma((t_rows,)),
        xs_m=dma((2 * nb,)),
        sp_m=dma((nb,)),
        s_s=dma((n,)),
        s_r=dma((n,)),
        a_s=dma((2, nb, t_rows)),
        a_r=dma((2, nb, t_rows)),
        c_s=dma((2, nb, t_rows)),
        c_r=dma((2, nb, t_rows)),
        hg_s=dma((2, nb)),
        hg_r=dma((2, nb)),
        hs_s=dma((2, nb)),
        hs_r=dma((2, nb)),
        hd_s=dma((2, nb)),
        hd_r=dma((2, nb)),
        e_s=dma((3, nb)),
        e_r=dma((3, nb)),
        co_s=dma((5,)),
        co_r=dma((5,)),
        g_s=dma((2, nplane)),
        g_r=dma((2, nplane)),
        p_s=dma((nplane,)),
        p_r=dma((nplane,)),
        x_s=dma((1,)),
        x_r=dma((1,)),
        d_s=dma((2, nb, t_rows)),
        d_r=dma((2, nb, t_rows)),
        f_s=dma((2,)),
        f_r=dma((2,)),
        r1_s=dma((2, nb // 2, 2)),
        r1_r=dma((2, nb // 2, 2)),
        r2_s=dma((4, nb // 2)),
        r2_r=dma((4, nb // 2)),
        r3_s=dma((4, nb // 4)),
        r3_r=dma((4, nb // 4)),
        gp_s=dma((max(n // 2 - 1, 1), wb)),
        gp_r=dma((wb,)),
        gq_s=dma((max(n // 2 - 1, 1), wb)),
        gq_r=dma((wb,)),
        gp_m=dma((wb,)),
        dl_m=dma((t_rows,)),
        dc_m=dma((nb // 4,)),
    )
    names = ("lg", "cells", "spat", "gmask", "slide", "ew", "em", "losses", "gp", "dlog", "dcell")
    names += tuple(scratch)
    sizes = (n, nsx, nsy, share, spots * nplane)
    anywhere, local = pl.BlockSpec(memory_space=pl.ANY), pl.BlockSpec(memory_space=pltpu.VMEM)
    losses, pred, d_logits, d_cells = pl.pallas_call(
        functools.partial(kernel, names, sizes),
        out_shape=(
            jax.ShapeDtypeStruct((2,), F32),
            jax.ShapeDtypeStruct((t_rows, width, wide), BF16),
            jax.ShapeDtypeStruct((t_rows, c_rows, width), BF16),
            jax.ShapeDtypeStruct((c_rows, genes // nplane), BF16),
        ),
        in_specs=[anywhere] * 3 + [local] * 4,
        out_specs=(pl.BlockSpec(memory_space=pltpu.SMEM), anywhere, anywhere, anywhere),
        scratch_shapes=list(scratch.values()),
        compiler_params=pltpu.CompilerParams(
            collective_id=0, has_side_effects=True, vmem_limit_bytes=VMEM
        ),
        cost_estimate=pl.CostEstimate(
            flops=6 * c_rows * spots * genes, bytes_accessed=32 << 20, transcendentals=c_rows * spots
        ),
    )(logits, cells_expr, spatial, gene_mask, slide_id, edge_weight, edge_mask)
    if wide > share:
        pred = lax.dynamic_slice_in_dim(pred, rem(lax.axis_index("cells") * share, wide), share, 2)
    tile = c_rows // 2 if c_rows % 64 == 0 else c_rows
    d_logits = pl.pallas_call(
        cells_first,
        grid=(c_rows // tile,),
        out_shape=jax.ShapeDtypeStruct(logits.shape, F32),
        in_specs=[pl.BlockSpec((t_rows, tile, width), lambda i: (0, i, 0))],
        out_specs=pl.BlockSpec((tile, t_rows, width), lambda i: (i, 0, 0)),
        compiler_params=pltpu.CompilerParams(vmem_limit_bytes=60 * 1024 * 1024),
    )(d_logits)
    return (losses, pred.astype(F32), d_logits, d_cells.astype(F32))


BEHIND = 3
LAG_SUM = 3
LAG_BACK = 3
VMEM = 64 * 1024 * 1024 - 512 * 1024


def solution(mesh):
    return jax.shard_map(
        per_device,
        mesh=mesh,
        in_specs=(
            P("cells", "sx", "sy"),
            P("cells", None),
            P("sx", "sy", None),
            P(),
            P("sx", "sy"),
            P(None, "sx", "sy"),
            P(None, "sx", "sy"),
        ),
        out_specs=(P(), P("sx", "sy", "cells"), P("cells", "sx", "sy"), P("cells", ("sx", "sy"))),
        check_vma=False,
    )
```

```python
import functools

import jax
import jax.numpy as jnp
from jax import lax
from jax.experimental import pallas as pl
from jax.experimental.pallas import tpu as pltpu
from jax.sharding import PartitionSpec as P

EPS = 1e-06
OFFSETS = ((0, 1), (0, -1), (1, 0), (-1, 0), (-1, 1), (1, -1))
LANES = 128
TOP = 32767.0
MESH = pl.DeviceIdType.MESH
F32, BF16, I16, I32 = jnp.float32, jnp.bfloat16, jnp.int16, jnp.int32
rem, div = lax.rem, lax.div


def loop(count, body):
    lax.fori_loop(0, count, lambda i, _: (body(i), 0)[1], 0)


def remote(src, dst, sent, got, to):
    return pltpu.make_async_remote_copy(
        src_ref=src, dst_ref=dst, send_sem=sent, recv_sem=got, device_id=to, device_id_type=MESH
    )


def wait(ref, sem):
    pltpu.make_async_copy(ref, ref, sem).wait()


def spread(row):
    parts = [
        jnp.broadcast_to(row[:, at : at + LANES], (LANES, LANES)).T
        for at in range(0, row.shape[1], LANES)
    ]
    return jnp.concatenate(parts, axis=0)


def fold(x):
    return jnp.sum(x.reshape(x.shape[0] // 8, 8, x.shape[1]), axis=0)


def kernel(names, sizes, *refs):
    n, nsx, nsy, share, all_spots = sizes
    o = dict(zip(names, refs, strict=True))
    lg, cells, spat, gmask, slide, ew, em = (o[k] for k in names[:7])
    losses, gp, dlog, dcell = (o[k] for k in names[7:11])
    xs, mm, mt, dm, srow, ab, sc, tt = (o[k] for k in names[11:19])
    gg, sm, sp, pad, hg, hs, hd, hq = (o[k] for k in names[19:27])
    es, er, cf, cb, hot, con, cor, acc = (o[k] for k in names[27:35])
    gs, gr, spx, gc, spr, dd, fm = (o[k] for k in names[35:42])
    pss, rs1, rs2, rs3, dcv, gpr, gps, gpb = (o[k] for k in names[42:50])

    c_rows, t_rows, width = lg.shape
    spots = t_rows * width
    nb = cells.shape[1] // 2 // LANES
    wl = width // LANES
    wb = gpr.shape[0]
    nplane = nsx * nsy
    half = nb // 2
    bpg = nb // 4
    tile = LANES
    tiles = c_rows // tile
    quarter = c_rows // 4
    sub = min(64, width)
    mid = slice(8, 8 + width)

    sx, sy, cz = (lax.axis_index(a) for a in ("sx", "sy", "cells"))
    here = sx * nsy + sy
    owner = (cz == 0) | (cz == n - 1)
    od = jnp.where(cz == 0, 0, 1)
    up, down = sx > 0, sx < nsx - 1
    mate = (sx, 1 - sy, cz)

    def gene_block(d, k):
        return jnp.where(d == 0, rem(k + half, nb), nb + k)

    for r in range(t_rows):
        pltpu.make_async_copy(lg.at[:, r, :], dm.at[r], o["lg_m"].at[r]).start()

    def load_cells(b):
        at = pl.ds(pl.multiple_of(b * LANES, LANES), LANES)
        return pltpu.make_async_copy(cells.at[:, at], xs.at[b], o["xs_m"].at[b])

    loop(2 * nb, lambda b: load_cells(b).start())

    def load_truth(k):
        at = pl.ds(pl.multiple_of(gene_block(od, k) * LANES, LANES), LANES)
        return pltpu.make_async_copy(spat.at[:, :, at], sp.at[k], o["sp_m"].at[k])

    @pl.when(owner)
    def _():
        loop(nb, lambda k: load_truth(k).start())

    barrier = pltpu.get_barrier_semaphore()

    def greet_line(j):
        to = (sx, sy, rem(cz + j + 1, n))
        pl.semaphore_signal(barrier, inc=1, device_id=to, device_id_type=MESH)

    def greet_plane(j):
        t = rem(here + j + 1, nplane)
        to = (div(t, nsy), rem(t, nsy), cz)
        pl.semaphore_signal(barrier, inc=1, device_id=to, device_id_type=MESH)

    loop(n - 1, greet_line)
    loop(nplane - 1, greet_plane)

    for r in range(t_rows):
        pltpu.make_async_copy(lg.at[:, r, :], dm.at[r], o["lg_m"].at[r]).wait()

        def exps(i, s, r=r):
            at = pl.ds(i * tile, tile)
            x = jnp.exp(dm[r, at, :])
            dm[r, at, :] = x
            return s + fold(x)

        s = lax.fori_loop(0, c_rows // tile, exps, jnp.zeros((8, width), F32))
        s = jnp.sum(s, axis=0, keepdims=True)
        for h in range(wl):
            srow[cz, pl.ds(r * wl + h, 1), :] = s[:, h * LANES : (h + 1) * LANES]

    pl.semaphore_wait(barrier, n - 1 + nplane - 1)

    def send_sums(j):
        to = (sx, sy, rem(cz + j + 1, n))
        remote(srow.at[cz], srow.at[cz], o["s_s"].at[j], o["s_r"].at[cz], to).start()

    loop(n - 1, send_sums)

    def turn(dst, first):
        def each(i):
            for r in range(t_rows):
                at = pl.ds(pl.multiple_of((i + first) * LANES, LANES), LANES)
                dst[i, r] = dm[r, at, :].T

        return each

    turned = ((gg, 0, min(tiles, nb)), (sm, nb, max(tiles - nb, 0)))
    for dst, first, count in turned:
        loop(count, turn(dst, first))

    def wait_sums(j):
        z = rem(cz + j + 1, n)
        wait(srow.at[z], o["s_r"].at[z])

    loop(n - 1, wait_sums)
    total = srow[0]
    for z in range(1, n):
        total = total + srow[z]
    inv = 1.0 / total
    inv_rows = [
        jnp.concatenate([inv[r * wl + h : r * wl + h + 1] for h in range(wl)], axis=1)
        for r in range(t_rows)
    ]
    for r in range(t_rows):
        acc[0, r] = spread(inv_rows[r])

    for dst, first, count in turned:
        def scale(i, dst=dst, first=first):
            at = pl.ds(pl.multiple_of((i + first) * LANES, LANES), LANES)
            for r in range(t_rows):
                mt[r, :, at] = (dst[i, r] * acc[0, r]).astype(BF16)

        loop(count, scale)

    def keep_mapping():
        for r in range(t_rows):
            def each(i, r=r):
                at = pl.ds(pl.multiple_of(i * LANES, LANES), LANES)
                mm[at, r * width : (r + 1) * width] = (dm[r, at, :] * inv_rows[r]).astype(BF16)

            loop(tiles, each)

    loop(2 * nb, lambda b: load_cells(b).wait())

    def coef_routes():
        return (
            (0, down, (sx + 1, sy, cz)),
            (1, up, (sx - 1, sy, cz)),
            (2, sx >= 0, mate),
            (3, down, (sx + 1, 1 - sy, cz)),
            (4, up, (sx - 1, 1 - sy, cz)),
        )


    def predict(d, pair, r):
        g = gene_block(d, 2 * pair)
        w = jnp.concatenate([xs[g], xs[g + 1]], axis=1)
        at = pl.ds(pl.multiple_of((2 * d + rem(pair, 2)) * width, 8), width)
        tt[r, at, :] = jnp.dot(mt[r], w, preferred_element_type=F32)

    def predicted(d, k, r):
        at = pl.ds(pl.multiple_of((2 * d + rem(div(k, 2), 2)) * width, 8), width)
        return tt[r, at, pl.ds(pl.multiple_of(rem(k, 2) * LANES, LANES), LANES)]

    def put(d, k, r, t):
        top = jnp.maximum(jnp.max(jnp.abs(t), axis=0, keepdims=True), 1e-30)
        ab[d, k, r] = jnp.round(t * (TOP / top)).astype(I32).astype(I16)
        sc[d, k, r] = top * (1.0 / TOP)

    def pass_on(d, k, r):
        to = (sx, sy, cz + 2 * d - 1)
        remote(ab.at[d, k, r], ab.at[d, k, r], o["a_s"].at[d, k, r], o["a_r"].at[d, k, r], to).start()
        remote(sc.at[d, k, r], sc.at[d, k, r], o["c_s"].at[d, k, r], o["c_r"].at[d, k, r], to).start()

    def chunk_of(q):
        return div(q, t_rows), rem(rem(q, t_rows) * (t_rows - 1), t_rows)

    @pl.when(owner)
    def _():
        d = 1 - od

        def first(q):
            k, r = chunk_of(q)

            @pl.when(rem(k, 2) == 0)
            def _():
                predict(d, div(k, 2), r)

            put(d, k, r, predicted(d, k, r))
            pass_on(d, k, r)

        loop(nb * t_rows, first)

        for r in range(t_rows):
            rows = [ew[j, r : r + 1, :] * em[j, r : r + 1, :].astype(F32) for j in range(6)]
            con[r] = jnp.concatenate(rows + [jnp.zeros((2, width), F32)], axis=0)
            for j in range(6):
                cf[j, r] = spread(rows[j])
            hot[r] = spread(slide[r : r + 1, :].astype(F32))
        acc[...] = jnp.zeros(acc.shape, F32)

        for slot, ok, to in coef_routes():
            @pl.when(ok)
            def _(slot=slot, to=to):
                remote(con, cor.at[slot], o["co_s"].at[slot], o["co_r"].at[slot], to).start()

        loop(nb, lambda k: load_truth(k).wait())

    def back_coefs():
        for slot, ok in ((0, up), (1, down), (2, sx >= 0), (3, up), (4, down)):
            @pl.when(ok)
            def _(slot=slot):
                wait(cor.at[slot], o["co_r"].at[slot])

        lane = lax.broadcasted_iota(I32, (8, width), 1)
        for j, (dr, dc) in enumerate(OFFSETS):
            for r in range(t_rows):
                at = r - dr
                if at < 0:
                    base, side, ok = cor[0, t_rows - 1], cor[3, t_rows - 1], up
                elif at >= t_rows:
                    base, side, ok = cor[1, 0], cor[4, 0], down
                else:
                    base, side, ok = con[at], cor[2, at], sx >= 0
                base = jnp.where(ok, base, 0.0)
                if dc:
                    by, edge = (1, 0) if dc == 1 else (width - 1, width - 1)
                    side = jnp.where(ok & (sy == (1 if dc == 1 else 0)), side, 0.0)
                    base = jnp.where(lane == edge, pltpu.roll(side, by, 1), pltpu.roll(base, by, 1))
                cb[j, r] = spread(base[j : j + 1]).astype(BF16)

    def send_edges(slot, which, k, rows):
        parts = [
            jnp.where(sy == 1, pad[slot, row, 8:9, :], pad[slot, row, 7 + width : 8 + width, :])
            for row in rows
        ]
        parts.append(jnp.zeros((8 - len(parts), LANES), F32))
        es[which, k] = jnp.concatenate(parts, axis=0)
        remote(es.at[which, k], er.at[which, k], o["e_s"].at[which, k], o["e_r"].at[which, k], mate).start()

    def take_edges(slot, which, k, rows):
        wait(er.at[which, k], o["e_r"].at[which, k])
        for i, row in enumerate(rows):
            edge = er[which, k, i : i + 1, :]
            pad[slot, row, 8 + width : 9 + width, :] = jnp.where(sy == 0, edge, 0.0)
            pad[slot, row, 7:8, :] = jnp.where(sy == 1, edge, 0.0)

    sides = ((0, up, 0), (1, down, t_rows + 1))

    def prepare(k):
        for side, ok, row in sides:
            @pl.when(ok)
            def _(side=side, row=row):
                wait(hg.at[side, k], o["hg_r"].at[side, k])
                wait(hs.at[side, k], o["hs_r"].at[side, k])
                pad[0, row, mid, :] = hg[side, k].astype(I32).astype(F32) * hs[side, k]

            @pl.when(jnp.logical_not(ok))
            def _(row=row):
                pad[0, row, mid, :] = jnp.zeros((width, LANES), F32)

        def rows(r):
            pad[0, r + 1, mid, :] = gg[k, r]

        loop(t_rows, rows)
        send_edges(0, 0, k, range(t_rows + 2))

    def smoothing(k):
        take_edges(0, 0, k, range(t_rows + 2))
        at = pl.ds(pl.multiple_of(gene_block(od, k) * LANES, LANES), LANES)
        mask = gmask[:, at].astype(F32)
        m0, m1 = mask[0:1], mask[1:2]

        def rows(r, sums):
            sums = list(sums)
            for u in range(0, width, sub):
                here_u = slice(u, u + sub)
                a = pad[0, r + 1, 8 + u : 8 + u + sub, :]
                for j, (dr, dc) in enumerate(OFFSETS):
                    a = a + cf[j, r, here_u, :] * pad[0, r + 1 + dr, 8 + dc + u : 8 + dc + u + sub, :]
                sm[k, r, here_u, :] = a
                t = sp[k, r, here_u, :]
                h = hot[r, here_u, :]
                mk = m0 + h * (m1 - m0)
                for i, x in enumerate((a * t, a * a, t * t)):
                    sums[2 * i] = sums[2 * i] + fold(x)
                    sums[2 * i + 1] = sums[2 * i + 1] + fold(x * h)
                    acc[i, r, here_u, :] = acc[i, r, here_u, :] + x * mk
            return tuple(sums)

        sums = lax.fori_loop(0, t_rows, rows, (jnp.zeros((8, LANES), F32),) * 6)
        parts = []
        for i in range(3):
            both = jnp.sum(sums[2 * i], axis=0, keepdims=True)
            one = jnp.sum(sums[2 * i + 1], axis=0, keepdims=True)
            parts += [both - one, one]
        gs[k] = jnp.concatenate(parts + [jnp.zeros((2, LANES), F32)], axis=0)

    def own_block(t, i):
        b = div(t * share, LANES) + i - od * nb
        return jnp.where(od == 0, rem(b + half, nb), b)

    def pred_copies(i, j):
        t = jnp.where(od == 0, j + 1, n - 2 - j)
        k = own_block(t, i)
        to = (sx, sy, t)
        return (
            remote(ab.at[od, k], gpr.at[i], o["gp_s"].at[j, i], o["gp_r"].at[i], to),
            remote(sc.at[od, k], gps.at[i], o["gq_s"].at[j, i], o["gq_r"].at[i], to),
        )

    def send_pred(i):
        def each(j):
            for copy in pred_copies(i, j):
                copy.start()

        loop(n // 2 - 1, each)

    early_pred = 2 if n == 4 else 0

    def plane_peer(j):
        t = rem(here + j + 1, nplane)
        return t, (div(t, nsy), rem(t, nsy), cz)

    gene_parts = (pl.ds(0, nb - 1), pl.ds(nb - 1, 1))

    def send_genes(part):
        at = gene_parts[part]

        def each(j):
            _, to = plane_peer(j)
            sems = o["g_s"].at[part, j], o["g_r"].at[part, here]
            remote(gs.at[at], gr.at[here, at], *sems, to).start()

        loop(nplane - 1, each)

    lead = max(n - 3, 0)

    def sum_step(s):
        def direction(d):
            own, first = cz == d * (n - 1), cz == (1 - d) * (n - 1)
            off = jnp.where(owner, 0, LAG_SUM * jnp.where(d == 1, cz - 1, n - 2 - cz))
            q = s - off

            @pl.when(jnp.logical_not(first) & (q >= 0) & (q < nb * t_rows))
            def _():
                k, r = chunk_of(q)
                wait(ab.at[d, k, r], o["a_r"].at[d, k, r])
                wait(sc.at[d, k, r], o["c_r"].at[d, k, r])
                got = ab[d, k, r].astype(I32).astype(F32) * sc[d, k, r]
                t = predicted(d, k, r) + got
                put(d, k, r, t)

                @pl.when(jnp.logical_not(own))
                def _():
                    pass_on(d, k, r)

                @pl.when(own)
                def _():
                    gg[k, r] = t
                    for side, ok, row, to in halo_routes():
                        @pl.when(ok & (r == row))
                        def _(side=side, row=row, to=to):
                            remote(ab.at[d, k, row], hg.at[side, k], o["hg_s"].at[side, k], o["hg_r"].at[side, k], to).start()
                            remote(sc.at[d, k, row], hs.at[side, k], o["hs_s"].at[side, k], o["hs_r"].at[side, k], to).start()

                    i = rem(q, t_rows)

                    @pl.when((k > 0) & (i == 1))
                    def _():
                        prepare(k - 1)

                    @pl.when((k > 0) & (i == t_rows - 1))
                    def _():
                        smoothing(k - 1)

                    @pl.when((k == nb - 1) & (i == t_rows - 1))
                    def _():
                        send_genes(0)

                    if early_pred:
                        @pl.when(q == 3 * nb * t_rows // 4)
                        def _():
                            for i in range(early_pred):
                                send_pred(i)

                @pl.when((rem(k, 2) == d) & (k + 2 - rem(k, 2) < nb))
                def _():
                    predict(d, div(k, 2) + 1, r)

        turn = cz - 1 > n - 2 - cz
        loop(2, lambda i: direction(jnp.where(turn, 1 - i, i)))

        @pl.when(owner & (s == half * t_rows))
        def _():
            back_coefs()

    def halo_routes():
        return ((1, up, 0, (sx - 1, sy, cz)), (0, down, t_rows - 1, (sx + 1, sy, cz)))

    def first_block(d):
        @pl.when(cz != (1 - d) * (n - 1))
        def _():
            loop(t_rows, lambda r: predict(d, 0, r))

    loop(2, first_block)
    keep_mapping()
    loop(nb * t_rows + LAG_SUM * lead, sum_step)

    def diff_smooth(k, r, at):
        tc0, tc1, sc0, sc1, m0, m1 = (gc[k, i : i + 1, :] for i in range(6))
        h = hot[r, at, :]
        mk = m0 + h * (m1 - m0)
        by_truth = tc0 + h * (tc1 - tc0) + mk * acc[1, r, at, :]
        by_smooth = sc0 + h * (sc1 - sc0) + mk * acc[2, r, at, :]
        return by_truth * sp[k, r, at, :] + by_smooth * sm[k, r, at, :]

    def send_borders(k):
        for side, ok, row, to in halo_routes():
            @pl.when(ok)
            def _(side=side, row=row, to=to):
                for u in range(0, width, sub):
                    hq[side, k, u : u + sub, :] = diff_smooth(k, row, slice(u, u + sub)).astype(BF16)
                remote(hq.at[side, k], hd.at[side, k], o["hd_s"].at[side, k], o["hd_r"].at[side, k], to).start()

    def diff_inside(k):
        slot = rem(k, 2)

        def rows(r):
            for u in range(0, width, sub):
                pad[slot, r + 1, 8 + u : 8 + u + sub, :] = diff_smooth(k, r, slice(u, u + sub))

        loop(t_rows, rows)
        send_edges(slot, 1, k, range(1, t_rows + 1))

    def diff_border(k):
        slot = rem(k, 2)
        for side, ok, row in sides:
            @pl.when(ok)
            def _(side=side, row=row):
                wait(hd.at[side, k], o["hd_r"].at[side, k])
                pad[slot, row, mid, :] = hd[side, k].astype(F32)

            @pl.when(jnp.logical_not(ok))
            def _(row=row):
                pad[slot, row, mid, :] = jnp.zeros((width, LANES), F32)

        send_edges(slot, 2, k, (0, t_rows + 1))

    back = cz + 1 - 2 * od

    def diff_pred(k, rows):
        slot = rem(k, 2)
        for r in rows:
            for u in range(0, width, sub):
                here_u = slice(u, u + sub)
                a = pad[slot, r + 1, 8 + u : 8 + u + sub, :]
                for j, (dr, dc) in enumerate(OFFSETS):
                    w = cb[j, r, here_u, :].astype(F32)
                    a = a + w * pad[slot, r + 1 - dr, 8 - dc + u : 8 - dc + u + sub, :]
                low = a.astype(BF16)
                dd[od, k, r, here_u, :] = low
                acc[0, r, here_u, :] = acc[0, r, here_u, :] + gg[k, r, here_u, :] * low.astype(F32)
            at = dd.at[od, k, r]
            remote(at, at, o["d_s"].at[od, k, r], o["d_r"].at[od, k, r], (sx, sy, back)).start()

    def back_chunk(q):
        i = rem(q, t_rows)
        return div(q, t_rows), jnp.where(i < t_rows - 2, i + 1, jnp.where(i == t_rows - 2, 0, i))

    def diff_inner(k):
        take_edges(rem(k, 2), 1, k, range(1, t_rows + 1))
        diff_pred(k, range(1, t_rows - 1))
        diff_border(k)

    def diff_outer(k):
        take_edges(rem(k, 2), 2, k, (0, t_rows + 1))
        diff_pred(k, (0, t_rows - 1))

    def spot_rows(i):
        return [
            jnp.sum(acc[i, r, h * LANES : (h + 1) * LANES, :].T, axis=0, keepdims=True)
            for r in range(t_rows)
            for h in range(wl)
        ]

    def put_pred(i):
        at = slice(i * LANES, (i + 1) * LANES)
        return pltpu.make_async_copy(gpb.at[i], gp.at[:, :, at], o["gp_m"].at[i])

    def put_own(i):
        k = own_block(cz, i)

        def rows(r):
            gpb[i, r] = gg[k, r].astype(BF16)

        loop(t_rows, rows)
        put_pred(i).start()

    @pl.when(owner)
    def _():
        prepare(nb - 1)
        smoothing(nb - 1)

        send_genes(1)
        for i in range(3):
            for at, row in enumerate(spot_rows(i)):
                spx[0, i, at : at + 1, :] = row
        remote(spx.at[0], spx.at[1], o["x_s"].at[0], o["x_r"].at[0], (sx, sy, n - 1 - cz)).start()
        gr[here] = gs[...]
        def wait_genes(j):
            t, _ = plane_peer(j)
            for part, at in enumerate(gene_parts):
                wait(gr.at[t, at], o["g_r"].at[part, t])

        loop(nplane - 1, wait_genes)
        count = jnp.maximum(jnp.sum(gmask[...].astype(F32), axis=1, keepdims=True), 1.0)

        def genes(k, gl):
            tot = gr[0, k]
            for t in range(1, nplane):
                tot = tot + gr[t, k]
            ib, ic = lax.rsqrt(tot[2:4] + EPS), lax.rsqrt(tot[4:6] + EPS)
            cos = tot[0:2] * ib * ic
            at = pl.ds(pl.multiple_of(gene_block(od, k) * LANES, LANES), LANES)
            mask = gmask[:, at].astype(F32)
            scale = -mask / (2.0 * count)
            gc[k, 0:2, :] = scale * ib * ic
            gc[k, 2:4, :] = -scale * cos * ib * ib
            gc[k, 4:6, :] = mask
            return gl + mask * cos / count

        gl = lax.fori_loop(0, nb, genes, jnp.zeros((2, LANES), F32))
        gene_part = jnp.sum(jnp.sum(gl, axis=0, keepdims=True), axis=1, keepdims=True)

        wait(spx.at[1], o["x_r"].at[0])
        a, b, c = (spx[0, i] + spx[1, i] for i in range(3))
        ib, ic = lax.rsqrt(b + EPS), lax.rsqrt(c + EPS)
        cos = a * ib * ic
        by_truth = (-1.0 / all_spots) * ib * ic
        by_smooth = (1.0 / all_spots) * cos * ib * ib
        for r in range(t_rows):
            for h in range(wl):
                at, i = slice(h * LANES, (h + 1) * LANES), r * wl + h
                acc[1, r, at, :] = spread(by_truth[i : i + 1])
                acc[2, r, at, :] = spread(by_smooth[i : i + 1])
        acc[0] = jnp.zeros(acc.shape[1:], F32)
        spot_part = jnp.sum(jnp.sum(cos, axis=0, keepdims=True), axis=1, keepdims=True)
        spr[here] = jnp.broadcast_to(spot_part, (8, LANES))
        fm[od, 1] = jnp.broadcast_to(gene_part, (8, LANES))

        def send_spot(j):
            _, to = plane_peer(j)
            remote(spr.at[here], spr.at[here], o["p_s"].at[j], o["p_r"].at[here], to).start()

        send_borders(0)
        diff_inside(0)
        send_borders(1)
        take_edges(0, 1, 0, range(1, t_rows + 1))
        diff_pred(0, range(1, t_rows - 1))
        loop(nb - 2, lambda k: send_borders(k + 2))
        loop(nplane - 1, send_spot)
        diff_border(0)

    def send_last():
        def wait_spot(j):
            t, _ = plane_peer(j)
            wait(spr.at[t], o["p_r"].at[t])

        loop(nplane - 1, wait_spot)
        spot_all = spr[0, 0:1, :]
        for t in range(1, nplane):
            spot_all = spot_all + spr[t, 0:1, :]
        rows = spot_rows(0)
        if len(rows) < 8:
            rows.append(jnp.zeros((8 - len(rows), LANES), F32))
        fm[od, 0] = jnp.concatenate(rows, axis=0)
        fm[od, 1, 1:2, :] = spot_all
        remote(fm.at[od], fm.at[od], o["f_s"].at[od], o["f_r"].at[od], (sx, sy, back)).start()
        for i in range(early_pred, wb):
            send_pred(i)


    sy_bit, sx_bit = div(sx, 2), rem(sx, 2)
    over_y, over_x = (sx + 2 - 4 * sy_bit, sy, cz), (sx + 1 - 2 * sx_bit, sy, cz)

    def place(k):
        jj = div(k, bpg)
        hi = div(jj, 2)
        return rem(jj, 2) == sy, hi * bpg + rem(k, bpg), jnp.where(sy_bit == 0, 1 - hi, hi) == sx_bit

    halves = (pl.ds(0, c_rows // 2), pl.ds(c_rows // 2, c_rows // 2))
    cuts = [pl.ds(i * quarter, quarter) for i in range(4)]

    def add_rows(dst, *terms):
        count = dst.shape[0] // 2

        def rows(i):
            at = pl.ds(pl.multiple_of(i * count, 8), count)
            dst[at, :] = sum(t[at, :].astype(F32) for t in terms).astype(dst.dtype)

        loop(2, rows)

    def multiply(k, h):
        half = halves[h]
        mine, at, _ = place(k)
        slot = rem(k, 2)
        block = jnp.concatenate([dd[i, k].reshape(spots, LANES) for i in range(2)], axis=1)
        out = jnp.dot(mm[half, :], block, preferred_element_type=F32).astype(BF16)
        pss[slot, 0, half, :] = out[:, :LANES]
        pss[slot, 1, half, :] = out[:, LANES:]

        @pl.when(jnp.logical_not(mine))
        def _():
            for d in range(2):
                src, dst = pss.at[slot, d, half], rs1.at[d, at, half]
                remote(src, dst, o["r1_s"].at[d, at, h], o["r1_r"].at[d, at, h], mate).start()

    def stays(final):
        return sy_bit, jnp.where(final, sy_bit, 1 - sy_bit)

    def scatter_1(k):
        mine, at, final = place(k)
        slot = rem(k, 2)

        @pl.when(mine)
        def _():
            for h, (stay, to) in enumerate(zip(stays(final), (over_y, over_x), strict=True)):
                d, half = 1 - stay, halves[h]
                wait(rs1.at[d, at, half], o["r1_r"].at[d, at, h])
                for i in (2 * h, 2 * h + 1):
                    src, sems = rs1.at[d, at, cuts[i]], (o["r2_s"].at[i, at], o["r2_r"].at[i, at])
                    add_rows(src, pss.at[slot, d, cuts[i]], src)
                    remote(src, rs2.at[at, cuts[i]], *sems, to).start()

        @pl.when(jnp.logical_not(mine))
        def _():
            for d in range(2):
                for h, half in enumerate(halves):
                    wait(pss.at[slot, d, half], o["r1_s"].at[d, at, h])

    def scatter_2(k):
        mine, at, final = place(k)
        slot = rem(k, 2)

        @pl.when(mine)
        def _():
            j = rem(k, bpg)
            for h, d in enumerate(stays(final)):
                wait(rs1.at[d, at, halves[h]], o["r1_r"].at[d, at, h])
            for i in (0, 2, 1, 3):
                h, cut = i // 2, cuts[i]
                d, to = stays(final)[h], (over_x, over_y)[h]
                part = rs2.at[at, cut]
                wait(part, o["r2_r"].at[i, at])
                add_rows(part, pss.at[slot, d, cut], rs1.at[d, at, cut], part)

                @pl.when(jnp.logical_not(final))
                def _(i=i, part=part, cut=cut, to=to):
                    remote(part, rs3.at[j, cut], o["r3_s"].at[i, j], o["r3_r"].at[i, j], to).start()

            for i in range(4):
                wait(rs1.at[1 - stays(final)[i // 2], at, cuts[i]], o["r2_s"].at[i, at])

    def put_cells(i):
        at = pl.ds(pl.multiple_of(i * LANES, LANES), LANES)
        return pltpu.make_async_copy(dcv.at[i], dcell.at[:, at], o["dc_m"].at[i])

    def scatter_3(k):
        mine, at, final = place(k)
        i = rem(k, bpg)

        @pl.when(mine & final)
        def _():
            for c in (0, 2, 1, 3):
                wait(rs3.at[i, cuts[c]], o["r3_r"].at[c, i])
                add_rows(dcv.at[i, cuts[c]], rs2.at[at, cuts[c]], rs3.at[i, cuts[c]])
            put_cells(i).start()

        @pl.when(mine & jnp.logical_not(final))
        def _():
            for c in range(4):
                wait(rs2.at[at, cuts[c]], o["r3_s"].at[c, i])

    def add_map(k, r):
        x = jnp.concatenate([xs[gene_block(0, k)], xs[gene_block(1, k)]], axis=1)
        d = jnp.concatenate([dd[0, k, r], dd[1, k, r]], axis=1)
        new = lax.dot_general(x, d, (((1,), (1,)), ((), ())), preferred_element_type=F32)
        dm[r] = jnp.where(k == 0, 0.0, dm[r]) + new

    def put_logits(r):
        return pltpu.make_async_copy(mm.at[:, r * width : (r + 1) * width], dlog.at[r], o["dl_m"].at[r])

    def finish(r):
        col = jnp.concatenate([fm[0, 0, i : i + 1] + fm[1, 0, i : i + 1] for i in range(r * wl, (r + 1) * wl)], axis=1)

        def rows(i):
            at = pl.ds(pl.multiple_of(i * tile, tile), tile)
            cols = slice(r * width, (r + 1) * width)
            low = mm[at, cols].astype(F32)
            mm[at, cols] = (low * (dm[r, at, :] - col)).astype(BF16)

        loop(c_rows // tile, rows)
        put_logits(r).start()

    def take_pred(i):
        wait(gpr.at[i], o["gp_r"].at[i])
        wait(gps.at[i], o["gq_r"].at[i])

        def rows(r):
            gpb[i, r] = (gpr[i, r].astype(I32).astype(F32) * gps[i, r]).astype(BF16)

        loop(t_rows, rows)
        put_pred(i).start()

    behind = BEHIND * t_rows
    lag = jnp.where(owner, behind, LAG_BACK * jnp.maximum(cz - 1, n - 2 - cz))

    def produce(k, piece):
        @pl.when(piece == 0)
        def _():
            diff_outer(k)

        @pl.when((piece == 1) & (k + 1 < nb))
        def _():
            diff_inside(k + 1)

        @pl.when((piece == 2) & (k + 1 < nb))
        def _():
            diff_inner(k + 1)

        @pl.when((piece == 1) & (k + 1 == nb))
        def _():
            send_last()

    def drain():
        loop(n - 1, lambda j: wait(srow.at[cz], o["s_s"].at[j]))

        def sent(d):
            own, end = cz == d * (n - 1), cz == (1 - d) * (n - 1)

            @pl.when(jnp.logical_not(own))
            def _():
                def each(q):
                    k, r = div(q, t_rows), rem(q, t_rows)
                    wait(ab.at[d, k, r], o["a_s"].at[d, k, r])
                    wait(sc.at[d, k, r], o["c_s"].at[d, k, r])

                loop(nb * t_rows, each)

            @pl.when(jnp.logical_not(end))
            def _():
                def each(q):
                    k, r = div(q, t_rows), rem(q, t_rows)
                    wait(dd.at[d, k, r], o["d_s"].at[d, k, r])

                loop(nb * t_rows, each)
                wait(fm.at[d], o["f_s"].at[d])

        loop(2, sent)

        @pl.when(owner)
        def _():
            for i in range(wb):
                def each(j, i=i):
                    for copy in pred_copies(i, j):
                        copy.wait_send()

                loop(n // 2 - 1, each)
            for slot, ok, _ in coef_routes():
                @pl.when(ok)
                def _(slot=slot):
                    wait(con, o["co_s"].at[slot])

            def each(k):
                for side, ok, row, _ in halo_routes():
                    @pl.when(ok)
                    def _(side=side, row=row):
                        wait(ab.at[od, k, row], o["hg_s"].at[side, k])
                        wait(sc.at[od, k, row], o["hs_s"].at[side, k])
                        wait(hq.at[side, k], o["hd_s"].at[side, k])

                for which in range(3):
                    wait(es.at[which, k], o["e_s"].at[which, k])

            loop(nb, each)
            wait(spx.at[0], o["x_s"].at[0])

            def each_peer(j):
                for part, at in enumerate(gene_parts):
                    wait(gs.at[at], o["g_s"].at[part, j])
                wait(spr.at[here], o["p_s"].at[j])

            loop(nplane - 1, each_peer)

    def back_step(s):
        for i in range(wb):
            @pl.when(owner & (s == 2 * i + 1))
            def _(i=i):
                put_own(i)

        @pl.when(owner & (s < nb * t_rows))
        def _():
            produce(div(s, t_rows), rem(s, t_rows))

        def direction(d):
            own, end = cz == d * (n - 1), cz == (1 - d) * (n - 1)
            off = jnp.where(owner, behind, LAG_BACK * jnp.where(d == 0, cz - 1, n - 2 - cz))
            q = s - off
            to = (sx, sy, cz + 1 - 2 * d)

            @pl.when(jnp.logical_not(own) & (q >= 0) & (q < nb * t_rows))
            def _():
                k, r = back_chunk(q)
                at = dd.at[d, k, r]
                wait(at, o["d_r"].at[d, k, r])

                @pl.when(jnp.logical_not(end))
                def _():
                    remote(at, at, o["d_s"].at[d, k, r], o["d_r"].at[d, k, r], to).start()

            @pl.when(jnp.logical_not(own) & (q == nb * t_rows + 2))
            def _():
                wait(fm.at[d], o["f_r"].at[d])

                @pl.when(jnp.logical_not(end))
                def _():
                    remote(fm.at[d], fm.at[d], o["f_s"].at[d], o["f_r"].at[d], to).start()

        turn = cz - 1 < n - 2 - cz
        loop(2, lambda i: direction(jnp.where(turn, 1 - i, i)))
        q = s - lag

        w = q - t_rows + 1
        k, piece = div(w, t_rows), rem(w, t_rows)

        for h in range(2):
            @pl.when((w >= 0) & (k < nb) & (piece == h))
            def _(h=h):
                multiply(k, h)

        @pl.when((q >= 0) & (q < nb * t_rows))
        def _():
            add_map(*back_chunk(q))

        @pl.when((w >= 0) & (k == nb))
        def _():
            for r in range(t_rows):
                @pl.when(piece == r)
                def _(r=r):
                    finish(r)

        for stage, back_by, at in ((scatter_1, 0, 2), (scatter_2, 1, 2), (scatter_3, 2, 2)):
            @pl.when((w >= 0) & (piece == at) & (k >= back_by) & (k < nb + back_by))
            def _(stage=stage, back_by=back_by):
                stage(k - back_by)

        @pl.when(w == nb * t_rows + t_rows - 1)
        def _():
            drain()

        @pl.when((w == (nb + 1) * t_rows) & jnp.logical_not(owner))
        def _():
            for i in range(wb):
                take_pred(i)

    loop(t_rows * (nb + 4) + max(LAG_BACK * lead, behind), back_step)

    losses[0] = jnp.max(fm[0, 1, 0:1, :] + fm[1, 1, 0:1, :]) * -0.5
    losses[1] = jnp.max(fm[0, 1, 1:2, :]) * (-1.0 / all_spots)

    for r in range(t_rows):
        put_logits(r).wait()
    for i in range(bpg):
        put_cells(i).wait()

    for i in range(wb):
        put_pred(i).wait()


def cells_first(x, out):
    for r in range(x.shape[0]):
        out[:, r, :] = x[r].astype(F32)


def per_device(logits, cells_expr, spatial, gene_mask, slide_id, edge_weight, edge_mask):
    c_rows, t_rows, width = logits.shape
    genes = cells_expr.shape[1]
    n, nsx, nsy = (lax.axis_size(a) for a in ("cells", "sx", "sy"))
    spots = t_rows * width
    share = genes // n
    wide = max(share, LANES)
    wb = wide // LANES
    nb = genes // 2 // LANES
    nplane = nsx * nsy
    grid = (t_rows, width, LANES)
    vm, dma = pltpu.VMEM, pltpu.SemaphoreType.DMA
    scratch = dict(
        xs=vm((2 * nb, c_rows, LANES), BF16),
        mm=vm((c_rows, spots), BF16),
        mt=vm((t_rows, width, c_rows), BF16),
        dm=vm((t_rows, c_rows, width), F32),
        srow=vm((n, spots // LANES, LANES), F32),
        ab=vm((2, nb, *grid), I16),
        sc=vm((2, nb, t_rows, 1, LANES), F32),
        tt=vm((t_rows, 4 * width, 2 * LANES), F32),
        gg=vm((nb, *grid), F32),
        sm=vm((nb, *grid), F32),
        sp=vm((nb, *grid), F32),
        pad=vm((2, t_rows + 2, width + 16, LANES), F32),
        hg=vm((2, nb, width, LANES), I16),
        hs=vm((2, nb, 1, LANES), F32),
        hd=vm((2, nb, width, LANES), BF16),
        hq=vm((2, nb, width, LANES), BF16),
        es=vm((3, nb, 8, LANES), F32),
        er=vm((3, nb, 8, LANES), F32),
        cf=vm((6, *grid), F32),
        cb=vm((6, *grid), BF16),
        hot=vm(grid, F32),
        con=vm((t_rows, 8, width), F32),
        cor=vm((5, t_rows, 8, width), F32),
        acc=vm((3, *grid), F32),
        gs=vm((nb, 8, LANES), F32),
        gr=vm((nplane, nb, 8, LANES), F32),
        spx=vm((2, 3, spots // LANES, LANES), F32),
        gc=vm((nb, 8, LANES), F32),
        spr=vm((nplane, 8, LANES), F32),
        dd=vm((2, nb, *grid), BF16),
        fm=vm((2, 2, 8, LANES), F32),
        pss=vm((2, 2, c_rows, LANES), BF16),
        rs1=vm((2, nb // 2, c_rows, LANES), BF16),
        rs2=vm((nb // 2, c_rows, LANES), BF16),
        rs3=vm((nb // 4, c_rows, LANES), BF16),
        dcv=vm((nb // 4, c_rows, LANES), BF16),
        gpr=vm((wb, *grid), I16),
        gps=vm((wb, t_rows, 1, LANES), F32),
        gpb=vm((wb, *grid), BF16),
        lg_m=dma((t_rows,)),
        xs_m=dma((2 * nb,)),
        sp_m=dma((nb,)),
        s_s=dma((n,)),
        s_r=dma((n,)),
        a_s=dma((2, nb, t_rows)),
        a_r=dma((2, nb, t_rows)),
        c_s=dma((2, nb, t_rows)),
        c_r=dma((2, nb, t_rows)),
        hg_s=dma((2, nb)),
        hg_r=dma((2, nb)),
        hs_s=dma((2, nb)),
        hs_r=dma((2, nb)),
        hd_s=dma((2, nb)),
        hd_r=dma((2, nb)),
        e_s=dma((3, nb)),
        e_r=dma((3, nb)),
        co_s=dma((5,)),
        co_r=dma((5,)),
        g_s=dma((2, nplane)),
        g_r=dma((2, nplane)),
        p_s=dma((nplane,)),
        p_r=dma((nplane,)),
        x_s=dma((1,)),
        x_r=dma((1,)),
        d_s=dma((2, nb, t_rows)),
        d_r=dma((2, nb, t_rows)),
        f_s=dma((2,)),
        f_r=dma((2,)),
        r1_s=dma((2, nb // 2, 2)),
        r1_r=dma((2, nb // 2, 2)),
        r2_s=dma((4, nb // 2)),
        r2_r=dma((4, nb // 2)),
        r3_s=dma((4, nb // 4)),
        r3_r=dma((4, nb // 4)),
        gp_s=dma((max(n // 2 - 1, 1), wb)),
        gp_r=dma((wb,)),
        gq_s=dma((max(n // 2 - 1, 1), wb)),
        gq_r=dma((wb,)),
        gp_m=dma((wb,)),
        dl_m=dma((t_rows,)),
        dc_m=dma((nb // 4,)),
    )
    names = ("lg", "cells", "spat", "gmask", "slide", "ew", "em", "losses", "gp", "dlog", "dcell")
    names += tuple(scratch)
    sizes = (n, nsx, nsy, share, spots * nplane)
    anywhere, local = pl.BlockSpec(memory_space=pl.ANY), pl.BlockSpec(memory_space=pltpu.VMEM)
    losses, pred, d_logits, d_cells = pl.pallas_call(
        functools.partial(kernel, names, sizes),
        out_shape=(
            jax.ShapeDtypeStruct((2,), F32),
            jax.ShapeDtypeStruct((t_rows, width, wide), BF16),
            jax.ShapeDtypeStruct((t_rows, c_rows, width), BF16),
            jax.ShapeDtypeStruct((c_rows, genes // nplane), BF16),
        ),
        in_specs=[anywhere] * 3 + [local] * 4,
        out_specs=(pl.BlockSpec(memory_space=pltpu.SMEM), anywhere, anywhere, anywhere),
        scratch_shapes=list(scratch.values()),
        compiler_params=pltpu.CompilerParams(
            collective_id=0, has_side_effects=True, vmem_limit_bytes=VMEM
        ),
        cost_estimate=pl.CostEstimate(
            flops=6 * c_rows * spots * genes, bytes_accessed=32 << 20, transcendentals=c_rows * spots
        ),
    )(logits, cells_expr, spatial, gene_mask, slide_id, edge_weight, edge_mask)
    if wide > share:
        pred = lax.dynamic_slice_in_dim(pred, rem(lax.axis_index("cells") * share, wide), share, 2)
    tile = c_rows // 2 if c_rows % 64 == 0 else c_rows
    d_logits = pl.pallas_call(
        cells_first,
        grid=(c_rows // tile,),
        out_shape=jax.ShapeDtypeStruct(logits.shape, F32),
        in_specs=[pl.BlockSpec((t_rows, tile, width), lambda i: (0, i, 0))],
        out_specs=pl.BlockSpec((tile, t_rows, width), lambda i: (i, 0, 0)),
        compiler_params=pltpu.CompilerParams(vmem_limit_bytes=60 * 1024 * 1024),
    )(d_logits)
    return (losses, pred.astype(F32), d_logits, d_cells.astype(F32))


BEHIND = 3
LAG_SUM = 3
LAG_BACK = 3
VMEM = 64 * 1024 * 1024 - 512 * 1024


def solution(mesh):
    return jax.shard_map(
        per_device,
        mesh=mesh,
        in_specs=(
            P("cells", "sx", "sy"),
            P("cells", None),
            P("sx", "sy", None),
            P(),
            P("sx", "sy"),
            P(None, "sx", "sy"),
            P(None, "sx", "sy"),
        ),
        out_specs=(P(), P("sx", "sy", "cells"), P("cells", "sx", "sy"), P("cells", ("sx", "sy"))),
        check_vma=False,
    )
```
